32 devices in a mesh: wide: 8 (over y, x, core), narrow: 4 (over z).
Axes of the slice: x: 2, y: 2, z: 4, core: 2. Of those that a mesh axis runs over, the one named last changes fastest.
Arguments:
- tokens: bfloat16 [8, 1024, 1024], P('wide', 'narrow'), may hold values from -6 to 6
- memory: bfloat16 [8, 1024, 1024], P('wide', 'narrow'), may hold values from -6 to 6
- dec_ids: int32 [8, 1024], P('wide'), may hold values from 0 to 3, as said below
- enc_ids: int32 [8, 1024], P('wide'), may hold values from 0 to 3, as said below
- cotangent: bfloat16 [8, 1024, 1024], P('wide', 'narrow'), may hold values from -6 to 6
- query_weight: float32 [2, 1024, 1024], P(None, ('wide', 'narrow')), may hold values from -0.1875 to 0.1875
- query_moment: float32 [2, 1024, 1024], P(None, ('wide', 'narrow')), may hold values from -256 to 256
- query_trail: float32 [2, 1024, 1024], P(None, ('wide', 'narrow')), may hold values from -0.1875 to 0.1875
- keyval_weight: float32 [2, 1024, 1024], P(None, ('wide', 'narrow')), may hold values from -0.1875 to 0.1875
- keyval_moment: float32 [2, 1024, 1024], P(None, ('wide', 'narrow')), may hold values from -256 to 256
- keyval_trail: float32 [2, 1024, 1024], P(None, ('wide', 'narrow')), may hold values from -0.1875 to 0.1875
- output_weight: float32 [2, 1024, 1024], P(None, None, ('wide', 'narrow')), may hold values from -1.5 to 1.5
- output_moment: float32 [2, 1024, 1024], P(None, None, ('wide', 'narrow')), may hold values from -256 to 256
- output_trail: float32 [2, 1024, 1024], P(None, None, ('wide', 'narrow')), may hold values from -1.5 to 1.5
- inner_weight: float32 [1024, 5632], P(('wide', 'narrow')), may hold values from -0.1875 to 0.1875
- inner_moment: float32 [1024, 5632], P(('wide', 'narrow')), may hold values from -256 to 256
- inner_trail: float32 [1024, 5632], P(('wide', 'narrow')), may hold values from -0.1875 to 0.1875
- outer_weight: float32 [2816, 1024], P(None, ('wide', 'narrow')), may hold values from -0.109375 to 0.109375
- outer_moment: float32 [2816, 1024], P(None, ('wide', 'narrow')), may hold values from -256 to 256
- outer_trail: float32 [2816, 1024], P(None, ('wide', 'narrow')), may hold values from -0.109375 to 0.109375
- norm_gains: float32 [3, 1024], P(None, ('wide', 'narrow')), may hold values from 0.1 to 1.9
- gains_moment: float32 [3, 1024], P(None, ('wide', 'narrow')), may hold values from -256 to 256
- gains_trail: float32 [3, 1024], P(None, ('wide', 'narrow')), may hold values from 0.25 to 1.75
Outputs:
- block_out: bfloat16 [8, 1024, 1024], P('wide', 'narrow')
- input_grad: float32 [8, 1024, 1024], P('wide', 'narrow')
- memory_grad: float32 [8, 1024, 1024], P('wide', 'narrow')
- new_query: float32 [2, 1024, 1024], P(None, ('wide', 'narrow'))
- new_query_moment: float32 [2, 1024, 1024], P(None, ('wide', 'narrow'))
- new_query_trail: float32 [2, 1024, 1024], P(None, ('wide', 'narrow'))
- query_copy: bfloat16 [2, 1024, 1024], P(None, ('wide', 'narrow'))
- new_keyval: float32 [2, 1024, 1024], P(None, ('wide', 'narrow'))
- new_keyval_moment: float32 [2, 1024, 1024], P(None, ('wide', 'narrow'))
- new_keyval_trail: float32 [2, 1024, 1024], P(None, ('wide', 'narrow'))
- keyval_copy: bfloat16 [2, 1024, 1024], P(None, ('wide', 'narrow'))
- new_output: float32 [2, 1024, 1024], P(None, None, ('wide', 'narrow'))
- new_output_moment: float32 [2, 1024, 1024], P(None, None, ('wide', 'narrow'))
- new_output_trail: float32 [2, 1024, 1024], P(None, None, ('wide', 'narrow'))
- output_copy: bfloat16 [2, 1024, 1024], P(None, None, ('wide', 'narrow'))
- new_inner: float32 [1024, 5632], P(('wide', 'narrow'))
- new_inner_moment: float32 [1024, 5632], P(('wide', 'narrow'))
- new_inner_trail: float32 [1024, 5632], P(('wide', 'narrow'))
- inner_copy: bfloat16 [1024, 5632], P(('wide', 'narrow'))
- new_outer: float32 [2816, 1024], P(None, ('wide', 'narrow'))
- new_outer_moment: float32 [2816, 1024], P(None, ('wide', 'narrow'))
- new_outer_trail: float32 [2816, 1024], P(None, ('wide', 'narrow'))
- outer_copy: bfloat16 [2816, 1024], P(None, ('wide', 'narrow'))
- new_gains: float32 [3, 1024], P(None, ('wide', 'narrow'))
- new_gains_moment: float32 [3, 1024], P(None, ('wide', 'narrow'))
- new_gains_trail: float32 [3, 1024], P(None, ('wide', 'narrow'))
- gains_copy: bfloat16 [3, 1024], P(None, ('wide', 'narrow'))
The draws below stay inside these ranges and needn't reach their ends.
Inputs may be any that keep to these rules, and one draw needn't show every extreme that they name: `dec_ids`: A row's ids never fall and each of its 4 documents holds one position or more; decoder and encoder ids of a row name the same documents. `enc_ids`: A row's ids never fall and each of its 4 documents holds one position or more.
All inputs are finite; a program needn't handle non-finite values.
Results may differ from the reference program's by a relative error of at most 0.02.
The reference program's roundings to bfloat16 on the way count: a program that leaves them out, or rounds other values in their place, can miss the bound.
Values may be sent and summed in bfloat16 or wider, within the bound.
No kernel may reach another device: no remote copies, remote signals or barrier semaphores. Data moves between devices by JAX's collectives and lax.ppermute only.
A program may use at most 256 MiB of HBM per device.

```python
import math
import jax
import jax.numpy as jnp
from jax import lax

D = 1024
FF = 2816
HDIM = 64
TPOS = 256
MPOS = 256
DOCS = 4
QW = 1024
KVW = 512
ROWS = 8
LEN = 1024
MLEN = 1024


def long_document(key):
    return jax.random.randint(key, (ROWS, 1), 0, DOCS)


def segment_ids(key, chosen, length, span):
    sizes = jax.random.randint(key, (ROWS, DOCS), 1, span // DOCS + 1)
    slots = jnp.arange(DOCS)[None, :]
    sizes = jnp.where(slots == chosen, 0, sizes)
    sizes = jnp.where(slots == chosen, length - jnp.sum(sizes, axis=1, keepdims=True), sizes)
    bounds = jnp.cumsum(sizes, axis=1)[:, :DOCS - 1]
    places = jnp.arange(length)
    return jnp.sum((places[None, :, None] >= bounds[:, None, :]).astype(jnp.int32), axis=2).astype(jnp.int32)


def draw_dec_ids(key, part):
    chosen = long_document(key)
    key = jax.random.fold_in(key, 11)
    return segment_ids(key, chosen, LEN, TPOS)


def draw_enc_ids(key, part):
    chosen = long_document(key)
    key = jax.random.fold_in(key, 23)
    return segment_ids(key, chosen, MLEN, MPOS)


def steps_of(rng, dims, split, least, high):
    def one(position, shards_of):
        steps = jax.random.uniform(jax.random.fold_in(jax.random.fold_in(rng, 6), position), (shards_of,), jnp.float32, least / len(split), high / len(split))
        return jnp.repeat(jnp.exp(steps), dims[position] // shards_of).reshape((-1,) + (1,) * (len(dims) - position - 1))

    loudness = one(*split[0])
    for cut in split[1:]:
        loudness = loudness * one(*cut)
    return loudness


def gaussian(own_key, shape, scale, bound, split=(), kind=jnp.bfloat16):
    values = scale * jax.random.normal(own_key, shape, jnp.float32)
    if split:
        values = values * steps_of(own_key, shape, split, -0.22, 0.18)
    return jnp.clip(values, -bound, bound).astype(kind)


def setup_inputs(seed: int = 0) -> dict:
    arg_keys = jax.random.split(jax.random.key(seed), 24)
    return {
        "tokens": gaussian(arg_keys[0], (ROWS, LEN, D), 1.0, 6.0, ((0, 8), (1, 4))),
        "memory": gaussian(arg_keys[1], (ROWS, MLEN, D), 1.0, 6.0, ((0, 8), (1, 4))),
        "dec_ids": draw_dec_ids(jax.random.fold_in(arg_keys[23], 71), 0),
        "enc_ids": draw_enc_ids(jax.random.fold_in(arg_keys[23], 71), 0),
        "cotangent": gaussian(arg_keys[4], (ROWS, LEN, D), 1.0, 6.0, ((0, 8), (1, 4))),
        "query_weight": gaussian(arg_keys[5], (2, D, QW), D ** -0.5, 0.1875, ((1, 32),), jnp.float32),
        "query_moment": gaussian(arg_keys[6], (2, D, QW), (0.5 * (ROWS * LEN) ** 0.5), 256.0, ((1, 32),), jnp.float32),
        "query_trail": gaussian(arg_keys[7], (2, D, QW), D ** -0.5, 0.1875, ((1, 32),), jnp.float32),
        "keyval_weight": gaussian(arg_keys[8], (2, D, 2 * KVW), D ** -0.5, 0.1875, ((1, 32),), jnp.float32),
        "keyval_moment": gaussian(arg_keys[9], (2, D, 2 * KVW), (0.5 * (ROWS * LEN) ** 0.5), 256.0, ((1, 32),), jnp.float32),
        "keyval_trail": gaussian(arg_keys[10], (2, D, 2 * KVW), D ** -0.5, 0.1875, ((1, 32),), jnp.float32),
        "output_weight": gaussian(arg_keys[11], (2, QW, D), (max(QW // 64, 1)) ** -0.5, 1.5, ((2, 32),), jnp.float32),
        "output_moment": gaussian(arg_keys[12], (2, QW, D), (0.5 * (ROWS * LEN) ** 0.5), 256.0, ((2, 32),), jnp.float32),
        "output_trail": gaussian(arg_keys[13], (2, QW, D), (max(QW // 64, 1)) ** -0.5, 1.5, ((2, 32),), jnp.float32),
        "inner_weight": gaussian(arg_keys[14], (D, 2 * FF), D ** -0.5, 0.1875, ((0, 32),), jnp.float32),
        "inner_moment": gaussian(arg_keys[15], (D, 2 * FF), (0.5 * (ROWS * LEN) ** 0.5), 256.0, ((0, 32),), jnp.float32),
        "inner_trail": gaussian(arg_keys[16], (D, 2 * FF), D ** -0.5, 0.1875, ((0, 32),), jnp.float32),
        "outer_weight": gaussian(arg_keys[17], (FF, D), FF ** -0.5, 0.109375, ((1, 32),), jnp.float32),
        "outer_moment": gaussian(arg_keys[18], (FF, D), (0.5 * (ROWS * LEN) ** 0.5), 256.0, ((1, 32),), jnp.float32),
        "outer_trail": gaussian(arg_keys[19], (FF, D), FF ** -0.5, 0.109375, ((1, 32),), jnp.float32),
        "norm_gains": jnp.clip(1.0 + 0.18 * jax.random.normal(arg_keys[20], (3, D), jnp.float32), 0.1, 1.9),
        "gains_moment": gaussian(arg_keys[21], (3, D), (0.5 * (ROWS * LEN) ** 0.5), 256.0, ((1, 32),), jnp.float32),
        "gains_trail": jnp.clip(0.25 + 1.5 * jax.random.uniform(arg_keys[22], (3, D), jnp.float32) ** steps_of(arg_keys[22], (3, D), ((1, 32),), -0.2, 0.2), 0.25, 1.75),
    }


EPS = 1e-06
NEG = -1e+30
RATE = 0.02
OUTPUT_RATE = 0.15
HIGH = lax.Precision.HIGHEST

@jax.custom_vjp
def low(v):
    return lax.optimization_barrier(v.astype(jnp.bfloat16)).astype(jnp.float32)

@jax.custom_vjp
def low_back(v):
    return v

def low_keep(v):
    return (low(v), None)

def low_pass(kept, grad):
    return (grad,)

def back_keep(v):
    return (v, None)

def back_low(kept, grad):
    return (low(grad),)
low.defvjp(low_keep, low_pass)
low_back.defvjp(back_keep, back_low)

def rms_norm(hidden, gain):
    return hidden * lax.rsqrt(lax.optimization_barrier(jnp.mean(hidden * hidden, axis=-1, keepdims=True)) + EPS) * gain

def matmul(left, right):
    return jnp.dot(left, right, precision=HIGH, preferred_element_type=jnp.float32)

def attend(query, keys, values, mask):
    count = query.shape[0]
    span = keys.shape[0]
    groups = keys.shape[1] // HDIM
    shared = query.shape[1] // keys.shape[1]
    query_sets = query.reshape(count, groups, shared, HDIM).transpose(1, 0, 2, 3)
    key_sets = keys.reshape(span, groups, HDIM).transpose(1, 0, 2)
    value_sets = values.reshape(span, groups, HDIM).transpose(1, 0, 2)

    def one_group(items):
        query_part, key_part, value_part = items
        raw = low_back(jnp.einsum('nhd,md->hnm', query_part, key_part, precision=HIGH))
        logits = jnp.where(mask[None], raw * HDIM ** (-0.5), NEG)
        peak = lax.optimization_barrier(jnp.max(logits, axis=-1, keepdims=True))
        weights = jnp.where(mask[None], jnp.exp(logits - peak), 0.0)
        probs = low(weights / lax.optimization_barrier(jnp.sum(weights, axis=-1, keepdims=True)))
        return jnp.einsum('hnm,md->nhd', probs, value_part, precision=HIGH)
    result = lax.map(jax.checkpoint(one_group), (query_sets, key_sets, value_sets))
    return result.transpose(1, 0, 2, 3).reshape(count, -1)

def layer(hidden, mem, dec, enc, w_query, w_keyval, w_output, w_inner, w_outer, gains):
    places = jnp.arange(hidden.shape[0])
    self_mask = (dec[:, None] == dec[None, :]) & (places[:, None] >= places[None, :])
    cross_mask = dec[:, None] == enc[None, :]
    key_width = w_keyval.shape[2] // 2
    inner_width = w_outer.shape[0]
    normed = low(rms_norm(hidden, gains[0]))
    query = low_back(low(matmul(normed, w_query[0])))
    keyval = low_back(low(matmul(normed, w_keyval[0])))
    context = low_back(low(attend(query, keyval[:, :key_width], keyval[:, key_width:], self_mask)))
    after_one = hidden + low_back(matmul(context, w_output[0]))
    normed = low(rms_norm(after_one, gains[1]))
    query = low_back(low(matmul(normed, w_query[1])))
    keyval = low_back(low(matmul(mem, w_keyval[1])))
    context = low_back(low(attend(query, keyval[:, :key_width], keyval[:, key_width:], cross_mask)))
    after_two = after_one + low_back(matmul(context, w_output[1]))
    normed = low(rms_norm(after_two, gains[2]))
    inner = low_back(matmul(normed, w_inner))
    activated = low(jax.nn.gelu(inner[:, :inner_width]) * inner[:, inner_width:])
    return after_two + low_back(matmul(activated, w_outer))

def advance(master, moment, trail, grad, rate):
    new_moment = 0.5 * moment + 0.5 * grad
    new_master = master - rate * (grad + 0.5 * new_moment)
    new_trail = 0.5 * trail + 0.5 * new_master
    return (new_master, new_moment, new_trail, new_master.astype(jnp.bfloat16))

def reference(tokens, memory, dec_ids, enc_ids, cotangent, query_weight, query_moment, query_trail, keyval_weight, keyval_moment, keyval_trail, output_weight, output_moment, output_trail, inner_weight, inner_moment, inner_trail, outer_weight, outer_moment, outer_trail, norm_gains, gains_moment, gains_trail):
    masters = (query_weight, keyval_weight, output_weight, inner_weight, outer_weight, norm_gains)
    rounded = tuple((w.astype(jnp.bfloat16).astype(jnp.float32) for w in masters))

    def per_row(total, items):
        row_tokens, row_memory, row_dec, row_enc, row_cot = items

        def run(hidden, mem, w_query, w_keyval, w_output, w_inner, w_outer, gains):
            return layer(hidden, mem, row_dec, row_enc, w_query, w_keyval, w_output, w_inner, w_outer, gains)
        result, pull = jax.vjp(run, row_tokens.astype(jnp.float32), row_memory.astype(jnp.float32), rounded[0], rounded[1], rounded[2], rounded[3], rounded[4], rounded[5])
        grads = pull(row_cot.astype(jnp.float32))
        total = tuple((a + b for a, b in zip(total, grads[2:])))
        return (total, (result.astype(jnp.bfloat16), grads[0], grads[1]))
    zeros = tuple((jnp.zeros(w.shape, jnp.float32) for w in rounded))
    totals, outs = lax.scan(per_row, zeros, (tokens, memory, dec_ids, enc_ids, cotangent))
    block_out, input_grad, memory_grad = outs
    rate = RATE / math.sqrt(ROWS * LEN)
    output_rate = OUTPUT_RATE / math.sqrt(ROWS * LEN)
    new_query = advance(query_weight, query_moment, query_trail, totals[0], rate)
    new_keyval = advance(keyval_weight, keyval_moment, keyval_trail, totals[1], rate)
    new_output = advance(output_weight, output_moment, output_trail, totals[2], output_rate)
    new_inner = advance(inner_weight, inner_moment, inner_trail, totals[3], rate)
    new_outer = advance(outer_weight, outer_moment, outer_trail, totals[4], rate)
    new_gains = advance(norm_gains, gains_moment, gains_trail, totals[5], rate)
    return (block_out, input_grad, memory_grad, new_query[0], new_query[1], new_query[2], new_query[3], new_keyval[0], new_keyval[1], new_keyval[2], new_keyval[3], new_output[0], new_output[1], new_output[2], new_output[3], new_inner[0], new_inner[1], new_inner[2], new_inner[3], new_outer[0], new_outer[1], new_outer[2], new_outer[3], new_gains[0], new_gains[1], new_gains[2], new_gains[3])
```

```python
import math

import jax
import jax.numpy as jnp
from jax import lax
from jax.experimental import pallas as pl
from jax.experimental.pallas import tpu as pltpu
from jax.sharding import PartitionSpec as P

HDIM = 64
PAIR = 2 * HDIM
EPS = 1e-06
NEG = -1e30
RATE = 0.02
OUTPUT_RATE = 0.15
BF16 = jnp.bfloat16
F32 = jnp.float32


def dot(left, right, sides):
    return lax.dot_general(
        left, right, (((sides[0],), (sides[1],)), ((), ())), preferred_element_type=F32
    )


def matmul(left, right):
    return dot(left, right, (1, 0))


def matmul_right(left, right):
    return dot(left, right, (1, 1))


def matmul_left(left, right):
    return dot(left, right, (0, 0))


def in_group(block, group):
    low = lax.broadcasted_iota(jnp.int32, block.shape, 1) < HDIM
    turned = jnp.concatenate([block[:, HDIM:], block[:, :HDIM]], axis=1)
    zero = jnp.zeros_like(block)
    if group == 0:
        return jnp.where(low, block, zero), jnp.where(low, turned, zero)
    return jnp.where(low, zero, turned), jnp.where(low, zero, block)


def forward_kernel(query_ref, key_ref, value_ref, bias_ref, out_ref, stat_ref):
    keys = key_ref[...]
    values = value_ref[...].T
    for group in range(2):
        columns = slice(group * PAIR, (group + 1) * PAIR)
        rows = slice(group * HDIM, (group + 1) * HDIM)
        block = query_ref[:, columns] * jnp.asarray(HDIM**-0.5, BF16)
        parts = []
        for side, query in enumerate(in_group(block, group)):
            logits = dot(keys, query, (1, 1)) + bias_ref[...]
            peak = jnp.max(logits, axis=0, keepdims=True)
            weights = jnp.exp(logits - peak)
            total = jnp.sum(weights, axis=0, keepdims=True)
            probs = (weights * (1.0 / total)).astype(BF16)
            parts.append(dot(values, probs, (1, 0))[rows])
            stat_ref[0, pl.ds(2 * group + side, 1), :] = peak + jnp.log(total)
        out_ref[:, columns] = jnp.concatenate(parts, axis=0).T.astype(BF16)


def backward_kernel(
    query_ref, key_ref, value_ref, grad_ref, bias_ref, stat_ref, dquery_ref, dkey_ref, dvalue_ref
):
    keys = key_ref[...]
    values = value_ref[...]
    keys_turned = keys.T
    dkey, dvalue = None, None
    for group in range(2):
        columns = slice(group * PAIR, (group + 1) * PAIR)
        rows = slice(group * HDIM, (group + 1) * HDIM)
        queries = in_group(query_ref[:, columns] * jnp.asarray(HDIM**-0.5, BF16), group)
        grads = in_group(grad_ref[:, columns], group)
        parts = []
        for side in range(2):
            logits = dot(keys, queries[side], (1, 1)) + bias_ref[...]
            probs = jnp.exp(logits - stat_ref[0, pl.ds(2 * group + side, 1), :])
            dprobs = dot(values, grads[side], (1, 1))
            dots = jnp.sum(probs * dprobs, axis=0, keepdims=True)
            dlogits = (probs * (dprobs - dots)).astype(BF16)
            parts.append(dot(keys_turned, dlogits, (1, 0))[rows])
            more_key = dot(dlogits, queries[side], (1, 0))
            more_value = dot(probs.astype(BF16), grads[side], (1, 0))
            dkey = more_key if dkey is None else dkey + more_key
            dvalue = more_value if dvalue is None else dvalue + more_value
        dquery_ref[:, columns] = (jnp.concatenate(parts, axis=0).T * HDIM**-0.5).astype(BF16)
    dkey_ref[...] = dkey
    dvalue_ref[...] = dvalue


def attention_specs(count, span, steps):
    query = pl.BlockSpec((count, 2 * PAIR), lambda i: (0, i))
    keys = pl.BlockSpec((span, PAIR), lambda i: (0, i))
    values = pl.BlockSpec((span, PAIR), lambda i: (0, i + steps))
    bias = pl.BlockSpec((span, count), lambda i: (0, 0))
    stat = pl.BlockSpec((1, 8, count), lambda i: (i, 0, 0))
    return query, keys, values, bias, stat


def attention(query, keyval, bias):
    count, width = query.shape
    span = keyval.shape[0]
    steps = width // (2 * PAIR)
    q_spec, k_spec, v_spec, b_spec, s_spec = attention_specs(count, span, steps)
    return pl.pallas_call(
        forward_kernel,
        grid=(steps,),
        in_specs=[q_spec, k_spec, v_spec, b_spec],
        out_specs=[q_spec, s_spec],
        out_shape=[
            jax.ShapeDtypeStruct((count, width), BF16),
            jax.ShapeDtypeStruct((steps, 8, count), F32),
        ],
        compiler_params=pltpu.CompilerParams(vmem_limit_bytes=48 * 2**20),
        cost_estimate=pl.CostEstimate(
            flops=4 * count * span * width, bytes_accessed=8 * span * width, transcendentals=0
        ),
    )(query, keyval, keyval, bias)


def attention_back(query, keyval, grad, bias, stat):
    count, width = query.shape
    span = keyval.shape[0]
    steps = width // (2 * PAIR)
    q_spec, k_spec, v_spec, b_spec, s_spec = attention_specs(count, span, steps)
    return pl.pallas_call(
        backward_kernel,
        grid=(steps,),
        in_specs=[q_spec, k_spec, v_spec, q_spec, b_spec, s_spec],
        out_specs=[q_spec, k_spec, k_spec],
        out_shape=[
            jax.ShapeDtypeStruct((count, width), BF16),
            jax.ShapeDtypeStruct((span, width // 2), F32),
            jax.ShapeDtypeStruct((span, width // 2), F32),
        ],
        compiler_params=pltpu.CompilerParams(vmem_limit_bytes=48 * 2**20),
        cost_estimate=pl.CostEstimate(
            flops=10 * count * span * width, bytes_accessed=16 * span * width, transcendentals=0
        ),
    )(query, keyval, keyval, grad, bias, stat)


def flip(value, bit):
    count = lax.axis_size("wide")
    return lax.ppermute(value, "wide", [(i, i ^ (1 << bit)) for i in range(count)])


def onward(value):
    count = lax.axis_size("narrow")
    return lax.ppermute(value, "narrow", [(i, (i + 1) % count) for i in range(count)])


def high_bits():
    return list(range(1, lax.axis_size("wide").bit_length() - 1))


def ring_gather(part):
    count = lax.axis_size("narrow")
    here = lax.axis_index("narrow")
    whole = lax.dynamic_update_index_in_dim(
        jnp.zeros((count,) + part.shape, part.dtype), part, here, 0
    )
    moving = part
    for step in range(1, count):
        moving = onward(moving)
        whole = lax.dynamic_update_index_in_dim(whole, moving, (here - step) % count, 0)
    return whole.reshape((count * part.shape[0],) + part.shape[1:])


def ring_scatter(value):
    count = lax.axis_size("narrow")
    here = lax.axis_index("narrow")
    blocks = value.reshape((count, value.shape[0] // count) + value.shape[1:])

    def block(step):
        return lax.dynamic_index_in_dim(blocks, (here - step) % count, 0, keepdims=False)

    moving = block(1)
    for step in range(2, count + 1):
        moving = onward(moving.astype(BF16)).astype(F32) + block(step % count)
    return moving


def gather_weight(shard, order):
    here = lax.axis_index("wide")
    blocks = {0: ring_gather(shard)}
    for bit in order:
        blocks |= {mask ^ (1 << bit): flip(part, bit) for mask, part in blocks.items()}
    own = jnp.zeros((len(blocks),) + blocks[0].shape, shard.dtype)
    for mask, part in blocks.items():
        own = lax.dynamic_update_index_in_dim(own, part, (here ^ mask) >> 1, 0)
    own = own.reshape((-1, shard.shape[1]))
    return own, flip(own, 0)


def scatter_grad(left, right, order):
    here = lax.axis_index("wide")
    half = left.shape[1] // 2
    away = flip(matmul_left(left[:, half:], right).astype(BF16), 0)
    mine = (matmul_left(left[:, :half], right) + away.astype(F32)).astype(BF16)
    bits = sorted(order, reverse=True)
    mine = mine.reshape((2,) * len(bits) + (-1, right.shape[1]))
    for bit in reversed(order):
        axis = bits.index(bit)
        bits.remove(bit)
        place = (here >> bit) & 1
        keep = lax.dynamic_index_in_dim(mine, place, axis, keepdims=False)
        send = lax.dynamic_index_in_dim(mine, 1 - place, axis, keepdims=False)
        mine = (keep.astype(F32) + flip(send, bit).astype(F32)).astype(BF16)
    return ring_scatter(mine)


def swap_order(value):
    sides = lax.axis_size("wide") // 2
    mine_first = lax.axis_index("wide") % 2 == 0
    rows, width = value.shape
    return rows, width, sides, mine_first


def to_own(value):
    rows, width, sides, even = swap_order(value)
    split = value.reshape(rows, sides, 2, width // (2 * sides))
    first, second = (split[:, :, i].reshape(rows, width // 2) for i in range(2))
    return jnp.where(
        even,
        jnp.concatenate([first, second], axis=1),
        jnp.concatenate([second, first], axis=1),
    )


def from_own(value):
    rows, width, sides, even = swap_order(value)
    own, other = (
        part.reshape(rows, sides, 1, width // (2 * sides))
        for part in (value[:, : width // 2], value[:, width // 2 :])
    )
    return jnp.where(
        even,
        jnp.concatenate([own, other], axis=2),
        jnp.concatenate([other, own], axis=2),
    ).reshape(rows, width)


def into(value, weight):
    half = value.shape[1] // 2
    return matmul(value[:, :half], weight[0]) + matmul(value[:, half:], weight[1])


def out_of(value, weight):
    return jnp.concatenate([matmul_right(value, part) for part in weight], axis=1)


def norm_scale(hidden):
    return lax.rsqrt(jnp.mean(hidden * hidden, axis=-1, keepdims=True) + EPS)


def rms_norm(hidden, gain):
    return hidden * norm_scale(hidden) * gain


def gated(gate, up):
    return jax.nn.gelu(gate) * up


def advance(master, moment, trail, grad, rate):
    new_moment = 0.5 * moment + 0.5 * grad
    new_master = master - rate * (grad + 0.5 * new_moment)
    new_trail = 0.5 * trail + 0.5 * new_master
    return (new_master, new_moment, new_trail, new_master.astype(BF16))


def after(value, earlier):
    return lax.optimization_barrier((value, earlier))[0]


def on_device(
    tokens,
    memory,
    dec_ids,
    enc_ids,
    cotangent,
    query_weight,
    query_moment,
    query_trail,
    keyval_weight,
    keyval_moment,
    keyval_trail,
    output_weight,
    output_moment,
    output_trail,
    inner_weight,
    inner_moment,
    inner_trail,
    outer_weight,
    outer_moment,
    outer_trail,
    norm_gains,
    gains_moment,
    gains_trail,
):
    order = high_bits()
    turned = order[::-1]
    rows, local_len, width = tokens.shape
    mem_local = memory.shape[1]
    narrow_count = lax.axis_size("narrow")
    seq_len = local_len * narrow_count
    depth = width // 2
    inner_width = outer_weight.shape[0]
    gain_cols = jnp.pad(norm_gains.astype(BF16).T, ((0, 0), (0, PAIR - norm_gains.shape[0])))
    q_shard, kv_shard, in_shard = (
        w.astype(BF16) for w in (query_weight, keyval_weight, inner_weight)
    )
    o_shard = output_weight.astype(BF16).transpose(0, 2, 1)
    out_shard = outer_weight.astype(BF16).T

    kv_one_gains = gather_weight(jnp.concatenate([kv_shard[0], gain_cols], axis=1), turned)
    w_q_one = gather_weight(q_shard[0], order)
    tokens_row = ring_gather(tokens.reshape(local_len, width))
    w_o_one = gather_weight(o_shard[0], order)
    w_kv_two = gather_weight(kv_shard[1], turned)
    memory_row = ring_gather(memory.reshape(mem_local, width))
    w_q_two = gather_weight(q_shard[1], order)
    w_o_two = gather_weight(o_shard[1], turned)
    w_gate = gather_weight(in_shard[:, :inner_width], order)
    w_up = gather_weight(in_shard[:, inner_width:], turned)
    w_out_one = gather_weight(out_shard[:, : inner_width // 2], order)
    w_out_two = gather_weight(out_shard[:, inner_width // 2 :], turned)

    kv_width = keyval_weight.shape[2]
    w_kv_one = tuple(part[:, :kv_width] for part in kv_one_gains)
    gains = jnp.concatenate([part[:, kv_width : kv_width + 3] for part in kv_one_gains], axis=0)
    gains = gains.astype(F32).T
    first = lax.axis_index("narrow") * local_len
    dec_row, enc_row = dec_ids[0], enc_ids[0]
    own_ids = lax.dynamic_slice_in_dim(dec_row, first, local_len, 0)
    places = jnp.arange(seq_len, dtype=jnp.int32)
    own_places = first + jnp.arange(local_len, dtype=jnp.int32)
    self_bias = jnp.where(
        (own_ids[None, :] == dec_row[:, None]) & (own_places[None, :] >= places[:, None]), 0.0, NEG
    ).astype(F32)
    cross_bias = jnp.where(own_ids[None, :] == enc_row[:, None], 0.0, NEG).astype(F32)

    hidden = to_own(tokens.reshape(local_len, width)).astype(F32)
    normed_one = rms_norm(hidden, gains[0]).astype(BF16)
    normed_row = rms_norm(to_own(tokens_row).astype(F32), gains[0]).astype(BF16)
    query_one = into(normed_one, w_q_one).astype(BF16)
    keyval_one = into(normed_row, w_kv_one).astype(BF16)
    context_one, stat_one = attention(query_one, keyval_one, self_bias)
    after_one = hidden + out_of(context_one, w_o_one)
    normed_two = rms_norm(after_one, gains[1]).astype(BF16)
    query_two = into(normed_two, w_q_two).astype(BF16)
    keyval_two = into(to_own(memory_row), w_kv_two).astype(BF16)
    mem_own = to_own(memory.reshape(mem_local, width))
    context_two, stat_two = attention(query_two, keyval_two, cross_bias)
    after_two = after_one + out_of(context_two, w_o_two)
    normed_three = rms_norm(after_two, gains[2]).astype(BF16)
    gate = into(normed_three, w_gate)
    up = into(normed_three, w_up)
    activated = gated(gate, up).astype(BF16)
    act_one, act_two = activated[:, : inner_width // 2], activated[:, inner_width // 2 :]
    result = after_two + out_of(act_one, w_out_one) + out_of(act_two, w_out_two)
    block_out = from_own(result.astype(BF16)).reshape(rows, local_len, width)

    grad_ffn = to_own(cotangent.reshape(local_len, width))
    grad_out = grad_ffn.astype(F32)
    sum_out_one = scatter_grad(grad_ffn, act_one, order)
    sum_out_two = scatter_grad(grad_ffn, act_two, turned)
    grad_act = jnp.concatenate([into(grad_ffn, w_out_one), into(grad_ffn, w_out_two)], axis=1)
    grad_gate, grad_up = (g.astype(BF16) for g in jax.vjp(gated, gate, up)[1](grad_act))
    sum_gate = scatter_grad(normed_three, grad_gate, order)
    sum_up = scatter_grad(normed_three, grad_up, turned)
    grad_normed = out_of(grad_gate, w_gate) + out_of(grad_up, w_up)
    grad_hidden, grad_gain_three = jax.vjp(rms_norm, after_two, gains[2])[1](grad_normed)
    grad_two = grad_out + grad_hidden
    grad_branch = grad_two.astype(BF16)
    sum_o_two = scatter_grad(grad_branch, context_two, turned)
    grad_context = into(grad_branch, w_o_two).astype(BF16)
    query_grad_two, key_grad, value_grad = attention_back(
        query_two, keyval_two, grad_context, cross_bias, stat_two
    )
    sum_q_two = scatter_grad(normed_two, query_grad_two, order)
    grad_normed_two = out_of(query_grad_two, w_q_two)
    keyval_grad_two = ring_scatter(jnp.concatenate([key_grad, value_grad], axis=1)).astype(BF16)
    sum_kv_two = scatter_grad(mem_own, keyval_grad_two, turned)
    memory_grad = from_own(out_of(keyval_grad_two, w_kv_two)).reshape(rows, mem_local, width)
    grad_hidden, grad_gain_two = jax.vjp(rms_norm, after_one, gains[1])[1](grad_normed_two)
    grad_one = grad_two + grad_hidden
    grad_branch = grad_one.astype(BF16)
    sum_o_one = scatter_grad(grad_branch, context_one, order)
    grad_context = into(grad_branch, w_o_one).astype(BF16)
    query_grad_one, key_grad, value_grad = attention_back(
        query_one, keyval_one, grad_context, self_bias, stat_one
    )
    sum_q_one = scatter_grad(normed_one, query_grad_one, order)
    keyval_grad_one = ring_scatter(jnp.concatenate([key_grad, value_grad], axis=1)).astype(BF16)
    sum_kv_one = scatter_grad(normed_one, keyval_grad_one, turned)
    grad_normed_one = out_of(query_grad_one, w_q_one) + out_of(keyval_grad_one, w_kv_one)
    grad_hidden, grad_gain_one = jax.vjp(rms_norm, hidden, gains[0])[1](grad_normed_one)
    input_grad = from_own(grad_one + grad_hidden).reshape(rows, local_len, width)
    full_gains = jnp.stack([grad_gain_one, grad_gain_two, grad_gain_three])
    sum_gains = lax.psum_scatter(
        from_own(full_gains), ("wide", "narrow"), scatter_dimension=1, tiled=True
    )
    sum_query = jnp.stack([sum_q_one, sum_q_two])
    sum_keyval = jnp.stack([sum_kv_one, sum_kv_two])
    sum_output = jnp.stack([sum_o_one, sum_o_two]).transpose(0, 2, 1)
    sum_inner = jnp.concatenate([sum_gate, sum_up], axis=1)
    sum_outer = jnp.concatenate([sum_out_one, sum_out_two], axis=1).T
    token_total = rows * lax.axis_size("wide") * seq_len
    rate = RATE / math.sqrt(token_total)
    output_rate = OUTPUT_RATE / math.sqrt(token_total)
    new_query = advance(query_weight, query_moment, query_trail, sum_query, rate)
    new_keyval = advance(keyval_weight, keyval_moment, keyval_trail, sum_keyval, rate)
    new_output = advance(output_weight, output_moment, output_trail, sum_output, output_rate)
    new_inner = advance(inner_weight, inner_moment, inner_trail, sum_inner, rate)
    new_outer = advance(outer_weight, outer_moment, outer_trail, sum_outer, rate)
    new_gains = advance(norm_gains, gains_moment, gains_trail, sum_gains, rate)
    return (
        block_out,
        input_grad,
        memory_grad,
        new_query[0],
        new_query[1],
        new_query[2],
        new_query[3],
        new_keyval[0],
        new_keyval[1],
        new_keyval[2],
        new_keyval[3],
        new_output[0],
        new_output[1],
        new_output[2],
        new_output[3],
        new_inner[0],
        new_inner[1],
        new_inner[2],
        new_inner[3],
        new_outer[0],
        new_outer[1],
        new_outer[2],
        new_outer[3],
        new_gains[0],
        new_gains[1],
        new_gains[2],
        new_gains[3],
    )


def solution(mesh):
    in_specs = (
        P("wide", "narrow", None),
        P("wide", "narrow", None),
        P("wide", None),
        P("wide", None),
        P("wide", "narrow", None),
        P(None, ("wide", "narrow"), None),
        P(None, ("wide", "narrow"), None),
        P(None, ("wide", "narrow"), None),
        P(None, ("wide", "narrow"), None),
        P(None, ("wide", "narrow"), None),
        P(None, ("wide", "narrow"), None),
        P(None, None, ("wide", "narrow")),
        P(None, None, ("wide", "narrow")),
        P(None, None, ("wide", "narrow")),
        P(("wide", "narrow"), None),
        P(("wide", "narrow"), None),
        P(("wide", "narrow"), None),
        P(None, ("wide", "narrow")),
        P(None, ("wide", "narrow")),
        P(None, ("wide", "narrow")),
        P(None, ("wide", "narrow")),
        P(None, ("wide", "narrow")),
        P(None, ("wide", "narrow")),
    )
    out_specs = (
        P("wide", "narrow", None),
        P("wide", "narrow", None),
        P("wide", "narrow", None),
        P(None, ("wide", "narrow"), None),
        P(None, ("wide", "narrow"), None),
        P(None, ("wide", "narrow"), None),
        P(None, ("wide", "narrow"), None),
        P(None, ("wide", "narrow"), None),
        P(None, ("wide", "narrow"), None),
        P(None, ("wide", "narrow"), None),
        P(None, ("wide", "narrow"), None),
        P(None, None, ("wide", "narrow")),
        P(None, None, ("wide", "narrow")),
        P(None, None, ("wide", "narrow")),
        P(None, None, ("wide", "narrow")),
        P(("wide", "narrow"), None),
        P(("wide", "narrow"), None),
        P(("wide", "narrow"), None),
        P(("wide", "narrow"), None),
        P(None, ("wide", "narrow")),
        P(None, ("wide", "narrow")),
        P(None, ("wide", "narrow")),
        P(None, ("wide", "narrow")),
        P(None, ("wide", "narrow")),
        P(None, ("wide", "narrow")),
        P(None, ("wide", "narrow")),
        P(None, ("wide", "narrow")),
    )
    return jax.shard_map(
        on_device, mesh=mesh, in_specs=in_specs, out_specs=out_specs, check_vma=False
    )
```

```python
import math

import jax
import jax.numpy as jnp
from jax import lax
from jax.experimental import pallas as pl
from jax.experimental.pallas import tpu as pltpu
from jax.sharding import PartitionSpec as P

HDIM = 64
PAIR = 2 * HDIM
EPS = 1e-06
NEG = -1e30
RATE = 0.02
OUTPUT_RATE = 0.15
BF16 = jnp.bfloat16
F32 = jnp.float32


def dot(left, right, sides):
    return lax.dot_general(
        left, right, (((sides[0],), (sides[1],)), ((), ())), preferred_element_type=F32
    )


def matmul(left, right):
    return dot(left, right, (1, 0))


def matmul_right(left, right):
    return dot(left, right, (1, 1))


def matmul_left(left, right):
    return dot(left, right, (0, 0))


def in_group(block, group):
    low = lax.broadcasted_iota(jnp.int32, block.shape, 1) < HDIM
    turned = jnp.concatenate([block[:, HDIM:], block[:, :HDIM]], axis=1)
    zero = jnp.zeros_like(block)
    if group == 0:
        return jnp.where(low, block, zero), jnp.where(low, turned, zero)
    return jnp.where(low, zero, turned), jnp.where(low, zero, block)


def forward_kernel(query_ref, key_ref, value_ref, bias_ref, out_ref, stat_ref):
    keys = key_ref[...]
    values = value_ref[...].T
    for group in range(2):
        columns = slice(group * PAIR, (group + 1) * PAIR)
        rows = slice(group * HDIM, (group + 1) * HDIM)
        block = query_ref[:, columns] * jnp.asarray(HDIM**-0.5, BF16)
        parts = []
        for side, query in enumerate(in_group(block, group)):
            logits = dot(keys, query, (1, 1)) + bias_ref[...]
            peak = jnp.max(logits, axis=0, keepdims=True)
            weights = jnp.exp(logits - peak)
            total = jnp.sum(weights, axis=0, keepdims=True)
            probs = (weights * (1.0 / total)).astype(BF16)
            parts.append(dot(values, probs, (1, 0))[rows])
            stat_ref[0, pl.ds(2 * group + side, 1), :] = peak + jnp.log(total)
        out_ref[:, columns] = jnp.concatenate(parts, axis=0).T.astype(BF16)


def backward_kernel(
    query_ref, key_ref, value_ref, grad_ref, bias_ref, stat_ref, dquery_ref, dkey_ref, dvalue_ref
):
    keys = key_ref[...]
    values = value_ref[...]
    keys_turned = keys.T
    dkey, dvalue = None, None
    for group in range(2):
        columns = slice(group * PAIR, (group + 1) * PAIR)
        rows = slice(group * HDIM, (group + 1) * HDIM)
        queries = in_group(query_ref[:, columns] * jnp.asarray(HDIM**-0.5, BF16), group)
        grads = in_group(grad_ref[:, columns], group)
        parts = []
        for side in range(2):
            logits = dot(keys, queries[side], (1, 1)) + bias_ref[...]
            probs = jnp.exp(logits - stat_ref[0, pl.ds(2 * group + side, 1), :])
            dprobs = dot(values, grads[side], (1, 1))
            dots = jnp.sum(probs * dprobs, axis=0, keepdims=True)
            dlogits = (probs * (dprobs - dots)).astype(BF16)
            parts.append(dot(keys_turned, dlogits, (1, 0))[rows])
            more_key = dot(dlogits, queries[side], (1, 0))
            more_value = dot(probs.astype(BF16), grads[side], (1, 0))
            dkey = more_key if dkey is None else dkey + more_key
            dvalue = more_value if dvalue is None else dvalue + more_value
        dquery_ref[:, columns] = (jnp.concatenate(parts, axis=0).T * HDIM**-0.5).astype(BF16)
    dkey_ref[...] = dkey.astype(BF16)
    dvalue_ref[...] = dvalue.astype(BF16)


def attention_specs(count, span, steps):
    query = pl.BlockSpec((count, 2 * PAIR), lambda i: (0, i))
    keys = pl.BlockSpec((span, PAIR), lambda i: (0, i))
    values = pl.BlockSpec((span, PAIR), lambda i: (0, i + steps))
    bias = pl.BlockSpec((span, count), lambda i: (0, 0))
    stat = pl.BlockSpec((1, 8, count), lambda i: (i, 0, 0))
    return query, keys, values, bias, stat


def attention(query, keyval, bias):
    count, width = query.shape
    span = keyval.shape[0]
    steps = width // (2 * PAIR)
    q_spec, k_spec, v_spec, b_spec, s_spec = attention_specs(count, span, steps)
    return pl.pallas_call(
        forward_kernel,
        grid=(steps,),
        in_specs=[q_spec, k_spec, v_spec, b_spec],
        out_specs=[q_spec, s_spec],
        out_shape=[
            jax.ShapeDtypeStruct((count, width), BF16),
            jax.ShapeDtypeStruct((steps, 8, count), F32),
        ],
        compiler_params=pltpu.CompilerParams(vmem_limit_bytes=48 * 2**20),
        cost_estimate=pl.CostEstimate(
            flops=4 * count * span * width, bytes_accessed=8 * span * width, transcendentals=0
        ),
    )(query, keyval, keyval, bias)


def attention_back(query, keyval, grad, bias, stat):
    count, width = query.shape
    span = keyval.shape[0]
    steps = width // (2 * PAIR)
    q_spec, k_spec, v_spec, b_spec, s_spec = attention_specs(count, span, steps)
    return pl.pallas_call(
        backward_kernel,
        grid=(steps,),
        in_specs=[q_spec, k_spec, v_spec, q_spec, b_spec, s_spec],
        out_specs=[q_spec, k_spec, k_spec],
        out_shape=[
            jax.ShapeDtypeStruct((count, width), BF16),
            jax.ShapeDtypeStruct((span, width // 2), BF16),
            jax.ShapeDtypeStruct((span, width // 2), BF16),
        ],
        compiler_params=pltpu.CompilerParams(vmem_limit_bytes=48 * 2**20),
        cost_estimate=pl.CostEstimate(
            flops=10 * count * span * width, bytes_accessed=16 * span * width, transcendentals=0
        ),
    )(query, keyval, keyval, grad, bias, stat)


def flip(value, bit):
    count = lax.axis_size("wide")
    return lax.ppermute(value, "wide", [(i, i ^ (1 << bit)) for i in range(count)])


def shift(value, step):
    count = lax.axis_size("narrow")
    return lax.ppermute(value, "narrow", [(i, (i + step) % count) for i in range(count)])


def sync(*values):
    return lax.optimization_barrier(values)


def sync_pieces(pieces, *more):
    arrays, more = sync([piece for piece, _, _ in pieces], more)
    return ([(array, *rest) for array, (_, *rest) in zip(arrays, pieces)], *more)


def place_kernel(jobs, spot_ref, *refs):
    count = sum(len(pieces) for pieces, _ in jobs)
    sources, targets = iter(refs[:count]), iter(refs[count:])
    for pieces, widths in jobs:
        outs, first = [], 0
        for width in widths:
            outs.append((next(targets), first, width))
            first += width
        for (rows, wide), number, begin in pieces:
            source = next(sources)
            spot = pl.multiple_of(spot_ref[number] * rows, rows)
            for target, first, width in outs:
                low, high = max(begin, first), min(begin + wide, first + width)
                if low < high:
                    target[pl.ds(spot, rows), low - first : high - first] = source[
                        :, low - begin : high - begin
                    ]


def place(groups, spots, widths):
    jobs = [
        (tuple((piece.shape, number, begin) for piece, number, begin in pieces), cut)
        for pieces, cut in zip(groups, widths)
    ]
    flat = [piece for pieces in groups for piece, _, _ in pieces]
    out_shape = [
        jax.ShapeDtypeStruct(
            ((1 + max(number for _, number, _ in pieces)) * pieces[0][0].shape[0], part), BF16
        )
        for pieces, cut in zip(groups, widths)
        for part in cut
    ]
    if flat[0].shape[0] % 16:
        outs = []
        for pieces, cut in zip(groups, widths):
            rows = pieces[0][0].shape[0]
            whole = jnp.zeros((out_shape[len(outs)].shape[0], sum(cut)), BF16)
            for piece, number, begin in pieces:
                whole = lax.dynamic_update_slice(whole, piece, (spots[number] * rows, begin))
            first = 0
            for part in cut:
                outs.append(whole[:, first : first + part])
                first += part
        return outs
    size = sum(piece.size for piece in flat) * 2
    whole = pl.BlockSpec(memory_space=pltpu.VMEM)
    return pl.pallas_call(
        lambda *refs: place_kernel(jobs, *refs),
        in_specs=[pl.BlockSpec(memory_space=pltpu.SMEM)] + [whole] * len(flat),
        out_specs=[whole] * len(out_shape),
        out_shape=out_shape,
        compiler_params=pltpu.CompilerParams(vmem_limit_bytes=48 * 2**20),
        cost_estimate=pl.CostEstimate(flops=0, bytes_accessed=2 * size, transcendentals=0),
    )(spots, *flat)


def spread(value):
    count = lax.axis_size("narrow")
    return [value] + [shift(value, step) for step in range(1, count)]


def spread_join(pieces):
    count = lax.axis_size("narrow")
    spots = (lax.axis_index("narrow") - jnp.arange(count, dtype=jnp.int32)) % count
    numbered = [(piece, number, 0) for number, piece in enumerate(pieces)]
    return place([numbered], spots, [(pieces[0].shape[1],)])[0]


def collect(value):
    count = lax.axis_size("narrow")
    here = lax.axis_index("narrow")
    rows = value.shape[0] // count

    def block(step):
        return lax.dynamic_slice_in_dim(value, (here + step) % count * rows, rows, 0)

    return [block(0)] + [shift(block(step), step) for step in range(1, count)]


def total(parts):
    return sum(part.astype(F32) for part in parts)


def high_bits():
    return list(range(1, lax.axis_size("wide").bit_length() - 1))


def mirror_first(value):
    return {0: value} | {1 << bit: flip(value, bit) for bit in high_bits()}


def mirror_rest(known):
    bits = high_bits()
    width = known[0].shape[1]
    middle = width // (2 * PAIR) * PAIR
    pieces = [(value, mask >> 1, 0) for mask, value in known.items()]
    for order, low, high in ((bits, 0, middle), (bits[::-1], middle, width)):
        have = {0: known[0][:, low:high]}
        for bit in order:
            have |= {
                mask ^ (1 << bit): known[1 << bit][:, low:high] if mask == 0 else flip(part, bit)
                for mask, part in have.items()
            }
        pieces += [(part, mask >> 1, low) for mask, part in have.items() if mask not in known]
    return pieces


def mirror_join(pieces):
    count = lax.axis_size("wide") // 2
    width = pieces[0][0].shape[1]
    own = place([pieces], jnp.arange(count, dtype=jnp.int32), [(width,)])[0]
    return own, flip(own, 0)


def columns(weight, first, width):
    return tuple(part[:, first : first + width] for part in weight)


class Sum:
    def __init__(self, left, right, turned):
        bits = high_bits()
        self.order = bits if turned else bits[::-1]
        sides = 1 << len(bits)
        masks = sorted(
            range(sides),
            key=lambda mask: [-((mask << 1) >> bit & 1) for bit in self.order[:1]]
            + [(mask << 1) >> bit & 1 for bit in self.order[1:]],
        )
        half = left.shape[1] // 2
        cut = half // sides

        def pick(start, chosen):
            return jnp.concatenate(
                [left[:, start + mask * cut : start + (mask + 1) * cut] for mask in chosen], axis=1
            )

        self.mine = [pick(0, masks[: sides // 2]), pick(0, masks[sides // 2 :])]
        self.right = right
        self.state = [matmul_left(pick(half, masks), right).astype(BF16)]

    def over_core(self):
        self.state = [flip(part, 0) for part in self.state]
        return self

    def add_own(self):
        away = self.state[0]
        rows = away.shape[0] // 2
        self.state = [
            (matmul_left(left, self.right) + part.astype(F32)).astype(BF16)
            for left, part in zip(self.mine, (away[:rows], away[rows:]))
        ]
        return self

    def over_first(self):
        self.state = [flip(self.state[0], self.order[0]), self.state[1]]
        return self

    def whole(self):
        return (self.state[0].astype(F32) + self.state[1].astype(F32)).astype(BF16)

    def over_rest(self):
        for bit in self.order[1:]:
            whole = self.whole()
            rows = whole.shape[0] // 2
            self.state = [flip(whole[rows:], bit), whole[:rows]]
        return self


def over_chain(sums):
    return collect(jnp.concatenate([one.whole() for one in sums], axis=1))


def hold(sums, *values):
    flat, tree = jax.tree.flatten(([one.state for one in sums], values))
    states, values = jax.tree.unflatten(tree, lax.optimization_barrier(flat))
    for one, state in zip(sums, states):
        one.state = state
    return values


def block_order():
    count = lax.axis_size("wide")
    here = lax.axis_index("wide")
    masks = [mask << 1 for mask in range(count // 2)]
    return [here ^ mask for mask in masks + [mask + 1 for mask in masks]]


def blocks_kernel(count, spot_ref, *refs):
    for source, target in zip(refs[: len(refs) // 2], refs[len(refs) // 2 :]):
        width = source.shape[1] // count
        for number in range(count):
            spot = pl.multiple_of(spot_ref[number] * width, PAIR)
            target[:, number * width : (number + 1) * width] = source[:, pl.ds(spot, width)]


def blocks(values, spots):
    count = len(spots)
    whole = pl.BlockSpec(memory_space=pltpu.VMEM)
    return pl.pallas_call(
        lambda *refs: blocks_kernel(count, *refs),
        in_specs=[pl.BlockSpec(memory_space=pltpu.SMEM)] + [whole] * len(values),
        out_specs=[whole] * len(values),
        out_shape=[jax.ShapeDtypeStruct(value.shape, value.dtype) for value in values],
        compiler_params=pltpu.CompilerParams(vmem_limit_bytes=48 * 2**20),
        cost_estimate=pl.CostEstimate(flops=0, bytes_accessed=2**22, transcendentals=0),
    )(jnp.stack(spots).astype(jnp.int32), *values)


def to_own(*values):
    return blocks(values, block_order())


def from_own(*values):
    count = lax.axis_size("wide")
    here = lax.axis_index("wide")
    places = [((j ^ here) >> 1) + ((j ^ here) & 1) * (count // 2) for j in range(count)]
    return blocks(values, places)


def all_sum(value):
    for bit in range(lax.axis_size("wide").bit_length() - 1):
        value = value + flip(value, bit)
    count = lax.axis_size("narrow")
    return sum([value] + [shift(value, step) for step in range(1, count)])


def shard_place():
    return lax.axis_index("wide") * lax.axis_size("narrow") + lax.axis_index("narrow")


def into(value, weight):
    half = value.shape[1] // 2
    return matmul(value[:, :half], weight[0]) + matmul(value[:, half:], weight[1])


def out_of(value, weight):
    return jnp.concatenate([matmul_right(value, part) for part in weight], axis=1)


def rms_norm(hidden, gain):
    return hidden * lax.rsqrt(jnp.mean(hidden * hidden, axis=-1, keepdims=True) + EPS) * gain


def gated(gate, up):
    return jax.nn.gelu(gate) * up


def advance(master, moment, trail, grad, rate):
    new_moment = 0.5 * moment + 0.5 * grad
    new_master = master - rate * (grad + 0.5 * new_moment)
    new_trail = 0.5 * trail + 0.5 * new_master
    return (new_master, new_moment, new_trail, new_master.astype(BF16))


def on_device(
    tokens,
    memory,
    dec_ids,
    enc_ids,
    cotangent,
    query_weight,
    query_moment,
    query_trail,
    keyval_weight,
    keyval_moment,
    keyval_trail,
    output_weight,
    output_moment,
    output_trail,
    inner_weight,
    inner_moment,
    inner_trail,
    outer_weight,
    outer_moment,
    outer_trail,
    norm_gains,
    gains_moment,
    gains_trail,
):
    rows, local_len, width = tokens.shape
    mem_local = memory.shape[1]
    narrow_count = lax.axis_size("narrow")
    seq_len = local_len * narrow_count
    inner_width = outer_weight.shape[0]
    half_inner = inner_width // 2
    q_width, kv_width = query_weight.shape[2], keyval_weight.shape[2]
    gain_count, gain_width = norm_gains.shape

    gain_cols = jnp.pad(norm_gains.astype(BF16).T, ((0, 0), (0, PAIR - gain_count)))
    shard0 = jnp.concatenate(
        [query_weight[0].astype(BF16), keyval_weight[0].astype(BF16), gain_cols], axis=1
    )
    g0 = spread(shard0)
    shard1 = jnp.concatenate(
        [
            output_weight[0].T.astype(BF16),
            query_weight[1].astype(BF16),
            keyval_weight[1].astype(BF16),
            output_weight[1].T.astype(BF16),
        ],
        axis=1,
    )
    shard2 = inner_weight.astype(BF16)
    shard3 = outer_weight.T.astype(BF16)
    tokens_own, memory_own, grad_ffn = to_own(
        tokens.reshape(local_len, width),
        memory.reshape(mem_local, width),
        cotangent.reshape(local_len, width),
    )
    first = lax.axis_index("narrow") * local_len
    dec_row, enc_row = dec_ids[0], enc_ids[0]
    own_ids = lax.dynamic_slice_in_dim(dec_row, first, local_len, 0)
    places = jnp.arange(seq_len, dtype=jnp.int32)
    own_places = first + jnp.arange(local_len, dtype=jnp.int32)
    self_bias = jnp.where(
        (own_ids[None, :] == dec_row[:, None]) & (own_places[None, :] >= places[:, None]), 0.0, NEG
    ).astype(F32)
    cross_bias = jnp.where(own_ids[None, :] == enc_row[:, None], 0.0, NEG).astype(F32)
    g0, shard1, tokens_own, memory_own, grad_ffn = sync(
        g0, shard1, tokens_own, memory_own, grad_ffn
    )
    g0 = mirror_first(spread_join(g0))
    g1 = spread(shard1)
    g0, shard2, shard3, self_bias, cross_bias = sync(g0, shard2, shard3, self_bias, cross_bias)
    g0 = mirror_rest(g0)
    g0, g1 = sync_pieces(g0, g1)
    row = spread(tokens_own)
    g1 = mirror_first(spread_join(g1))
    w_zero = mirror_join(g0)
    gains = jnp.concatenate(columns(w_zero, q_width + kv_width, gain_count), axis=0)
    gains = gains.astype(F32).T
    hidden = tokens_own.astype(F32)
    normed_one = rms_norm(hidden, gains[0]).astype(BF16)
    query_one = into(normed_one, columns(w_zero, 0, q_width)).astype(BF16)
    w_kv_one = columns(w_zero, q_width, kv_width)
    g1, query_one = sync(g1, query_one)
    g1 = mirror_rest(g1)
    g1, row = sync_pieces(g1, row)
    g2 = spread(shard2)
    w_one = mirror_join(g1)
    w_o_one, w_q_two = columns(w_one, 0, width), columns(w_one, width, q_width)
    w_kv_two = columns(w_one, width + q_width, kv_width)
    w_o_two = columns(w_one, width + q_width + kv_width, width)
    normed_row = rms_norm(spread_join(row).astype(F32), gains[0]).astype(BF16)
    keyval_one = into(normed_row, w_kv_one).astype(BF16)
    keyval_one, memory_own = sync(keyval_one, memory_own)
    row = spread(memory_own)
    context_one, stat_one = attention(query_one, keyval_one, self_bias)
    context_one, g2 = sync(context_one, g2)
    g2 = mirror_first(spread_join(g2))
    after_one = hidden + out_of(context_one, w_o_one)
    normed_two = rms_norm(after_one, gains[1]).astype(BF16)
    query_two = into(normed_two, w_q_two).astype(BF16)
    row, g2, query_two = sync(row, g2, query_two)
    shard3, query_two = sync(shard3, query_two)
    g3 = spread(shard3)
    g2 = mirror_rest(g2)
    keyval_two = into(spread_join(row), w_kv_two).astype(BF16)
    context_two, stat_two = attention(query_two, keyval_two, cross_bias)
    g2, g3, context_two = sync_pieces(g2, g3, context_two)
    g3 = mirror_first(spread_join(g3))
    w_in = mirror_join(g2)
    after_two = after_one + out_of(context_two, w_o_two)
    normed_three = rms_norm(after_two, gains[2]).astype(BF16)
    g3, w_in, normed_three = sync(g3, w_in, normed_three)
    g3 = mirror_rest(g3)
    gate = into(normed_three, columns(w_in, 0, inner_width))
    up = into(normed_three, columns(w_in, inner_width, inner_width))
    activated = gated(gate, up).astype(BF16)
    act_one, act_two = activated[:, :half_inner], activated[:, half_inner:]
    sum_outs = [Sum(grad_ffn, act_one, False), Sum(grad_ffn, act_two, True)]
    for one in sum_outs:
        one.over_core()
    (activated,) = hold(sum_outs, activated)
    g3, activated = sync_pieces(g3, activated)
    w_out = mirror_join(g3)
    for one in sum_outs:
        one.add_own().over_first()
    grad_act = into(grad_ffn, w_out)
    grad_gate, grad_up = (g.astype(BF16) for g in jax.vjp(gated, gate, up)[1](grad_act))
    sum_ins = [Sum(normed_three, grad_gate, False), Sum(normed_three, grad_up, True)]
    grad_gate, grad_up = hold(sum_ins, grad_gate, grad_up)
    for one in sum_ins:
        one.over_core()
    result = after_two + out_of(activated, w_out)
    (block_out,) = from_own(result.astype(BF16))
    grad_normed = out_of(grad_gate, columns(w_in, 0, inner_width)) + out_of(
        grad_up, columns(w_in, inner_width, inner_width)
    )
    grad_hidden, grad_gain_three = jax.vjp(rms_norm, after_two, gains[2])[1](grad_normed)
    grad_two = grad_ffn.astype(F32) + grad_hidden
    grad_branch = grad_two.astype(BF16)
    grad_context = into(grad_branch, w_o_two).astype(BF16)
    grad_branch, grad_context, block_out = hold(
        sum_ins + sum_outs, grad_branch, grad_context, block_out
    )
    for one in sum_ins:
        one.add_own().over_first()
    for one in sum_outs:
        one.over_rest()
    sum_o_two = Sum(grad_branch, context_two, False)
    (grad_context,) = hold([sum_o_two], grad_context)
    sum_o_two.over_core()
    query_grad_two, key_grad, value_grad = attention_back(
        query_two, keyval_two, grad_context, cross_bias, stat_two
    )
    query_grad_two, key_grad, value_grad = hold(
        sum_outs + [sum_o_two], query_grad_two, key_grad, value_grad
    )
    keyval_parts = collect(jnp.concatenate([key_grad, value_grad], axis=1))
    outer_parts = over_chain(sum_outs)
    sum_q_two = Sum(normed_two, query_grad_two, True).over_core()
    grad_normed_two = out_of(query_grad_two, w_q_two)
    grad_hidden, grad_gain_two = jax.vjp(rms_norm, after_one, gains[1])[1](grad_normed_two)
    grad_one = grad_two + grad_hidden
    grad_branch = grad_one.astype(BF16)
    grad_context = into(grad_branch, w_o_one).astype(BF16)
    grad_branch, grad_context = hold(sum_ins + [sum_q_two], grad_branch, grad_context)
    for one in sum_ins:
        one.over_rest()
    for one in (sum_o_two, sum_q_two):
        one.add_own().over_first()
    sum_o_one = Sum(grad_branch, context_one, False)
    (grad_context,) = hold([sum_o_one], grad_context)
    sum_o_one.over_core()
    query_grad_one, key_grad, value_grad = attention_back(
        query_one, keyval_one, grad_context, self_bias, stat_one
    )
    query_grad_one, key_grad, value_grad, keyval_parts, outer_parts = hold(
        sum_ins + [sum_o_two, sum_q_two, sum_o_one],
        query_grad_one,
        key_grad,
        value_grad,
        keyval_parts,
        outer_parts,
    )
    keyval_partial = jnp.concatenate([key_grad, value_grad], axis=1)
    parts_one = collect(keyval_partial)
    inner_parts = over_chain(sum_ins)
    for one in (sum_o_two, sum_q_two):
        one.over_rest()
    sum_q_one = Sum(normed_one, query_grad_one, False).over_core()
    sum_kv_one = Sum(normed_row, keyval_partial, True).over_core()
    keyval_grad_two = total(keyval_parts).astype(BF16)
    sum_kv_two = Sum(memory_own, keyval_grad_two, True).over_core()
    sum_o_one.add_own().over_first()
    (memory_grad,) = from_own(out_of(keyval_grad_two, w_kv_two))
    (memory_grad,) = hold([sum_q_one, sum_kv_one, sum_kv_two], memory_grad)
    for one in (sum_q_one, sum_kv_one, sum_kv_two):
        one.add_own().over_first()
    grad_part = out_of(query_grad_one, columns(w_zero, 0, q_width))
    (grad_part,) = hold([sum_o_two, sum_q_two, sum_o_one], grad_part)
    two_parts = over_chain([sum_o_two, sum_q_two])
    sum_o_one.over_rest()
    inner_parts, outer_parts = hold(
        [sum_o_one, sum_q_one, sum_kv_one, sum_kv_two], inner_parts, outer_parts
    )
    for one in (sum_q_one, sum_kv_one, sum_kv_two):
        one.over_rest()
    sum_inner = total(inner_parts)
    sum_outer = total(outer_parts).T
    parts_one, sum_inner, sum_outer = hold(
        [sum_o_one, sum_q_one, sum_kv_one, sum_kv_two], parts_one, sum_inner, sum_outer
    )
    last_parts = over_chain([sum_o_one, sum_kv_two, sum_q_one, sum_kv_one])
    keyval_grad_one = total(parts_one).astype(BF16)
    grad_normed_one = grad_part + out_of(keyval_grad_one, w_kv_one)
    grad_hidden, grad_gain_one = jax.vjp(rms_norm, hidden, gains[0])[1](grad_normed_one)
    (input_grad,) = from_own(grad_one + grad_hidden)
    (full_gains,) = from_own(jnp.stack([grad_gain_one, grad_gain_two, grad_gain_three]))
    sum_gains = lax.dynamic_slice_in_dim(
        all_sum(full_gains), shard_place() * gain_width, gain_width, 1
    )
    sum_two, sum_last = total(two_parts), total(last_parts)
    first_kv = width + kv_width + q_width
    sum_query = jnp.stack([sum_last[:, width + kv_width : first_kv], sum_two[:, width:]])
    sum_keyval = jnp.stack([sum_last[:, first_kv:], sum_last[:, width : width + kv_width]])
    sum_output = jnp.stack([sum_last[:, :width], sum_two[:, :width]]).transpose(0, 2, 1)
    block_out = block_out.reshape(rows, local_len, width)
    input_grad = input_grad.reshape(rows, local_len, width)
    memory_grad = memory_grad.reshape(rows, mem_local, width)
    token_total = rows * lax.axis_size("wide") * seq_len
    rate = RATE / math.sqrt(token_total)
    output_rate = OUTPUT_RATE / math.sqrt(token_total)
    new_query = advance(query_weight, query_moment, query_trail, sum_query, rate)
    new_keyval = advance(keyval_weight, keyval_moment, keyval_trail, sum_keyval, rate)
    new_output = advance(output_weight, output_moment, output_trail, sum_output, output_rate)
    new_inner = advance(inner_weight, inner_moment, inner_trail, sum_inner, rate)
    new_outer = advance(outer_weight, outer_moment, outer_trail, sum_outer, rate)
    new_gains = advance(norm_gains, gains_moment, gains_trail, sum_gains, rate)
    return (
        block_out,
        input_grad,
        memory_grad,
        new_query[0],
        new_query[1],
        new_query[2],
        new_query[3],
        new_keyval[0],
        new_keyval[1],
        new_keyval[2],
        new_keyval[3],
        new_output[0],
        new_output[1],
        new_output[2],
        new_output[3],
        new_inner[0],
        new_inner[1],
        new_inner[2],
        new_inner[3],
        new_outer[0],
        new_outer[1],
        new_outer[2],
        new_outer[3],
        new_gains[0],
        new_gains[1],
        new_gains[2],
        new_gains[3],
    )


def solution(mesh):
    in_specs = (
        P("wide", "narrow", None),
        P("wide", "narrow", None),
        P("wide", None),
        P("wide", None),
        P("wide", "narrow", None),
        P(None, ("wide", "narrow"), None),
        P(None, ("wide", "narrow"), None),
        P(None, ("wide", "narrow"), None),
        P(None, ("wide", "narrow"), None),
        P(None, ("wide", "narrow"), None),
        P(None, ("wide", "narrow"), None),
        P(None, None, ("wide", "narrow")),
        P(None, None, ("wide", "narrow")),
        P(None, None, ("wide", "narrow")),
        P(("wide", "narrow"), None),
        P(("wide", "narrow"), None),
        P(("wide", "narrow"), None),
        P(None, ("wide", "narrow")),
        P(None, ("wide", "narrow")),
        P(None, ("wide", "narrow")),
        P(None, ("wide", "narrow")),
        P(None, ("wide", "narrow")),
        P(None, ("wide", "narrow")),
    )
    out_specs = (
        P("wide", "narrow", None),
        P("wide", "narrow", None),
        P("wide", "narrow", None),
        P(None, ("wide", "narrow"), None),
        P(None, ("wide", "narrow"), None),
        P(None, ("wide", "narrow"), None),
        P(None, ("wide", "narrow"), None),
        P(None, ("wide", "narrow"), None),
        P(None, ("wide", "narrow"), None),
        P(None, ("wide", "narrow"), None),
        P(None, ("wide", "narrow"), None),
        P(None, None, ("wide", "narrow")),
        P(None, None, ("wide", "narrow")),
        P(None, None, ("wide", "narrow")),
        P(None, None, ("wide", "narrow")),
        P(("wide", "narrow"), None),
        P(("wide", "narrow"), None),
        P(("wide", "narrow"), None),
        P(("wide", "narrow"), None),
        P(None, ("wide", "narrow")),
        P(None, ("wide", "narrow")),
        P(None, ("wide", "narrow")),
        P(None, ("wide", "narrow")),
        P(None, ("wide", "narrow")),
        P(None, ("wide", "narrow")),
        P(None, ("wide", "narrow")),
        P(None, ("wide", "narrow")),
    )
    return jax.shard_map(
        on_device, mesh=mesh, in_specs=in_specs, out_specs=out_specs, check_vma=False
    )
```

```python
import math

import jax
import jax.numpy as jnp
from jax import lax
from jax.experimental import pallas as pl
from jax.experimental.pallas import tpu as pltpu
from jax.sharding import PartitionSpec as P

HDIM = 64
PAIR = 2 * HDIM
EPS = 1e-06
NEG = -1e30
RATE = 0.02
OUTPUT_RATE = 0.15
LIMIT = 16 * 2**20
BF16 = jnp.bfloat16
F32 = jnp.float32


def dot(left, right, sides):
    return lax.dot_general(
        left, right, (((sides[0],), (sides[1],)), ((), ())), preferred_element_type=F32
    )


def matmul(left, right):
    return dot(left, right, (1, 0))


def matmul_right(left, right):
    return dot(left, right, (1, 1))


def matmul_left(left, right):
    return dot(left, right, (0, 0))


def in_group(block, group):
    low = lax.broadcasted_iota(jnp.int32, block.shape, 1) < HDIM
    turned = jnp.concatenate([block[:, HDIM:], block[:, :HDIM]], axis=1)
    zero = jnp.zeros_like(block)
    if group == 0:
        return jnp.where(low, block, zero), jnp.where(low, turned, zero)
    return jnp.where(low, zero, turned), jnp.where(low, zero, block)


def allowed(kid_ref, qid_ref, bias_ref, span, order):
    keep = kid_ref[:span] == qid_ref[...]
    if order:
        count = qid_ref.shape[1]
        keys = lax.broadcasted_iota(jnp.int32, keep.shape, 0)
        queries = lax.broadcasted_iota(jnp.int32, keep.shape, 1) + pl.program_id(0) * count
        keep &= keys <= queries
    bias_ref[:span] = jnp.where(keep, 0.0, NEG).astype(F32)


def by_span(order, count, full, body):
    if not order:
        body(full)
        return
    for number in range(full // count):
        pl.when(pl.program_id(0) == number)(lambda number=number: body((number + 1) * count))


def forward_kernel(order, query_ref, key_ref, value_ref, kid_ref, qid_ref, *rest):
    out_ref, stat_ref, bias_ref = rest
    count, width = query_ref.shape

    def body(span):
        allowed(kid_ref, qid_ref, bias_ref, span, order)
        keys = key_ref[:span]
        values = value_ref[:span].T
        for group in range(width // PAIR):
            columns = slice(group * PAIR, (group + 1) * PAIR)
            rows = slice(group * HDIM, (group + 1) * HDIM)
            block = query_ref[:, columns] * jnp.asarray(HDIM**-0.5, BF16)
            parts = []
            for side, query in enumerate(in_group(block, group)):
                logits = dot(keys, query, (1, 1)) + bias_ref[:span]
                peak = jnp.max(logits, axis=0, keepdims=True)
                weights = jnp.exp(logits - peak)
                total = jnp.sum(weights, axis=0, keepdims=True)
                probs = (weights * (1.0 / total)).astype(BF16)
                parts.append(dot(values, probs, (1, 0))[rows])
                stat_ref[0, pl.ds(2 * group + side, 1), :] = peak + jnp.log(total)
            out_ref[:, columns] = jnp.concatenate(parts, axis=0).T.astype(BF16)

    by_span(order, count, key_ref.shape[0], body)


def backward_kernel(
    order, query_ref, key_ref, value_ref, kid_ref, qid_ref, grad_ref, stat_ref, *rest
):
    dquery_ref, dkeyval_ref, bias_ref, key_sum, value_sum = rest
    count, width = query_ref.shape

    @pl.when(pl.program_id(0) == 0)
    def _():
        key_sum[...] = jnp.zeros_like(key_sum)
        value_sum[...] = jnp.zeros_like(value_sum)

    def body(span):
        allowed(kid_ref, qid_ref, bias_ref, span, order)
        keys = key_ref[:span]
        values = value_ref[:span]
        keys_turned = keys.T
        dkey, dvalue = None, None
        for group in range(width // PAIR):
            columns = slice(group * PAIR, (group + 1) * PAIR)
            rows = slice(group * HDIM, (group + 1) * HDIM)
            queries = in_group(query_ref[:, columns] * jnp.asarray(HDIM**-0.5, BF16), group)
            grads = in_group(grad_ref[:, columns], group)
            parts = []
            for side in range(2):
                logits = dot(keys, queries[side], (1, 1)) + bias_ref[:span]
                probs = jnp.exp(logits - stat_ref[0, pl.ds(2 * group + side, 1), :])
                dprobs = dot(values, grads[side], (1, 1))
                dots = jnp.sum(probs * dprobs, axis=0, keepdims=True)
                dlogits = (probs * (dprobs - dots)).astype(BF16)
                parts.append(dot(keys_turned, dlogits, (1, 0))[rows])
                more_key = dot(dlogits, queries[side], (1, 0))
                more_value = dot(probs.astype(BF16), grads[side], (1, 0))
                dkey = more_key if dkey is None else dkey + more_key
                dvalue = more_value if dvalue is None else dvalue + more_value
            dquery_ref[:, columns] = (jnp.concatenate(parts, axis=0).T * HDIM**-0.5).astype(BF16)
        key_sum[:span] += dkey
        value_sum[:span] += dvalue

    by_span(order, count, key_ref.shape[0], body)

    @pl.when(pl.program_id(0) == pl.num_programs(0) - 1)
    def _():
        dkeyval_ref[:, :PAIR] = key_sum[...].astype(BF16)
        dkeyval_ref[:, PAIR:] = value_sum[...].astype(BF16)


def attention_specs(joint, count):
    span, width = joint.shape
    q_width = width - 2 * PAIR
    query = pl.BlockSpec((count, q_width), lambda i: (i, 0))
    keys = pl.BlockSpec((span, PAIR), lambda i: (0, q_width // PAIR))
    values = pl.BlockSpec((span, PAIR), lambda i: (0, q_width // PAIR + 1))
    key_ids = pl.BlockSpec((span, 1), lambda i: (0, 0))
    query_ids = pl.BlockSpec((1, count), lambda i: (0, i))
    stat = pl.BlockSpec((1, 8, count), lambda i: (i, 0, 0))
    return q_width, [query, keys, values, key_ids, query_ids], stat


def attention(joint, key_ids, query_ids, count, order):
    span = joint.shape[0]
    q_width, specs, s_spec = attention_specs(joint, count)
    return pl.pallas_call(
        lambda *refs: forward_kernel(order, *refs),
        grid=(span // count,),
        in_specs=specs,
        out_specs=[specs[0], s_spec],
        out_shape=[
            jax.ShapeDtypeStruct((span, q_width), BF16),
            jax.ShapeDtypeStruct((span // count, 8, count), F32),
        ],
        scratch_shapes=[pltpu.VMEM((span, count), F32)],
        compiler_params=pltpu.CompilerParams(vmem_limit_bytes=2 * LIMIT),
        cost_estimate=pl.CostEstimate(
            flops=4 * span * span * q_width, bytes_accessed=8 * span * q_width, transcendentals=0
        ),
    )(joint, joint, joint, key_ids, query_ids)


def attention_back(joint, grad, stat, key_ids, query_ids, count, order):
    span = joint.shape[0]
    q_width, specs, s_spec = attention_specs(joint, count)
    whole = pl.BlockSpec((span, 2 * PAIR), lambda i: (0, 0))
    return pl.pallas_call(
        lambda *refs: backward_kernel(order, *refs),
        grid=(span // count,),
        in_specs=specs + [specs[0], s_spec],
        out_specs=[specs[0], whole],
        out_shape=[
            jax.ShapeDtypeStruct((span, q_width), BF16),
            jax.ShapeDtypeStruct((span, 2 * PAIR), BF16),
        ],
        scratch_shapes=[
            pltpu.VMEM((span, count), F32),
            pltpu.VMEM((span, PAIR), F32),
            pltpu.VMEM((span, PAIR), F32),
        ],
        compiler_params=pltpu.CompilerParams(vmem_limit_bytes=2 * LIMIT),
        cost_estimate=pl.CostEstimate(
            flops=10 * span * span * q_width, bytes_accessed=16 * span * q_width, transcendentals=0
        ),
    )(joint, joint, joint, key_ids, query_ids, grad, stat)


def flip(value, bit):
    count = lax.axis_size("wide")
    return lax.ppermute(value, "wide", [(i, i ^ (1 << bit)) for i in range(count)])


def shift(value, step):
    count = lax.axis_size("narrow")
    return lax.ppermute(value, "narrow", [(i, (i + step) % count) for i in range(count)])


def sync(*values):
    return lax.optimization_barrier(values)


def place(pieces, widths):
    rows = pieces[0][0].shape[0]
    count = 1 + max(number for _, number, _ in pieces)

    def kernel(*refs):
        first = 0
        for target, cut in zip(refs[len(pieces) :], widths):
            for source, (piece, number, begin) in zip(refs, pieces):
                low, high = max(begin, first), min(begin + piece.shape[1], first + cut)
                if low < high:
                    target[number * rows : (number + 1) * rows, low - first : high - first] = source[
                        :, low - begin : high - begin
                    ]
            first += cut

    shapes = [jax.ShapeDtypeStruct((count * rows, cut), BF16) for cut in widths]
    return small_call(kernel, shapes, [piece for piece, _, _ in pieces])


def far(value):
    return pltpu.with_memory_space_constraint(value, pltpu.HBM)


def trade(value):
    return lax.all_to_all(value, "narrow", 0, 0, tiled=True)


def spread(value):
    count = lax.axis_size("narrow")
    return trade(jnp.concatenate([value] * count, axis=0))


def near_steps():
    return sorted({1, lax.axis_size("narrow") - 1})


def far_steps():
    return [s for s in range(1, lax.axis_size("narrow")) if s not in near_steps()]


def spread_steps(value, steps):
    return {step: shift(value, step) for step in steps}


def spread_join(value, came, *widths):
    count = lax.axis_size("narrow")
    pieces = [value] + [came[step] for step in sorted(came)]
    rows, width = value.shape
    widths = widths or (width,)
    firsts = [sum(widths[:number]) for number in range(len(widths))]
    spots = (lax.axis_index("narrow") - jnp.arange(count, dtype=jnp.int32)) % count
    if rows % 16:
        whole = jnp.zeros((count, rows, width), value.dtype)
        for number, piece in enumerate(pieces):
            whole = lax.dynamic_update_index_in_dim(whole, piece, spots[number], 0)
        whole = whole.reshape(count * rows, width)
        return [whole[:, first : first + wide] for first, wide in zip(firsts, widths)]

    def kernel(spot_ref, *refs):
        for number, source in enumerate(refs[:count]):
            spot = pl.multiple_of(spot_ref[number] * rows, rows)
            for target, first, wide in zip(refs[count:], firsts, widths):
                target[pl.ds(spot, rows), :] = source[:, first : first + wide]

    whole = pl.BlockSpec(memory_space=pltpu.VMEM)
    return pl.pallas_call(
        kernel,
        in_specs=[pl.BlockSpec(memory_space=pltpu.SMEM)] + [whole] * count,
        out_specs=[whole] * len(widths),
        out_shape=[jax.ShapeDtypeStruct((count * rows, wide), value.dtype) for wide in widths],
        compiler_params=pltpu.CompilerParams(vmem_limit_bytes=LIMIT),
        cost_estimate=pl.CostEstimate(flops=0, bytes_accessed=2**22, transcendentals=0),
    )(spots, *pieces)


def tight(width):
    return -(-width // PAIR) * PAIR


def cut_columns(parts):
    count = lax.axis_size("narrow")
    rows = parts[0].shape[0]
    shares = [part.shape[1] // count for part in parts]
    width = sum(tight(share) for share in shares)

    def kernel(*refs):
        target = refs[-1]
        for number in range(count):
            first = 0
            for source, share in zip(refs, shares):
                block = source[:, number * share : (number + 1) * share]
                if share % PAIR:
                    zeros = jnp.zeros((rows, tight(share) - share), BF16)
                    block = jnp.concatenate([block, zeros], axis=1)
                target[number * rows : (number + 1) * rows, first : first + tight(share)] = block
                first += tight(share)

    return small_call(kernel, [jax.ShapeDtypeStruct((count * rows, width), BF16)], parts)[0]


def join_columns(value, share, kinds=1):
    count = lax.axis_size("narrow")
    rows = value.shape[0] // count

    def kernel(source, target):
        for kind in range(kinds):
            for number in range(count):
                place = (kind * count + number) * share
                target[:, place : place + share] = source[
                    number * rows : (number + 1) * rows,
                    kind * tight(share) : kind * tight(share) + share,
                ]

    shape = jax.ShapeDtypeStruct((rows, kinds * share * count), BF16)
    return small_call(kernel, [shape], (value,))[0]


def vmem(*arrays):
    size = sum(math.prod(shape) * jnp.dtype(kind).itemsize for shape, kind in arrays)
    return pltpu.CompilerParams(vmem_limit_bytes=min(56 * 2**20, max(LIMIT, size + LIMIT)))


def small_call(kernel, out_shape, args):
    whole = pl.BlockSpec(memory_space=pltpu.VMEM)
    return pl.pallas_call(
        kernel,
        in_specs=[whole] * len(args),
        out_specs=[whole] * len(out_shape),
        out_shape=out_shape,
        compiler_params=vmem(*[(v.shape, v.dtype) for v in (*args, *out_shape)]),
        cost_estimate=pl.CostEstimate(flops=0, bytes_accessed=2**22, transcendentals=0),
    )(*args)


def total(value):
    count = lax.axis_size("narrow")
    return jnp.sum(value.reshape((count, -1) + value.shape[1:]).astype(F32), axis=0)


def high_bits():
    return list(range(1, lax.axis_size("wide").bit_length() - 1))


def mirror_first(value):
    return {0: value} | {1 << bit: flip(value, bit) for bit in high_bits()}


def mirror_rest(known):
    bits = high_bits()
    width = known[0].shape[1]
    middle = width // (2 * PAIR) * PAIR
    came = {}
    for order, low, high in ((bits, 0, middle), (bits[::-1], middle, width)):
        have = {0: known[0][:, low:high]}
        for bit in order:
            have |= {
                mask ^ (1 << bit): known[1 << bit][:, low:high] if mask == 0 else flip(part, bit)
                for mask, part in have.items()
            }
        came |= {(mask, low): part for mask, part in have.items() if mask not in known}
    return came


def half_rest(known, turned):
    order = high_bits()[::-1] if turned else high_bits()
    have = {0: known[0]}
    for bit in order:
        have |= {
            mask ^ (1 << bit): known[1 << bit] if mask == 0 else flip(part, bit)
            for mask, part in have.items()
        }
    return {mask: part for mask, part in have.items() if mask not in known}


def half_join(*halves):
    pieces, first = [], 0
    for known, came in halves:
        pieces += [(value, mask >> 1, first) for mask, value in (known | came).items()]
        first += known[0].shape[1]
    (own,) = place(pieces, (first,))
    return own, flip(own, 0)


def mirror_join(known, came, widths):
    pieces = [(value, mask >> 1, 0) for mask, value in known.items()]
    pieces += [(value, mask >> 1, low) for (mask, low), value in came.items()]
    return place(pieces, widths)


def turned_gains(own, other, first):
    def kernel(own_ref, other_ref, out_ref):
        half = own_ref.shape[0]
        for number, source in enumerate((own_ref, other_ref)):
            out_ref[:, number * half : (number + 1) * half] = source[...].astype(F32).T[:8]

    part = pl.BlockSpec((own.shape[0], PAIR), lambda i: (0, first // PAIR))
    return pl.pallas_call(
        kernel,
        grid=(1,),
        in_specs=[part, part],
        out_specs=pl.BlockSpec((8, 2 * own.shape[0]), lambda i: (0, 0)),
        out_shape=jax.ShapeDtypeStruct((8, 2 * own.shape[0]), F32),
    )(far(own), far(other))


def column_block(width):
    return max(b for b in range(PAIR, 1537, PAIR) if width % b == 0)


class Unit:
    def __init__(self, left, right, plane, first, width):
        self.left, self.right, self.plane, self.first, self.width = left, right, plane, first, width


def by_step(starts, values, step):
    found = values[0]
    for start, value in zip(starts[1:], values[1:]):
        found = jnp.where(step >= start, value, found)
    return found


def grad_product(lanes, rows, away, came, joint):
    units = [unit for lane in lanes for unit in lane]
    lane_of = [number for number, lane in enumerate(lanes) for _ in lane]
    tokens, features = units[0].left.shape
    count = lax.axis_size("wide")
    cut, tall = features // count, len(rows[0])
    block = min(column_block(unit.width) for unit in units)
    counts = [unit.width // block for unit in units]
    starts = [sum(counts[:number]) for number in range(len(units))]
    lane_starts = [starts[lane_of.index(number)] for number in range(len(lanes))]
    lane_counts = [sum(unit.width for unit in lane) // block for lane in lanes]
    lefts = list({id(unit.left): unit.left for unit in units}.values())
    left_of = [[left is unit.left for left in lefts].index(True) for unit in units]

    def unit_spec(number, unit):
        return pl.BlockSpec(
            (1, tokens, block),
            lambda i: (
                unit.plane,
                0,
                jnp.clip(i - starts[number], 0, counts[number] - 1) + unit.first // block,
            ),
        )

    def away_spec(place):
        return pl.BlockSpec(
            (cut, block), lambda i: (by_step(lane_starts, [row[place] for row in rows], i), i)
        )

    def lane_spec(number, height, row):
        return pl.BlockSpec(
            (height, block),
            lambda i: (row, jnp.clip(i - lane_starts[number], 0, lane_counts[number] - 1)),
        )

    in_specs = [pl.BlockSpec(left.shape, lambda i: (0, 0)) for left in lefts]
    in_specs += [unit_spec(number, unit) for number, unit in enumerate(units)]
    args = lefts + [unit.right for unit in units]
    if away is not None:
        in_specs += [away_spec(place) for place in range(tall)]
        args += [away] * tall
    at = {}
    for number, pairs in enumerate(came):
        for place in range(tall):
            at[number, place] = []
            for array, row_blocks in pairs:
                at[number, place].append(len(args))
                in_specs.append(lane_spec(number, cut, row_blocks[place]))
                args.append(array)
    widths = [sum(unit.width for unit in lane) for lane in lanes]
    if joint:
        out_specs = [pl.BlockSpec((tall * cut, block), lambda i: (0, i))]
        out_shape = [pltpu.HBM((tall * cut, sum(widths)), BF16)]
    else:
        out_specs = [lane_spec(number, tall * cut, 0) for number in range(len(lanes))]
        out_shape = [pltpu.HBM((tall * cut, width), BF16) for width in widths]

    def kernel(*refs):
        outs, turned = refs[len(args) : -1], refs[-1]
        step = pl.program_id(0)
        for number, unit in enumerate(units):
            lane = lane_of[number]

            @pl.when(step == starts[number])
            def _():
                for place, row in enumerate(rows[lane]):
                    source = refs[left_of[number]][:, row * cut : (row + 1) * cut]
                    turned[place * cut : (place + 1) * cut, :] = source.T

            @pl.when((step >= starts[number]) & (step < starts[number] + counts[number]))
            def _():
                product = dot(turned[...], refs[len(lefts) + number][0], (1, 0))
                out = outs[0] if joint else outs[lane]
                for place in range(tall):
                    part = product[place * cut : (place + 1) * cut]
                    if away is not None:
                        part += refs[len(lefts) + len(units) + place][...].astype(F32)
                    for spot in at.get((lane, place), ()):
                        part += refs[spot][...].astype(F32)
                    out[place * cut : (place + 1) * cut, :] = part.astype(BF16)

    return pl.pallas_call(
        kernel,
        grid=(sum(counts),),
        in_specs=in_specs,
        out_specs=out_specs,
        out_shape=out_shape,
        scratch_shapes=[pltpu.VMEM((tall * cut, tokens), BF16)],
        compiler_params=vmem(
            *[((2, tokens, features), BF16)] * len(lefts),
            *[((2, tokens, block), BF16)] * len(units),
            *[((2, tall * cut, block), BF16)] * (2 + len(out_shape)),
            *[((2, cut, block), BF16)] * sum(len(pairs) * tall for pairs in came),
            ((tall * cut, block), F32),
        ),
        cost_estimate=pl.CostEstimate(
            flops=2 * tall * cut * sum(widths) * tokens,
            bytes_accessed=4 * tall * cut * sum(widths),
            transcendentals=0,
        ),
    )(*[far(value) for value in args])


class Sum:
    def __init__(self, *lanes):
        bits = high_bits()
        sides = 1 << len(bits)
        self.lanes = lanes
        self.orders = [bits if number % 2 else bits[::-1] for number in range(len(lanes))]
        self.came = [[] for _ in lanes]
        self.keep = []
        for order in self.orders:
            held, lists = list(range(sides)), []
            for bit in order:
                lists.append([mask for mask in held if mask << 1 >> bit & 1])
                held = [mask for mask in held if not mask << 1 >> bit & 1]
                lists.append(held)
            self.keep.append(lists)
        rows = [[sides + mask for mask in range(sides)]] * len(lanes)
        self.state = grad_product(lanes, rows, None, [[] for _ in lanes], True)

    def over_core(self):
        self.away = flip(self.state[0], 0)
        self.state = [self.away]
        return self

    def parts(self, which, level):
        last = level == len(self.orders[0])
        lanes, rows, came, starts = [], [], [], []
        for number in which:
            lists = self.keep[number]
            row = lists[2 * level - 1] if last else lists[2 * level]
            lanes.append(self.lanes[number])
            rows.append(row)
            came.append(
                [
                    (array, [lists[2 * step + 1].index(mask) for mask in row])
                    for step, array in enumerate(self.came[number])
                ]
            )
        return grad_product(lanes, rows, self.column_part(which), came, last)

    def column_part(self, which):
        widths = [sum(unit.width for unit in lane) for lane in self.lanes]
        first = sum(widths[: which[0]])
        wide = sum(widths[number] for number in which)
        if wide == sum(widths):
            return self.away
        return self.away[:, first : first + wide]

    def which(self, which):
        return list(which) or list(range(len(self.lanes)))

    def add_own(self, *which):
        which = self.which(which)
        self.ready = dict(zip(which, self.parts(which, 0)))
        self.state = [self.away, self.ready]
        return self

    def sync_from(self, state):
        self.state = state
        self.away = state[0]
        if len(state) > 1:
            self.ready = state[1]
        if len(state) > 2:
            self.came = state[2]

    def over_first(self, *which):
        for number in self.which(which):
            self.came[number] = [flip(self.ready[number], self.orders[number][0])]
        self.state = [self.away, self.ready, self.came]
        return self

    def over_rest(self, *which):
        which = self.which(which)
        for level in range(1, len(self.orders[0])):
            parts = self.parts(which, level)
            for number, part in zip(which, parts):
                self.came[number] = self.came[number] + [flip(part, self.orders[number][level])]
        self.state = [self.away, self.ready, self.came]
        return self

    def whole(self):
        return self.parts(self.which(()), len(self.orders[0]))[0]


def chain_sum(value):
    return lax.psum_scatter(value, "narrow", scatter_dimension=0, tiled=True)


def hold(sums, *values):
    flat, tree = jax.tree.flatten(([one.state for one in sums], values))
    states, values = jax.tree.unflatten(tree, lax.optimization_barrier(flat))
    for one, state in zip(sums, states):
        one.sync_from(state)
    return values


def block_order():
    count = lax.axis_size("wide")
    here = lax.axis_index("wide")
    masks = [mask << 1 for mask in range(count // 2)]
    return [here ^ mask for mask in masks + [mask + 1 for mask in masks]]


def blocks_kernel(count, spot_ref, *refs):
    for source, target in zip(refs[: len(refs) // 2], refs[len(refs) // 2 :]):
        width = source.shape[1] // count
        for number in range(count):
            spot = pl.multiple_of(spot_ref[number] * width, PAIR)
            target[:, number * width : (number + 1) * width] = source[:, pl.ds(spot, width)]


def blocks(values, spots):
    count = len(spots)
    whole = pl.BlockSpec(memory_space=pltpu.VMEM)
    return pl.pallas_call(
        lambda *refs: blocks_kernel(count, *refs),
        in_specs=[pl.BlockSpec(memory_space=pltpu.SMEM)] + [whole] * len(values),
        out_specs=[whole] * len(values),
        out_shape=[jax.ShapeDtypeStruct(value.shape, value.dtype) for value in values],
        compiler_params=pltpu.CompilerParams(vmem_limit_bytes=2 * LIMIT),
        cost_estimate=pl.CostEstimate(flops=0, bytes_accessed=2**22, transcendentals=0),
    )(jnp.stack(spots).astype(jnp.int32), *values)


def to_own(*values):
    return blocks(values, block_order())


def from_own(*values):
    count = lax.axis_size("wide")
    here = lax.axis_index("wide")
    places = [((j ^ here) >> 1) + ((j ^ here) & 1) * (count // 2) for j in range(count)]
    return blocks(values, places)


def all_sum_chain(value):
    return [value] + [shift(value, step) for step in range(1, lax.axis_size("narrow"))]


def all_sum_cube(value):
    count = lax.axis_size("wide")

    def over(mask):
        return lax.ppermute(value, "wide", [(i, i ^ mask) for i in range(count)])

    return [value] + [over(mask << 1) for mask in range(1, count // 2)]


def shard_place():
    return lax.axis_index("wide") * lax.axis_size("narrow") + lax.axis_index("narrow")


def matmul_block(width, first):
    fits = [b for b in range(PAIR, 1537, PAIR) if width % b == 0 and first % b == 0]
    return max(fits)


def into(value, weight, first, width, kind):
    tokens, features = value.shape
    half = features // 2
    block = matmul_block(width, first)
    if block == width:
        block //= 2

    def kernel(value_ref, own_ref, other_ref, out_ref):
        product = dot(value_ref[:, :half], own_ref[...], (1, 0))
        product += dot(value_ref[:, half:], other_ref[...], (1, 0))
        out_ref[...] = product.astype(kind)

    part = pl.BlockSpec((half, block), lambda i: (0, i + first // block))
    return pl.pallas_call(
        kernel,
        grid=(width // block,),
        in_specs=[pl.BlockSpec(value.shape, lambda i: (0, 0)), part, part],
        out_specs=pl.BlockSpec((tokens, block), lambda i: (0, i)),
        out_shape=jax.ShapeDtypeStruct((tokens, width), kind),
        compiler_params=vmem(
            (value.shape, F32), ((4, half, block), BF16), ((4, tokens, block), F32)
        ),
        cost_estimate=pl.CostEstimate(
            flops=2 * tokens * features * width,
            bytes_accessed=2 * features * width,
            transcendentals=0,
        ),
    )(value, *[far(part) for part in weight])


def out_of(value, weight, first):
    planes, tokens, width = value.shape
    half = weight[0].shape[0]
    block = matmul_block(width, first)
    if block == width and planes == 1:
        block //= 2
    steps = width // block

    def kernel(value_ref, own_ref, other_ref, out_ref):
        own = dot(value_ref[0], own_ref[...], (1, 1))
        other = dot(value_ref[0], other_ref[...], (1, 1))

        @pl.when(pl.program_id(0) == 0)
        def _():
            out_ref[:, :half] = own
            out_ref[:, half:] = other

        @pl.when(pl.program_id(0) > 0)
        def _():
            out_ref[:, :half] += own
            out_ref[:, half:] += other

    part = pl.BlockSpec((half, block), lambda i: (0, i + first // block))
    return pl.pallas_call(
        kernel,
        grid=(planes * steps,),
        in_specs=[
            pl.BlockSpec((1, tokens, block), lambda i: (i // steps, 0, i % steps)),
            part,
            part,
        ],
        out_specs=pl.BlockSpec((tokens, 2 * half), lambda i: (0, 0)),
        out_shape=jax.ShapeDtypeStruct((tokens, 2 * half), F32),
        compiler_params=vmem(
            ((2, tokens, block), BF16), ((4, half, block), BF16), ((4, tokens, 2 * half), F32)
        ),
        cost_estimate=pl.CostEstimate(
            flops=4 * tokens * half * width * planes,
            bytes_accessed=4 * half * width * planes,
            transcendentals=0,
        ),
    )(value, *[far(part) for part in weight])


def feed_forward(value, weight, width):
    tokens, features = value.shape
    half = features // 2
    block = matmul_block(width, width)

    def kernel(value_ref, own_gate, other_gate, own_up, other_up, gate_ref, up_ref, act_ref):
        own, other = value_ref[:, :half], value_ref[:, half:]
        gate = dot(own, own_gate[...], (1, 0)) + dot(other, other_gate[...], (1, 0))
        up = dot(own, own_up[...], (1, 0)) + dot(other, other_up[...], (1, 0))
        gate_ref[...] = gate
        up_ref[...] = up
        act_ref[...] = gated(gate, up).astype(BF16)

    gate_part = pl.BlockSpec((half, block), lambda i: (0, i))
    up_part = pl.BlockSpec((half, block), lambda i: (0, i + width // block))
    out = pl.BlockSpec((tokens, block), lambda i: (0, i))
    return pl.pallas_call(
        kernel,
        grid=(width // block,),
        in_specs=[pl.BlockSpec(value.shape, lambda i: (0, 0))]
        + [gate_part, gate_part, up_part, up_part],
        out_specs=[out] * 3,
        out_shape=[jax.ShapeDtypeStruct((tokens, width), kind) for kind in (F32, F32, BF16)],
        compiler_params=vmem(((8, half, block), BF16), ((9, tokens, block), F32)),
        cost_estimate=pl.CostEstimate(
            flops=4 * tokens * features * width,
            bytes_accessed=4 * features * width,
            transcendentals=0,
        ),
    )(value, *[far(part) for part in (*weight, *weight)])


def feed_back(value, weight, gate, up):
    tokens, features = value.shape
    half = features // 2
    width = gate.shape[1]
    block = matmul_block(width, 0)

    def kernel(value_ref, own_ref, other_ref, gate_ref, up_ref, out_ref):
        grad = dot(value_ref[:, :half], own_ref[...], (1, 0))
        grad += dot(value_ref[:, half:], other_ref[...], (1, 0))
        dgate, dup = jax.vjp(gated, gate_ref[...], up_ref[...])[1](grad)
        out_ref[0] = dgate.astype(BF16)
        out_ref[1] = dup.astype(BF16)

    part = pl.BlockSpec((half, block), lambda i: (0, i))
    wide = pl.BlockSpec((tokens, block), lambda i: (0, i))
    return pl.pallas_call(
        kernel,
        grid=(width // block,),
        in_specs=[pl.BlockSpec(value.shape, lambda i: (0, 0)), part, part, wide, wide],
        out_specs=pl.BlockSpec((2, tokens, block), lambda i: (0, 0, i)),
        out_shape=jax.ShapeDtypeStruct((2, tokens, width), BF16),
        compiler_params=vmem(((4, half, block), BF16), ((9, tokens, block), F32)),
        cost_estimate=pl.CostEstimate(
            flops=2 * tokens * features * width,
            bytes_accessed=4 * features * width,
            transcendentals=0,
        ),
    )(value, *[far(part) for part in weight], gate, up)


def rms_norm(hidden, gain):
    return hidden * lax.rsqrt(jnp.mean(hidden * hidden, axis=-1, keepdims=True) + EPS) * gain


def gated(gate, up):
    return jax.nn.gelu(gate) * up


def advance(master, moment, trail, grad, rate):
    new_moment = 0.5 * moment + 0.5 * grad
    new_master = master - rate * (grad + 0.5 * new_moment)
    new_trail = 0.5 * trail + 0.5 * new_master
    return (new_master, new_moment, new_trail, new_master.astype(BF16))


def on_device(
    tokens,
    memory,
    dec_ids,
    enc_ids,
    cotangent,
    query_weight,
    query_moment,
    query_trail,
    keyval_weight,
    keyval_moment,
    keyval_trail,
    output_weight,
    output_moment,
    output_trail,
    inner_weight,
    inner_moment,
    inner_trail,
    outer_weight,
    outer_moment,
    outer_trail,
    norm_gains,
    gains_moment,
    gains_trail,
):
    rows, local_len, width = tokens.shape
    mem_local = memory.shape[1]
    narrow_count = lax.axis_size("narrow")
    seq_len = local_len * narrow_count
    inner_width = outer_weight.shape[0]
    q_width, kv_width = query_weight.shape[2], keyval_weight.shape[2]
    gain_count, gain_width = norm_gains.shape
    q_share, kv_share = q_width // narrow_count, kv_width // (2 * narrow_count)

    gain_cols = jnp.pad(norm_gains.astype(BF16).T, ((0, 0), (0, PAIR - gain_count)))
    shard0 = jnp.concatenate(
        [query_weight[0].astype(BF16), keyval_weight[0].astype(BF16), gain_cols], axis=1
    )
    z0 = spread_steps(shard0, near_steps() + far_steps())
    shard1 = jnp.concatenate(
        [
            output_weight[0].T.astype(BF16),
            query_weight[1].astype(BF16),
            keyval_weight[1].astype(BF16),
            output_weight[1].T.astype(BF16),
        ],
        axis=1,
    )
    tokens_own, memory_own, grad_ffn = to_own(
        tokens.reshape(local_len, width),
        memory.reshape(mem_local, width),
        cotangent.reshape(local_len, width),
    )
    z0, shard1, tokens_own, memory_own, grad_ffn = sync(
        z0, shard1, tokens_own, memory_own, grad_ffn
    )
    dec_col, dec_row = dec_ids.reshape(-1, 1), dec_ids.reshape(1, -1)
    enc_col = enc_ids.reshape(-1, 1)
    g0 = mirror_first(*spread_join(shard0, z0))
    z1 = spread_steps(shard1, near_steps())
    shard2 = inner_weight.astype(BF16)
    shard3 = outer_weight.T.astype(BF16)
    hidden = tokens_own.astype(F32)
    g0, z1, shard1, shard2, shard3 = sync(g0, z1, shard1, shard2, shard3)
    r0 = mirror_rest(g0)
    z1 |= spread_steps(shard1, far_steps())
    r0, z1 = sync(r0, z1)
    (own,) = mirror_join(g0, r0, (q_width + kv_width + PAIR,))
    w_zero = (own, flip(own, 0))
    a1, b1 = spread_join(shard1, z1, width + q_width, kv_width + width)
    a1 = mirror_first(a1)
    z2 = spread_steps(shard2, near_steps())
    w_zero, b1 = sync(w_zero, b1)
    gains = turned_gains(*w_zero, q_width + kv_width)
    normed_one = rms_norm(hidden, gains[0]).astype(BF16)
    query_one = into(normed_one, w_zero, 0, q_width, BF16)
    keyval_one = into(normed_one, w_zero, q_width, kv_width, BF16)
    pieces = cut_columns([query_one, keyval_one[:, : kv_width // 2], keyval_one[:, kv_width // 2 :]])
    pieces, a1, b1, shard2, z2 = sync(pieces, a1, b1, shard2, z2)
    joint_one = trade(pieces)
    b1 = mirror_first(b1)
    joint_one, b1, shard2 = sync(joint_one, b1, shard2)
    ra1, rb1 = half_rest(a1, False), half_rest(b1, True)
    z2 |= spread_steps(shard2, far_steps())
    context, stat_one = attention(joint_one, dec_col, dec_row, local_len, True)
    context, ra1, rb1, z2 = sync(context, ra1, rb1, z2)
    came = trade(context)
    w_one = half_join((a1, ra1), (b1, rb1))
    a2, b2 = spread_join(shard2, z2, inner_width, inner_width)
    a2 = mirror_first(a2)
    came, w_one, shard3, b2 = sync(came, w_one, shard3, b2)
    kv_at, o_two_at = width + q_width, width + q_width + kv_width
    z3 = spread_steps(shard3, near_steps() + far_steps())
    context_one = join_columns(came, q_share)
    after_one = hidden + out_of(context_one[None], w_one, 0)
    normed_two = rms_norm(after_one, gains[1]).astype(BF16)
    query_two = into(normed_two, w_one, width, q_width, BF16)
    keyval_two = into(memory_own, w_one, kv_at, kv_width, BF16)
    pieces = cut_columns([query_two, keyval_two[:, : kv_width // 2], keyval_two[:, kv_width // 2 :]])
    a2, z3, pieces, after_one, b2, shard3 = sync(a2, z3, pieces, after_one, b2, shard3)
    joint_two = trade(pieces)
    b2 = mirror_first(b2)
    half_inner = inner_width // 2
    a3, b3 = spread_join(shard3, z3, half_inner, half_inner)
    joint_two, b2, a3, b3 = sync(joint_two, b2, a3, b3)
    ra2, rb2 = half_rest(a2, False), half_rest(b2, True)
    context, stat_two = attention(joint_two, enc_col, dec_row, local_len, False)
    context, ra2, rb2, a3, b3 = sync(context, ra2, rb2, a3, b3)
    came = trade(context)
    a3 = mirror_first(a3)
    w_in = half_join((a2, ra2), (b2, rb2))
    came, w_in, a3, b3 = sync(came, w_in, a3, b3)
    b3 = mirror_first(b3)
    context_two = join_columns(came, q_share)
    after_two = after_one + out_of(context_two[None], w_one, o_two_at)
    normed_three = rms_norm(after_two, gains[2]).astype(BF16)
    b3, normed_three, after_two = sync(b3, normed_three, after_two)
    ra3, rb3 = half_rest(a3, False), half_rest(b3, True)
    gate, up, activated = feed_forward(normed_three, w_in, inner_width)
    ra3, rb3, gate, up, activated = sync(ra3, rb3, gate, up, activated)
    w_out = half_join((a3, ra3), (b3, rb3))
    sum_outs = Sum(
        [Unit(grad_ffn, activated[None], 0, 0, half_inner)],
        [Unit(grad_ffn, activated[None], 0, half_inner, half_inner)],
    )
    w_out, activated = hold([sum_outs], w_out, activated)
    sum_outs.over_core()
    grad_inner = feed_back(grad_ffn, w_out, gate, up)
    (grad_inner,) = hold([sum_outs], grad_inner)
    sum_outs.add_own()
    sum_ins = Sum(
        [Unit(normed_three, grad_inner, 0, 0, half_inner)],
        [Unit(normed_three, grad_inner, 0, half_inner, half_inner)],
        [Unit(normed_three, grad_inner, 1, 0, half_inner)],
        [Unit(normed_three, grad_inner, 1, half_inner, half_inner)],
    )
    (grad_inner,) = hold([sum_outs, sum_ins], grad_inner)
    sum_outs.over_first()
    sum_ins.over_core()
    grad_normed = out_of(grad_inner, w_in, 0)
    grad_hidden, grad_gain_three = jax.vjp(rms_norm, after_two, gains[2])[1](grad_normed)
    grad_two = grad_ffn.astype(F32) + grad_hidden
    grad_branch = grad_two.astype(BF16)
    pieces = cut_columns([into(grad_branch, w_one, o_two_at, width, BF16)])
    pieces, grad_branch_two = hold([sum_ins, sum_outs], pieces, grad_branch)
    grad_context = trade(pieces)
    sum_outs.over_rest()
    sum_ins.add_own()
    outer_whole = sum_outs.whole()
    grad_context, outer_whole = hold([sum_ins], grad_context, outer_whole)
    sum_ins.over_first(0, 1)
    outer_parts = chain_sum(outer_whole)
    dquery, dkeyval = attention_back(
        joint_two, grad_context, stat_two, enc_col, dec_row, local_len, False
    )
    dquery, dkeyval, activated = hold([sum_ins], dquery, dkeyval, activated)
    came = trade(dquery)
    sum_ins.over_first(2, 3)
    result = after_two + out_of(activated[None], w_out, 0)
    (block_out,) = from_own(result.astype(BF16))
    came, dkeyval, block_out = hold([sum_ins], came, dkeyval, block_out)
    came_too = trade(dkeyval)
    sum_ins.over_rest()
    query_grad_two = join_columns(came, q_share)
    grad_normed_two = out_of(query_grad_two[None], w_one, width)
    grad_hidden, grad_gain_two = jax.vjp(rms_norm, after_one, gains[1])[1](grad_normed_two)
    grad_one = grad_two + grad_hidden
    grad_branch = grad_one.astype(BF16)
    pieces = cut_columns([into(grad_branch, w_one, 0, width, BF16)])
    pieces, grad_branch, came_too = hold([sum_ins], pieces, grad_branch, came_too)
    grad_context = trade(pieces)
    inner_whole = sum_ins.whole()
    keyval_grad_two = join_columns(came_too, kv_share, 2)
    sum_mid = Sum(
        [
            Unit(grad_branch_two, context_two[None], 0, 0, width),
            Unit(memory_own, keyval_grad_two[None], 0, 0, kv_width),
        ],
        [
            Unit(normed_two, query_grad_two[None], 0, 0, q_width),
            Unit(grad_branch, context_one[None], 0, 0, width),
        ],
    )
    grad_context, keyval_grad_two, inner_whole = hold(
        [sum_mid], grad_context, keyval_grad_two, inner_whole
    )
    sum_mid.over_core()
    inner_parts = chain_sum(inner_whole)
    dquery, dkeyval = attention_back(
        joint_one, grad_context, stat_one, dec_col, dec_row, local_len, True
    )
    dquery, dkeyval, keyval_grad_two = hold([sum_mid], dquery, dkeyval, keyval_grad_two)
    sum_mid.add_own()
    (dquery,) = hold([sum_mid], dquery)
    came = trade(dquery)
    sum_mid.over_first()
    (memory_grad,) = from_own(out_of(keyval_grad_two[None], w_one, kv_at))
    sum_outer = outer_parts.astype(F32).T
    came, sum_outer, memory_grad, dkeyval = hold(
        [sum_mid], came, sum_outer, memory_grad, dkeyval
    )
    came_too = trade(dkeyval)
    sum_mid.over_rest()
    query_grad_one = join_columns(came, q_share)
    grad_normed_one = out_of(query_grad_one[None], w_zero, 0)
    came_too, grad_normed_one = hold([sum_mid], came_too, grad_normed_one)
    keyval_grad_one = join_columns(came_too, kv_share, 2)
    sum_last = Sum(
        [Unit(normed_one, query_grad_one[None], 0, 0, q_width)],
        [Unit(normed_one, keyval_grad_one[None], 0, 0, kv_width)],
    )
    mid_whole = sum_mid.whole()
    keyval_grad_one, mid_whole = hold([sum_last], keyval_grad_one, mid_whole)
    sum_last.over_core()
    mid_parts = trade(mid_whole)
    grad_normed_one += out_of(keyval_grad_one[None], w_zero, q_width)
    grad_hidden, grad_gain_one = jax.vjp(rms_norm, hidden, gains[0])[1](grad_normed_one)
    input_grad, full_gains = from_own(
        grad_one + grad_hidden,
    ) + from_own(jnp.stack([grad_gain_one, grad_gain_two, grad_gain_three]))
    input_grad, full_gains, inner_parts = hold([sum_last], input_grad, full_gains, inner_parts)
    sum_last.add_own()
    full_gains, inner_parts = hold([sum_last], full_gains, inner_parts)
    sum_last.over_first()
    gain_parts = all_sum_cube(full_gains)
    sum_inner = inner_parts.astype(F32)
    gain_parts, sum_inner = hold([sum_last], gain_parts, sum_inner)
    sum_last.over_rest()
    part = sum(gain_parts)
    gain_parts = [part, flip(part, 0)]
    gain_parts, mid_parts = hold([sum_last], gain_parts, mid_parts)
    sum_two = total(mid_parts)
    last_parts = trade(sum_last.whole())
    full_gains = sum(all_sum_chain(sum(gain_parts)))
    sum_gains = lax.dynamic_slice_in_dim(full_gains, shard_place() * gain_width, gain_width, 1)
    sum_one = total(last_parts)
    after_kv, after_q = width + kv_width, width + kv_width + q_width
    sum_query = jnp.stack([sum_one[:, :q_width], sum_two[:, after_kv:after_q]])
    sum_keyval = jnp.stack([sum_one[:, q_width:], sum_two[:, width:after_kv]])
    sum_output = jnp.stack([sum_two[:, after_q:], sum_two[:, :width]]).transpose(0, 2, 1)
    block_out = block_out.reshape(rows, local_len, width)
    input_grad = input_grad.reshape(rows, local_len, width)
    memory_grad = memory_grad.reshape(rows, mem_local, width)
    token_total = rows * lax.axis_size("wide") * seq_len
    rate = RATE / math.sqrt(token_total)
    output_rate = OUTPUT_RATE / math.sqrt(token_total)
    new_query = advance(query_weight, query_moment, query_trail, sum_query, rate)
    new_keyval = advance(keyval_weight, keyval_moment, keyval_trail, sum_keyval, rate)
    new_output = advance(output_weight, output_moment, output_trail, sum_output, output_rate)
    new_inner = advance(inner_weight, inner_moment, inner_trail, sum_inner, rate)
    new_outer = advance(outer_weight, outer_moment, outer_trail, sum_outer, rate)
    new_gains = advance(norm_gains, gains_moment, gains_trail, sum_gains, rate)
    return (
        block_out,
        input_grad,
        memory_grad,
        new_query[0],
        new_query[1],
        new_query[2],
        new_query[3],
        new_keyval[0],
        new_keyval[1],
        new_keyval[2],
        new_keyval[3],
        new_output[0],
        new_output[1],
        new_output[2],
        new_output[3],
        new_inner[0],
        new_inner[1],
        new_inner[2],
        new_inner[3],
        new_outer[0],
        new_outer[1],
        new_outer[2],
        new_outer[3],
        new_gains[0],
        new_gains[1],
        new_gains[2],
        new_gains[3],
    )


def solution(mesh):
    in_specs = (
        P("wide", "narrow", None),
        P("wide", "narrow", None),
        P("wide", None),
        P("wide", None),
        P("wide", "narrow", None),
        P(None, ("wide", "narrow"), None),
        P(None, ("wide", "narrow"), None),
        P(None, ("wide", "narrow"), None),
        P(None, ("wide", "narrow"), None),
        P(None, ("wide", "narrow"), None),
        P(None, ("wide", "narrow"), None),
        P(None, None, ("wide", "narrow")),
        P(None, None, ("wide", "narrow")),
        P(None, None, ("wide", "narrow")),
        P(("wide", "narrow"), None),
        P(("wide", "narrow"), None),
        P(("wide", "narrow"), None),
        P(None, ("wide", "narrow")),
        P(None, ("wide", "narrow")),
        P(None, ("wide", "narrow")),
        P(None, ("wide", "narrow")),
        P(None, ("wide", "narrow")),
        P(None, ("wide", "narrow")),
    )
    out_specs = (
        P("wide", "narrow", None),
        P("wide", "narrow", None),
        P("wide", "narrow", None),
        P(None, ("wide", "narrow"), None),
        P(None, ("wide", "narrow"), None),
        P(None, ("wide", "narrow"), None),
        P(None, ("wide", "narrow"), None),
        P(None, ("wide", "narrow"), None),
        P(None, ("wide", "narrow"), None),
        P(None, ("wide", "narrow"), None),
        P(None, ("wide", "narrow"), None),
        P(None, None, ("wide", "narrow")),
        P(None, None, ("wide", "narrow")),
        P(None, None, ("wide", "narrow")),
        P(None, None, ("wide", "narrow")),
        P(("wide", "narrow"), None),
        P(("wide", "narrow"), None),
        P(("wide", "narrow"), None),
        P(("wide", "narrow"), None),
        P(None, ("wide", "narrow")),
        P(None, ("wide", "narrow")),
        P(None, ("wide", "narrow")),
        P(None, ("wide", "narrow")),
        P(None, ("wide", "narrow")),
        P(None, ("wide", "narrow")),
        P(None, ("wide", "narrow")),
        P(None, ("wide", "narrow")),
    )
    return jax.shard_map(
        on_device, mesh=mesh, in_specs=in_specs, out_specs=out_specs, check_vma=False
    )
```

```python
import math

import jax
import jax.numpy as jnp
from jax import lax
from jax.experimental import pallas as pl
from jax.experimental.pallas import tpu as pltpu
from jax.sharding import PartitionSpec as P

HDIM = 64
PAIR = 2 * HDIM
EPS = 1e-06
NEG = -1e30
RATE = 0.02
OUTPUT_RATE = 0.15
LIMIT = 16 * 2**20
BF16 = jnp.bfloat16
F32 = jnp.float32


def dot(left, right, sides):
    return lax.dot_general(
        left, right, (((sides[0],), (sides[1],)), ((), ())), preferred_element_type=F32
    )


def matmul(left, right):
    return dot(left, right, (1, 0))


def matmul_right(left, right):
    return dot(left, right, (1, 1))


def matmul_left(left, right):
    return dot(left, right, (0, 0))


def in_group(block, group):
    low = lax.broadcasted_iota(jnp.int32, block.shape, 1) < HDIM
    turned = jnp.concatenate([block[:, HDIM:], block[:, :HDIM]], axis=1)
    zero = jnp.zeros_like(block)
    if group == 0:
        return jnp.where(low, block, zero), jnp.where(low, turned, zero)
    return jnp.where(low, zero, turned), jnp.where(low, zero, block)


def allowed(kid_ref, qid_ref, bias_ref, span, order):
    keep = kid_ref[:span] == qid_ref[...]
    if order:
        count = qid_ref.shape[1]
        keys = lax.broadcasted_iota(jnp.int32, keep.shape, 0)
        queries = lax.broadcasted_iota(jnp.int32, keep.shape, 1) + pl.program_id(0) * count
        keep &= keys <= queries
    bias_ref[:span] = jnp.where(keep, 0.0, NEG).astype(F32)


def by_span(order, count, full, body):
    if not order:
        body(full)
        return
    for number in range(full // count):
        pl.when(pl.program_id(0) == number)(lambda number=number: body((number + 1) * count))


def forward_kernel(order, query_ref, key_ref, value_ref, kid_ref, qid_ref, *rest):
    out_ref, stat_ref, bias_ref = rest
    count, width = query_ref.shape

    def body(span):
        allowed(kid_ref, qid_ref, bias_ref, span, order)
        keys = key_ref[:span]
        values = value_ref[:span].T
        for group in range(width // PAIR):
            columns = slice(group * PAIR, (group + 1) * PAIR)
            rows = slice(group * HDIM, (group + 1) * HDIM)
            block = query_ref[:, columns] * jnp.asarray(HDIM**-0.5, BF16)
            parts = []
            for side, query in enumerate(in_group(block, group)):
                logits = dot(keys, query, (1, 1)) + bias_ref[:span]
                peak = jnp.max(logits, axis=0, keepdims=True)
                weights = jnp.exp(logits - peak)
                total = jnp.sum(weights, axis=0, keepdims=True)
                probs = (weights * (1.0 / total)).astype(BF16)
                parts.append(dot(values, probs, (1, 0))[rows])
                stat_ref[0, pl.ds(2 * group + side, 1), :] = peak + jnp.log(total)
            out_ref[:, columns] = jnp.concatenate(parts, axis=0).T.astype(BF16)

    by_span(order, count, key_ref.shape[0], body)


def backward_kernel(
    order, query_ref, key_ref, value_ref, kid_ref, qid_ref, grad_ref, stat_ref, *rest
):
    dquery_ref, dkeyval_ref, bias_ref, key_sum, value_sum = rest
    count, width = query_ref.shape

    @pl.when(pl.program_id(0) == 0)
    def _():
        key_sum[...] = jnp.zeros_like(key_sum)
        value_sum[...] = jnp.zeros_like(value_sum)

    def body(span):
        allowed(kid_ref, qid_ref, bias_ref, span, order)
        keys = key_ref[:span]
        values = value_ref[:span]
        keys_turned = keys.T
        dkey, dvalue = None, None
        for group in range(width // PAIR):
            columns = slice(group * PAIR, (group + 1) * PAIR)
            rows = slice(group * HDIM, (group + 1) * HDIM)
            queries = in_group(query_ref[:, columns] * jnp.asarray(HDIM**-0.5, BF16), group)
            grads = in_group(grad_ref[:, columns], group)
            parts = []
            for side in range(2):
                logits = dot(keys, queries[side], (1, 1)) + bias_ref[:span]
                probs = jnp.exp(logits - stat_ref[0, pl.ds(2 * group + side, 1), :])
                dprobs = dot(values, grads[side], (1, 1))
                dots = jnp.sum(probs * dprobs, axis=0, keepdims=True)
                dlogits = (probs * (dprobs - dots)).astype(BF16)
                parts.append(dot(keys_turned, dlogits, (1, 0))[rows])
                more_key = dot(dlogits, queries[side], (1, 0))
                more_value = dot(probs.astype(BF16), grads[side], (1, 0))
                dkey = more_key if dkey is None else dkey + more_key
                dvalue = more_value if dvalue is None else dvalue + more_value
            dquery_ref[:, columns] = (jnp.concatenate(parts, axis=0).T * HDIM**-0.5).astype(BF16)
        key_sum[:span] += dkey
        value_sum[:span] += dvalue

    by_span(order, count, key_ref.shape[0], body)

    @pl.when(pl.program_id(0) == pl.num_programs(0) - 1)
    def _():
        dkeyval_ref[:, :PAIR] = key_sum[...].astype(BF16)
        dkeyval_ref[:, PAIR:] = value_sum[...].astype(BF16)


def attention_specs(joint, count):
    span, width = joint.shape
    q_width = width - 2 * PAIR
    query = pl.BlockSpec((count, q_width), lambda i: (i, 0))
    keys = pl.BlockSpec((span, PAIR), lambda i: (0, q_width // PAIR))
    values = pl.BlockSpec((span, PAIR), lambda i: (0, q_width // PAIR + 1))
    key_ids = pl.BlockSpec((span, 1), lambda i: (0, 0))
    query_ids = pl.BlockSpec((1, count), lambda i: (0, i))
    stat = pl.BlockSpec((1, 8, count), lambda i: (i, 0, 0))
    return q_width, [query, keys, values, key_ids, query_ids], stat


def attention(joint, key_ids, query_ids, count, order):
    span = joint.shape[0]
    q_width, specs, s_spec = attention_specs(joint, count)
    return pl.pallas_call(
        lambda *refs: forward_kernel(order, *refs),
        grid=(span // count,),
        in_specs=specs,
        out_specs=[specs[0], s_spec],
        out_shape=[
            jax.ShapeDtypeStruct((span, q_width), BF16),
            jax.ShapeDtypeStruct((span // count, 8, count), F32),
        ],
        scratch_shapes=[pltpu.VMEM((span, count), F32)],
        compiler_params=pltpu.CompilerParams(vmem_limit_bytes=2 * LIMIT),
        cost_estimate=pl.CostEstimate(
            flops=4 * span * span * q_width, bytes_accessed=8 * span * q_width, transcendentals=0
        ),
    )(joint, joint, joint, key_ids, query_ids)


def attention_back(joint, grad, stat, key_ids, query_ids, count, order):
    span = joint.shape[0]
    q_width, specs, s_spec = attention_specs(joint, count)
    whole = pl.BlockSpec((span, 2 * PAIR), lambda i: (0, 0))
    return pl.pallas_call(
        lambda *refs: backward_kernel(order, *refs),
        grid=(span // count,),
        in_specs=specs + [specs[0], s_spec],
        out_specs=[specs[0], whole],
        out_shape=[
            jax.ShapeDtypeStruct((span, q_width), BF16),
            jax.ShapeDtypeStruct((span, 2 * PAIR), BF16),
        ],
        scratch_shapes=[
            pltpu.VMEM((span, count), F32),
            pltpu.VMEM((span, PAIR), F32),
            pltpu.VMEM((span, PAIR), F32),
        ],
        compiler_params=pltpu.CompilerParams(vmem_limit_bytes=2 * LIMIT),
        cost_estimate=pl.CostEstimate(
            flops=10 * span * span * q_width, bytes_accessed=16 * span * q_width, transcendentals=0
        ),
    )(joint, joint, joint, key_ids, query_ids, grad, stat)


def flip(value, bit):
    count = lax.axis_size("wide")
    return lax.ppermute(value, "wide", [(i, i ^ (1 << bit)) for i in range(count)])


def shift(value, step):
    count = lax.axis_size("narrow")
    return lax.ppermute(value, "narrow", [(i, (i + step) % count) for i in range(count)])


def sync(*values):
    return lax.optimization_barrier(values)


def place(pieces, widths):
    rows = pieces[0][0].shape[0]
    count = 1 + max(number for _, number, _ in pieces)

    def kernel(*refs):
        first = 0
        for target, cut in zip(refs[len(pieces) :], widths):
            for source, (piece, number, begin) in zip(refs, pieces):
                low, high = max(begin, first), min(begin + piece.shape[1], first + cut)
                if low < high:
                    target[number * rows : (number + 1) * rows, low - first : high - first] = source[
                        :, low - begin : high - begin
                    ]
            first += cut

    shapes = [jax.ShapeDtypeStruct((count * rows, cut), BF16) for cut in widths]
    return small_call(kernel, shapes, [piece for piece, _, _ in pieces])


def far(value):
    return pltpu.with_memory_space_constraint(value, pltpu.HBM)


def trade(value):
    return lax.all_to_all(value, "narrow", 0, 0, tiled=True)


def spread(value):
    count = lax.axis_size("narrow")
    return trade(jnp.concatenate([value] * count, axis=0))


def near_steps():
    return sorted({1, lax.axis_size("narrow") - 1})


def far_steps():
    return [s for s in range(1, lax.axis_size("narrow")) if s not in near_steps()]


def spread_steps(value, steps):
    return {step: shift(value, step) for step in steps}


def spread_join(value, came, *widths):
    count = lax.axis_size("narrow")
    pieces = [value] + [came[step] for step in sorted(came)]
    rows, width = value.shape
    widths = widths or (width,)
    firsts = [sum(widths[:number]) for number in range(len(widths))]
    spots = (lax.axis_index("narrow") - jnp.arange(count, dtype=jnp.int32)) % count
    if rows % 16:
        whole = jnp.zeros((count, rows, width), value.dtype)
        for number, piece in enumerate(pieces):
            whole = lax.dynamic_update_index_in_dim(whole, piece, spots[number], 0)
        whole = whole.reshape(count * rows, width)
        return [whole[:, first : first + wide] for first, wide in zip(firsts, widths)]

    def kernel(spot_ref, *refs):
        for number, source in enumerate(refs[:count]):
            spot = pl.multiple_of(spot_ref[number] * rows, rows)
            for target, first, wide in zip(refs[count:], firsts, widths):
                target[pl.ds(spot, rows), :] = source[:, first : first + wide]

    whole = pl.BlockSpec(memory_space=pltpu.VMEM)
    return pl.pallas_call(
        kernel,
        in_specs=[pl.BlockSpec(memory_space=pltpu.SMEM)] + [whole] * count,
        out_specs=[whole] * len(widths),
        out_shape=[jax.ShapeDtypeStruct((count * rows, wide), value.dtype) for wide in widths],
        compiler_params=pltpu.CompilerParams(vmem_limit_bytes=LIMIT),
        cost_estimate=pl.CostEstimate(flops=0, bytes_accessed=2**22, transcendentals=0),
    )(spots, *pieces)


def tight(width):
    return -(-width // PAIR) * PAIR


def cut_columns(parts):
    count = lax.axis_size("narrow")
    rows = parts[0].shape[0]
    shares = [part.shape[1] // count for part in parts]
    width = sum(tight(share) for share in shares)

    def kernel(*refs):
        target = refs[-1]
        for number in range(count):
            first = 0
            for source, share in zip(refs, shares):
                block = source[:, number * share : (number + 1) * share]
                if share % PAIR:
                    zeros = jnp.zeros((rows, tight(share) - share), BF16)
                    block = jnp.concatenate([block, zeros], axis=1)
                target[number * rows : (number + 1) * rows, first : first + tight(share)] = block
                first += tight(share)

    return small_call(kernel, [jax.ShapeDtypeStruct((count * rows, width), BF16)], parts)[0]


def join_columns(value, share, kinds=1):
    count = lax.axis_size("narrow")
    rows = value.shape[0] // count

    def kernel(source, target):
        for kind in range(kinds):
            for number in range(count):
                place = (kind * count + number) * share
                target[:, place : place + share] = source[
                    number * rows : (number + 1) * rows,
                    kind * tight(share) : kind * tight(share) + share,
                ]

    shape = jax.ShapeDtypeStruct((rows, kinds * share * count), BF16)
    return small_call(kernel, [shape], (value,))[0]


def vmem(*arrays):
    size = sum(math.prod(shape) * jnp.dtype(kind).itemsize for shape, kind in arrays)
    return pltpu.CompilerParams(vmem_limit_bytes=min(56 * 2**20, max(LIMIT, size + LIMIT)))


def small_call(kernel, out_shape, args):
    whole = pl.BlockSpec(memory_space=pltpu.VMEM)
    return pl.pallas_call(
        kernel,
        in_specs=[whole] * len(args),
        out_specs=[whole] * len(out_shape),
        out_shape=out_shape,
        compiler_params=vmem(*[(v.shape, v.dtype) for v in (*args, *out_shape)]),
        cost_estimate=pl.CostEstimate(flops=0, bytes_accessed=2**22, transcendentals=0),
    )(*args)


def total(value):
    count = lax.axis_size("narrow")
    return jnp.sum(value.reshape((count, -1) + value.shape[1:]).astype(F32), axis=0)


def high_bits():
    return list(range(1, lax.axis_size("wide").bit_length() - 1))


def mirror_first(value):
    return {0: value} | {1 << bit: flip(value, bit) for bit in high_bits()}


def mirror_rest(known):
    bits = high_bits()
    width = known[0].shape[1]
    middle = width // (2 * PAIR) * PAIR
    came = {}
    for order, low, high in ((bits, 0, middle), (bits[::-1], middle, width)):
        have = {0: known[0][:, low:high]}
        for bit in order:
            have |= {
                mask ^ (1 << bit): known[1 << bit][:, low:high] if mask == 0 else flip(part, bit)
                for mask, part in have.items()
            }
        came |= {(mask, low): part for mask, part in have.items() if mask not in known}
    return came


def half_rest(known, turned):
    order = high_bits()[::-1] if turned else high_bits()
    have = {0: known[0]}
    for bit in order:
        have |= {
            mask ^ (1 << bit): known[1 << bit] if mask == 0 else flip(part, bit)
            for mask, part in have.items()
        }
    return {mask: part for mask, part in have.items() if mask not in known}


def half_join(*halves):
    pieces, first = [], 0
    for known, came in halves:
        pieces += [(value, mask >> 1, first) for mask, value in (known | came).items()]
        first += known[0].shape[1]
    (own,) = place(pieces, (first,))
    return own, flip(own, 0)


def mirror_join(known, came, widths):
    pieces = [(value, mask >> 1, 0) for mask, value in known.items()]
    pieces += [(value, mask >> 1, low) for (mask, low), value in came.items()]
    return place(pieces, widths)


def turned_gains(own, other, first):
    def kernel(own_ref, other_ref, out_ref):
        half = own_ref.shape[0]
        for number, source in enumerate((own_ref, other_ref)):
            out_ref[:, number * half : (number + 1) * half] = source[...].astype(F32).T[:8]

    part = pl.BlockSpec((own.shape[0], PAIR), lambda i: (0, first // PAIR))
    return pl.pallas_call(
        kernel,
        grid=(1,),
        in_specs=[part, part],
        out_specs=pl.BlockSpec((8, 2 * own.shape[0]), lambda i: (0, 0)),
        out_shape=jax.ShapeDtypeStruct((8, 2 * own.shape[0]), F32),
    )(far(own), far(other))


def column_block(width):
    return max(b for b in range(PAIR, 1537, PAIR) if width % b == 0)


class Unit:
    def __init__(self, left, right, plane, first, width):
        self.left, self.right, self.plane, self.first, self.width = left, right, plane, first, width


def by_step(starts, values, step):
    found = values[0]
    for start, value in zip(starts[1:], values[1:]):
        found = jnp.where(step >= start, value, found)
    return found


def grad_product(lanes, rows, away, came, joint, begin=0):
    units = [unit for lane in lanes for unit in lane]
    lane_of = [number for number, lane in enumerate(lanes) for _ in lane]
    tokens, features = units[0].left.shape
    count = lax.axis_size("wide")
    cut, tall = features // count, len(rows[0])
    block = min(column_block(unit.width) for unit in units)
    counts = [unit.width // block for unit in units]
    starts = [sum(counts[:number]) for number in range(len(units))]
    lane_starts = [starts[lane_of.index(number)] for number in range(len(lanes))]
    lane_counts = [sum(unit.width for unit in lane) // block for lane in lanes]
    lefts = list({id(unit.left): unit.left for unit in units}.values())
    left_of = [[left is unit.left for left in lefts].index(True) for unit in units]

    def unit_spec(number, unit):
        return pl.BlockSpec(
            (1, tokens, block),
            lambda i: (
                unit.plane,
                0,
                jnp.clip(i - starts[number], 0, counts[number] - 1) + unit.first // block,
            ),
        )

    def away_spec(place):
        return pl.BlockSpec(
            (cut, block),
            lambda i: (by_step(lane_starts, [row[place] for row in rows], i), i + begin // block),
        )

    def lane_spec(number, height, row):
        return pl.BlockSpec(
            (height, block),
            lambda i: (row, jnp.clip(i - lane_starts[number], 0, lane_counts[number] - 1)),
        )

    side = 0 if rows[0][0] < count // 2 else 1
    in_specs = [pl.BlockSpec((tokens, features // 2), lambda i: (0, side)) for _ in lefts]
    in_specs += [unit_spec(number, unit) for number, unit in enumerate(units)]
    args = lefts + [unit.right for unit in units]
    if away is not None:
        in_specs += [away_spec(place) for place in range(tall)]
        args += [away] * tall
    at = {}
    for number, pairs in enumerate(came):
        for place in range(tall):
            at[number, place] = []
            for array, row_blocks in pairs:
                at[number, place].append(len(args))
                in_specs.append(lane_spec(number, cut, row_blocks[place]))
                args.append(array)
    widths = [sum(unit.width for unit in lane) for lane in lanes]
    if joint:
        out_specs = [pl.BlockSpec((tall * cut, block), lambda i: (0, i))]
        out_shape = [pltpu.HBM((tall * cut, sum(widths)), BF16)]
    else:
        out_specs = [lane_spec(number, tall * cut, 0) for number in range(len(lanes))]
        out_shape = [pltpu.HBM((tall * cut, width), BF16) for width in widths]

    def kernel(*refs):
        outs, turned = refs[len(args) : -1], refs[-1]
        step = pl.program_id(0)
        for number, unit in enumerate(units):
            lane = lane_of[number]

            @pl.when(step == starts[number])
            def _():
                for place, row in enumerate(rows[lane]):
                    first = (row - side * (count // 2)) * cut
                    source = refs[left_of[number]][:, first : first + cut]
                    turned[place * cut : (place + 1) * cut, :] = source.T

            @pl.when((step >= starts[number]) & (step < starts[number] + counts[number]))
            def _():
                product = dot(turned[...], refs[len(lefts) + number][0], (1, 0))
                out = outs[0] if joint else outs[lane]
                for place in range(tall):
                    part = product[place * cut : (place + 1) * cut]
                    if away is not None:
                        part += refs[len(lefts) + len(units) + place][...].astype(F32)
                    for spot in at.get((lane, place), ()):
                        part += refs[spot][...].astype(F32)
                    out[place * cut : (place + 1) * cut, :] = part.astype(BF16)

    return pl.pallas_call(
        kernel,
        grid=(sum(counts),),
        in_specs=in_specs,
        out_specs=out_specs,
        out_shape=out_shape,
        scratch_shapes=[pltpu.VMEM((tall * cut, tokens), BF16)],
        compiler_params=vmem(
            *[((2, tokens, features), BF16)] * len(lefts),
            *[((2, tokens, block), BF16)] * len(units),
            *[((2, tall * cut, block), BF16)] * (2 + len(out_shape)),
            *[((2, cut, block), BF16)] * sum(len(pairs) * tall for pairs in came),
            ((tall * cut, block), F32),
        ),
        cost_estimate=pl.CostEstimate(
            flops=2 * tall * cut * sum(widths) * tokens,
            bytes_accessed=4 * tall * cut * sum(widths),
            transcendentals=0,
        ),
    )(*[far(value) for value in args])


class Sum:
    def __init__(self, *lanes):
        bits = high_bits()
        sides = 1 << len(bits)
        self.lanes = lanes
        self.orders = [bits if number % 2 else bits[::-1] for number in range(len(lanes))]
        self.came = [[] for _ in lanes]
        self.keep = []
        for order in self.orders:
            held, lists = list(range(sides)), []
            for bit in order:
                lists.append([mask for mask in held if mask << 1 >> bit & 1])
                held = [mask for mask in held if not mask << 1 >> bit & 1]
                lists.append(held)
            self.keep.append(lists)
        rows = [[sides + mask for mask in range(sides)]] * len(lanes)
        self.state = grad_product(lanes, rows, None, [[] for _ in lanes], True)

    def over_core(self):
        self.away = flip(self.state[0], 0)
        self.state = [self.away]
        return self

    def parts(self, which, level):
        last = level == len(self.orders[0])
        lanes, rows, came, starts = [], [], [], []
        for number in which:
            lists = self.keep[number]
            row = lists[2 * level - 1] if last else lists[2 * level]
            lanes.append(self.lanes[number])
            rows.append(row)
            came.append(
                [
                    (array, [lists[2 * step + 1].index(mask) for mask in row])
                    for step, array in enumerate(self.came[number])
                ]
            )
        widths = [sum(unit.width for unit in lane) for lane in self.lanes]
        return grad_product(lanes, rows, self.away, came, last, sum(widths[: which[0]]))

    def which(self, which):
        return list(which) or list(range(len(self.lanes)))

    def add_own(self, *which):
        which = self.which(which)
        self.ready = dict(zip(which, self.parts(which, 0)))
        self.state = [self.away, self.ready]
        return self

    def sync_from(self, state):
        self.state = state
        self.away = state[0]
        if len(state) > 1:
            self.ready = state[1]
        if len(state) > 2:
            self.came = state[2]

    def over_first(self, *which):
        for number in self.which(which):
            self.came[number] = [flip(self.ready[number], self.orders[number][0])]
        self.state = [self.away, self.ready, self.came]
        return self

    def over_rest(self, *which):
        which = self.which(which)
        for level in range(1, len(self.orders[0])):
            parts = self.parts(which, level)
            for number, part in zip(which, parts):
                self.came[number] = self.came[number] + [flip(part, self.orders[number][level])]
        self.state = [self.away, self.ready, self.came]
        return self

    def whole(self, *which):
        return self.parts(self.which(which), len(self.orders[0]))[0]


def hold(sums, *values):
    flat, tree = jax.tree.flatten(([one.state for one in sums], values))
    states, values = jax.tree.unflatten(tree, lax.optimization_barrier(flat))
    for one, state in zip(sums, states):
        one.sync_from(state)
    return values


def block_order():
    count = lax.axis_size("wide")
    here = lax.axis_index("wide")
    masks = [mask << 1 for mask in range(count // 2)]
    return [here ^ mask for mask in masks + [mask + 1 for mask in masks]]


def blocks_kernel(count, spot_ref, *refs):
    for source, target in zip(refs[: len(refs) // 2], refs[len(refs) // 2 :]):
        width = source.shape[1] // count
        for number in range(count):
            spot = pl.multiple_of(spot_ref[number] * width, PAIR)
            target[:, number * width : (number + 1) * width] = source[:, pl.ds(spot, width)]


def blocks(values, spots):
    count = len(spots)
    whole = pl.BlockSpec(memory_space=pltpu.VMEM)
    return pl.pallas_call(
        lambda *refs: blocks_kernel(count, *refs),
        in_specs=[pl.BlockSpec(memory_space=pltpu.SMEM)] + [whole] * len(values),
        out_specs=[whole] * len(values),
        out_shape=[jax.ShapeDtypeStruct(value.shape, value.dtype) for value in values],
        compiler_params=pltpu.CompilerParams(vmem_limit_bytes=2 * LIMIT),
        cost_estimate=pl.CostEstimate(flops=0, bytes_accessed=2**22, transcendentals=0),
    )(jnp.stack(spots).astype(jnp.int32), *values)


def to_own(*values):
    return blocks(values, block_order())


def from_own(*values):
    count = lax.axis_size("wide")
    here = lax.axis_index("wide")
    places = [((j ^ here) >> 1) + ((j ^ here) & 1) * (count // 2) for j in range(count)]
    return blocks(values, places)


def all_sum_chain(value):
    return [value] + [shift(value, step) for step in range(1, lax.axis_size("narrow"))]


def all_sum_cube(value):
    count = lax.axis_size("wide")

    def over(mask):
        return lax.ppermute(value, "wide", [(i, i ^ mask) for i in range(count)])

    return [value] + [over(mask << 1) for mask in range(1, count // 2)]


def shard_place():
    return lax.axis_index("wide") * lax.axis_size("narrow") + lax.axis_index("narrow")


def matmul_block(width, first):
    fits = [b for b in range(PAIR, 1537, PAIR) if width % b == 0 and first % b == 0]
    return max(fits)


def into(value, weight, first, width, kind):
    tokens, features = value.shape
    half = features // 2
    block = matmul_block(width, first)
    if block == width:
        block //= 2

    def kernel(value_ref, own_ref, other_ref, out_ref):
        product = dot(value_ref[:, :half], own_ref[...], (1, 0))
        product += dot(value_ref[:, half:], other_ref[...], (1, 0))
        out_ref[...] = product.astype(kind)

    part = pl.BlockSpec((half, block), lambda i: (0, i + first // block))
    return pl.pallas_call(
        kernel,
        grid=(width // block,),
        in_specs=[pl.BlockSpec(value.shape, lambda i: (0, 0)), part, part],
        out_specs=pl.BlockSpec((tokens, block), lambda i: (0, i)),
        out_shape=jax.ShapeDtypeStruct((tokens, width), kind),
        compiler_params=vmem(
            (value.shape, F32), ((4, half, block), BF16), ((4, tokens, block), F32)
        ),
        cost_estimate=pl.CostEstimate(
            flops=2 * tokens * features * width,
            bytes_accessed=2 * features * width,
            transcendentals=0,
        ),
    )(value, *[far(part) for part in weight])


def out_of(value, weight, first):
    planes, tokens, width = value.shape
    half = weight[0].shape[0]
    block = matmul_block(width, first)
    if block == width and planes == 1:
        block //= 2
    steps = width // block

    def kernel(value_ref, own_ref, other_ref, out_ref):
        own = dot(value_ref[0], own_ref[...], (1, 1))
        other = dot(value_ref[0], other_ref[...], (1, 1))

        @pl.when(pl.program_id(0) == 0)
        def _():
            out_ref[:, :half] = own
            out_ref[:, half:] = other

        @pl.when(pl.program_id(0) > 0)
        def _():
            out_ref[:, :half] += own
            out_ref[:, half:] += other

    part = pl.BlockSpec((half, block), lambda i: (0, i + first // block))
    return pl.pallas_call(
        kernel,
        grid=(planes * steps,),
        in_specs=[
            pl.BlockSpec((1, tokens, block), lambda i: (i // steps, 0, i % steps)),
            part,
            part,
        ],
        out_specs=pl.BlockSpec((tokens, 2 * half), lambda i: (0, 0)),
        out_shape=jax.ShapeDtypeStruct((tokens, 2 * half), F32),
        compiler_params=vmem(
            ((2, tokens, block), BF16), ((4, half, block), BF16), ((4, tokens, 2 * half), F32)
        ),
        cost_estimate=pl.CostEstimate(
            flops=4 * tokens * half * width * planes,
            bytes_accessed=4 * half * width * planes,
            transcendentals=0,
        ),
    )(value, *[far(part) for part in weight])


def feed_forward(value, weight, width):
    tokens, features = value.shape
    half = features // 2
    block = matmul_block(width, width)

    def kernel(value_ref, own_gate, other_gate, own_up, other_up, gate_ref, up_ref, act_ref):
        own, other = value_ref[:, :half], value_ref[:, half:]
        gate = dot(own, own_gate[...], (1, 0)) + dot(other, other_gate[...], (1, 0))
        up = dot(own, own_up[...], (1, 0)) + dot(other, other_up[...], (1, 0))
        gate_ref[...] = gate
        up_ref[...] = up
        act_ref[...] = gated(gate, up).astype(BF16)

    gate_part = pl.BlockSpec((half, block), lambda i: (0, i))
    up_part = pl.BlockSpec((half, block), lambda i: (0, i + width // block))
    out = pl.BlockSpec((tokens, block), lambda i: (0, i))
    return pl.pallas_call(
        kernel,
        grid=(width // block,),
        in_specs=[pl.BlockSpec(value.shape, lambda i: (0, 0))]
        + [gate_part, gate_part, up_part, up_part],
        out_specs=[out] * 3,
        out_shape=[jax.ShapeDtypeStruct((tokens, width), kind) for kind in (F32, F32, BF16)],
        compiler_params=vmem(((8, half, block), BF16), ((9, tokens, block), F32)),
        cost_estimate=pl.CostEstimate(
            flops=4 * tokens * features * width,
            bytes_accessed=4 * features * width,
            transcendentals=0,
        ),
    )(value, *[far(part) for part in (*weight, *weight)])


def feed_back(value, weight, gate, up):
    tokens, features = value.shape
    half = features // 2
    width = gate.shape[1]
    block = matmul_block(width, 0)

    def kernel(value_ref, own_ref, other_ref, gate_ref, up_ref, out_ref):
        grad = dot(value_ref[:, :half], own_ref[...], (1, 0))
        grad += dot(value_ref[:, half:], other_ref[...], (1, 0))
        dgate, dup = jax.vjp(gated, gate_ref[...], up_ref[...])[1](grad)
        out_ref[0] = dgate.astype(BF16)
        out_ref[1] = dup.astype(BF16)

    part = pl.BlockSpec((half, block), lambda i: (0, i))
    wide = pl.BlockSpec((tokens, block), lambda i: (0, i))
    return pl.pallas_call(
        kernel,
        grid=(width // block,),
        in_specs=[pl.BlockSpec(value.shape, lambda i: (0, 0)), part, part, wide, wide],
        out_specs=pl.BlockSpec((2, tokens, block), lambda i: (0, 0, i)),
        out_shape=jax.ShapeDtypeStruct((2, tokens, width), BF16),
        compiler_params=vmem(((4, half, block), BF16), ((9, tokens, block), F32)),
        cost_estimate=pl.CostEstimate(
            flops=2 * tokens * features * width,
            bytes_accessed=4 * features * width,
            transcendentals=0,
        ),
    )(value, *[far(part) for part in weight], gate, up)


def rms_norm(hidden, gain):
    return hidden * lax.rsqrt(jnp.mean(hidden * hidden, axis=-1, keepdims=True) + EPS) * gain


def gated(gate, up):
    return jax.nn.gelu(gate) * up


def advance(master, moment, trail, grad, rate):
    new_moment = 0.5 * moment + 0.5 * grad
    new_master = master - rate * (grad + 0.5 * new_moment)
    new_trail = 0.5 * trail + 0.5 * new_master
    return (new_master, new_moment, new_trail, new_master.astype(BF16))


def on_device(
    tokens,
    memory,
    dec_ids,
    enc_ids,
    cotangent,
    query_weight,
    query_moment,
    query_trail,
    keyval_weight,
    keyval_moment,
    keyval_trail,
    output_weight,
    output_moment,
    output_trail,
    inner_weight,
    inner_moment,
    inner_trail,
    outer_weight,
    outer_moment,
    outer_trail,
    norm_gains,
    gains_moment,
    gains_trail,
):
    rows, local_len, width = tokens.shape
    mem_local = memory.shape[1]
    narrow_count = lax.axis_size("narrow")
    seq_len = local_len * narrow_count
    inner_width = outer_weight.shape[0]
    q_width, kv_width = query_weight.shape[2], keyval_weight.shape[2]
    gain_count, gain_width = norm_gains.shape
    q_share, kv_share = q_width // narrow_count, kv_width // (2 * narrow_count)

    gain_cols = jnp.pad(norm_gains.astype(BF16).T, ((0, 0), (0, PAIR - gain_count)))
    shard0 = jnp.concatenate(
        [query_weight[0].astype(BF16), keyval_weight[0].astype(BF16), gain_cols], axis=1
    )
    z0 = spread_steps(shard0, near_steps() + far_steps())
    shard1 = jnp.concatenate(
        [
            output_weight[0].T.astype(BF16),
            query_weight[1].astype(BF16),
            keyval_weight[1].astype(BF16),
            output_weight[1].T.astype(BF16),
        ],
        axis=1,
    )
    tokens_own, memory_own, grad_ffn = to_own(
        tokens.reshape(local_len, width),
        memory.reshape(mem_local, width),
        cotangent.reshape(local_len, width),
    )
    z0, shard1, tokens_own, memory_own, grad_ffn = sync(
        z0, shard1, tokens_own, memory_own, grad_ffn
    )
    dec_col, dec_row = dec_ids.reshape(-1, 1), dec_ids.reshape(1, -1)
    enc_col = enc_ids.reshape(-1, 1)
    g0 = mirror_first(*spread_join(shard0, z0))
    z1 = spread_steps(shard1, near_steps())
    shard2 = inner_weight.astype(BF16)
    shard3 = outer_weight.T.astype(BF16)
    hidden = tokens_own.astype(F32)
    g0, z1, shard1, shard2, shard3 = sync(g0, z1, shard1, shard2, shard3)
    r0 = mirror_rest(g0)
    z1 |= spread_steps(shard1, far_steps())
    r0, z1 = sync(r0, z1)
    (own,) = mirror_join(g0, r0, (q_width + kv_width + PAIR,))
    w_zero = (own, flip(own, 0))
    a1, b1 = spread_join(shard1, z1, width + q_width, kv_width + width)
    a1 = mirror_first(a1)
    z2 = spread_steps(shard2, near_steps())
    w_zero, b1 = sync(w_zero, b1)
    gains = turned_gains(*w_zero, q_width + kv_width)
    normed_one = rms_norm(hidden, gains[0]).astype(BF16)
    query_one = into(normed_one, w_zero, 0, q_width, BF16)
    keyval_one = into(normed_one, w_zero, q_width, kv_width, BF16)
    pieces = cut_columns([query_one, keyval_one[:, : kv_width // 2], keyval_one[:, kv_width // 2 :]])
    pieces, a1, b1, shard2, z2 = sync(pieces, a1, b1, shard2, z2)
    joint_one = trade(pieces)
    b1 = mirror_first(b1)
    joint_one, b1, shard2 = sync(joint_one, b1, shard2)
    ra1, rb1 = half_rest(a1, False), half_rest(b1, True)
    z2 |= spread_steps(shard2, far_steps())
    context, stat_one = attention(joint_one, dec_col, dec_row, local_len, True)
    context, ra1, rb1, z2 = sync(context, ra1, rb1, z2)
    came = trade(context)
    w_one = half_join((a1, ra1), (b1, rb1))
    a2, b2 = spread_join(shard2, z2, inner_width, inner_width)
    a2 = mirror_first(a2)
    came, w_one, shard3, b2 = sync(came, w_one, shard3, b2)
    kv_at, o_two_at = width + q_width, width + q_width + kv_width
    z3 = spread_steps(shard3, near_steps() + far_steps())
    context_one = join_columns(came, q_share)
    after_one = hidden + out_of(context_one[None], w_one, 0)
    normed_two = rms_norm(after_one, gains[1]).astype(BF16)
    query_two = into(normed_two, w_one, width, q_width, BF16)
    keyval_two = into(memory_own, w_one, kv_at, kv_width, BF16)
    pieces = cut_columns([query_two, keyval_two[:, : kv_width // 2], keyval_two[:, kv_width // 2 :]])
    a2, z3, pieces, after_one, b2, shard3 = sync(a2, z3, pieces, after_one, b2, shard3)
    joint_two = trade(pieces)
    b2 = mirror_first(b2)
    half_inner = inner_width // 2
    a3, b3 = spread_join(shard3, z3, half_inner, half_inner)
    joint_two, b2, a3, b3 = sync(joint_two, b2, a3, b3)
    ra2, rb2 = half_rest(a2, False), half_rest(b2, True)
    context, stat_two = attention(joint_two, enc_col, dec_row, local_len, False)
    context, ra2, rb2, a3, b3 = sync(context, ra2, rb2, a3, b3)
    came = trade(context)
    a3 = mirror_first(a3)
    w_in = half_join((a2, ra2), (b2, rb2))
    came, w_in, a3, b3 = sync(came, w_in, a3, b3)
    b3 = mirror_first(b3)
    context_two = join_columns(came, q_share)
    after_two = after_one + out_of(context_two[None], w_one, o_two_at)
    normed_three = rms_norm(after_two, gains[2]).astype(BF16)
    b3, normed_three, after_two = sync(b3, normed_three, after_two)
    ra3, rb3 = half_rest(a3, False), half_rest(b3, True)
    gate, up, activated = feed_forward(normed_three, w_in, inner_width)
    ra3, rb3, gate, up, activated = sync(ra3, rb3, gate, up, activated)
    w_out = half_join((a3, ra3), (b3, rb3))
    sum_outs = Sum(
        [Unit(grad_ffn, activated[None], 0, 0, half_inner)],
        [Unit(grad_ffn, activated[None], 0, half_inner, half_inner)],
    )
    w_out, activated = hold([sum_outs], w_out, activated)
    sum_outs.over_core()
    grad_inner = feed_back(grad_ffn, w_out, gate, up)
    (grad_inner,) = hold([sum_outs], grad_inner)
    sum_outs.add_own()
    sum_ins = Sum(
        [Unit(normed_three, grad_inner, 0, 0, half_inner)],
        [Unit(normed_three, grad_inner, 0, half_inner, half_inner)],
        [Unit(normed_three, grad_inner, 1, 0, half_inner)],
        [Unit(normed_three, grad_inner, 1, half_inner, half_inner)],
    )
    (grad_inner,) = hold([sum_outs, sum_ins], grad_inner)
    sum_outs.over_first()
    sum_ins.over_core()
    grad_normed = out_of(grad_inner, w_in, 0)
    grad_hidden, grad_gain_three = jax.vjp(rms_norm, after_two, gains[2])[1](grad_normed)
    grad_two = grad_ffn.astype(F32) + grad_hidden
    grad_branch = grad_two.astype(BF16)
    pieces = cut_columns([into(grad_branch, w_one, o_two_at, width, BF16)])
    pieces, grad_branch_two = hold([sum_ins, sum_outs], pieces, grad_branch)
    grad_context = trade(pieces)
    sum_outs.over_rest()
    sum_ins.add_own()
    outer_whole = sum_outs.whole()
    grad_context, outer_whole = hold([sum_ins], grad_context, outer_whole)
    sum_ins.over_first(0, 1)
    outer_parts = trade(outer_whole)
    dquery, dkeyval = attention_back(
        joint_two, grad_context, stat_two, enc_col, dec_row, local_len, False
    )
    dquery, dkeyval, activated, outer_parts = hold(
        [sum_ins], dquery, dkeyval, activated, outer_parts
    )
    came = trade(dquery)
    sum_ins.over_first(2, 3)
    result = after_two + out_of(activated[None], w_out, 0)
    (block_out,) = from_own(result.astype(BF16))
    came, dkeyval, block_out = hold([sum_ins], came, dkeyval, block_out)
    came_too = trade(dkeyval)
    sum_ins.over_rest()
    query_grad_two = join_columns(came, q_share)
    grad_normed_two = out_of(query_grad_two[None], w_one, width)
    grad_hidden, grad_gain_two = jax.vjp(rms_norm, after_one, gains[1])[1](grad_normed_two)
    grad_one = grad_two + grad_hidden
    grad_branch = grad_one.astype(BF16)
    pieces = cut_columns([into(grad_branch, w_one, 0, width, BF16)])
    pieces, grad_branch, came_too = hold([sum_ins], pieces, grad_branch, came_too)
    grad_context = trade(pieces)
    gate_whole = sum_ins.whole(0, 1)
    keyval_grad_two = join_columns(came_too, kv_share, 2)
    sum_mid = Sum(
        [
            Unit(grad_branch_two, context_two[None], 0, 0, width),
            Unit(memory_own, keyval_grad_two[None], 0, 0, kv_width),
        ],
        [
            Unit(normed_two, query_grad_two[None], 0, 0, q_width),
            Unit(grad_branch, context_one[None], 0, 0, width),
        ],
    )
    grad_context, keyval_grad_two, gate_whole = hold(
        [sum_mid, sum_ins], grad_context, keyval_grad_two, gate_whole
    )
    sum_mid.over_core()
    gate_parts = trade(gate_whole)
    dquery, dkeyval = attention_back(
        joint_one, grad_context, stat_one, dec_col, dec_row, local_len, True
    )
    sum_mid.add_own()
    dquery, dkeyval, keyval_grad_two, outer_parts, gate_parts = hold(
        [sum_mid], dquery, dkeyval, keyval_grad_two, outer_parts, gate_parts
    )
    came = trade(dquery)
    sum_mid.over_first()
    (memory_grad,) = from_own(out_of(keyval_grad_two[None], w_one, kv_at))
    sum_outer = total(outer_parts).T
    up_whole = sum_ins.whole(2, 3)
    came, sum_outer, memory_grad, dkeyval, up_whole = hold(
        [sum_mid], came, sum_outer, memory_grad, dkeyval, up_whole
    )
    came_too = trade(dkeyval)
    sum_mid.over_rest()
    query_grad_one = join_columns(came, q_share)
    grad_normed_one = out_of(query_grad_one[None], w_zero, 0)
    came_too, grad_normed_one = hold([sum_mid], came_too, grad_normed_one)
    keyval_grad_one = join_columns(came_too, kv_share, 2)
    sum_last = Sum(
        [Unit(normed_one, query_grad_one[None], 0, 0, q_width)],
        [Unit(normed_one, keyval_grad_one[None], 0, 0, kv_width)],
    )
    up_parts = trade(up_whole)
    mid_whole = sum_mid.whole()
    keyval_grad_one, mid_whole = hold([sum_last], keyval_grad_one, mid_whole)
    sum_last.over_core()
    mid_parts = trade(mid_whole)
    (keyval_grad_one,) = hold([sum_last], keyval_grad_one)
    sum_last.add_own()
    (keyval_grad_one,) = hold([sum_last], keyval_grad_one)
    sum_last.over_first()
    grad_normed_one += out_of(keyval_grad_one[None], w_zero, q_width)
    grad_hidden, grad_gain_one = jax.vjp(rms_norm, hidden, gains[0])[1](grad_normed_one)
    input_grad, full_gains = from_own(
        grad_one + grad_hidden,
    ) + from_own(jnp.stack([grad_gain_one, grad_gain_two, grad_gain_three]))
    input_grad, full_gains = hold([sum_last], input_grad, full_gains)
    sum_last.over_rest()
    gain_parts = all_sum_cube(full_gains)
    sum_inner = jnp.concatenate([total(gate_parts), total(up_parts)], axis=1)
    gain_parts, mid_parts = hold([sum_last], gain_parts, mid_parts)
    sum_two = total(mid_parts)
    last_parts = trade(sum_last.whole())
    part = sum(gain_parts)
    full_gains = sum(all_sum_chain(part + flip(part, 0)))
    sum_gains = lax.dynamic_slice_in_dim(full_gains, shard_place() * gain_width, gain_width, 1)
    sum_one = total(last_parts)
    after_kv, after_q = width + kv_width, width + kv_width + q_width
    sum_query = jnp.stack([sum_one[:, :q_width], sum_two[:, after_kv:after_q]])
    sum_keyval = jnp.stack([sum_one[:, q_width:], sum_two[:, width:after_kv]])
    sum_output = jnp.stack([sum_two[:, after_q:], sum_two[:, :width]]).transpose(0, 2, 1)
    block_out = block_out.reshape(rows, local_len, width)
    input_grad = input_grad.reshape(rows, local_len, width)
    memory_grad = memory_grad.reshape(rows, mem_local, width)
    token_total = rows * lax.axis_size("wide") * seq_len
    rate = RATE / math.sqrt(token_total)
    output_rate = OUTPUT_RATE / math.sqrt(token_total)
    new_query = advance(query_weight, query_moment, query_trail, sum_query, rate)
    new_keyval = advance(keyval_weight, keyval_moment, keyval_trail, sum_keyval, rate)
    new_output = advance(output_weight, output_moment, output_trail, sum_output, output_rate)
    new_inner = advance(inner_weight, inner_moment, inner_trail, sum_inner, rate)
    new_outer = advance(outer_weight, outer_moment, outer_trail, sum_outer, rate)
    new_gains = advance(norm_gains, gains_moment, gains_trail, sum_gains, rate)
    return (
        block_out,
        input_grad,
        memory_grad,
        new_query[0],
        new_query[1],
        new_query[2],
        new_query[3],
        new_keyval[0],
        new_keyval[1],
        new_keyval[2],
        new_keyval[3],
        new_output[0],
        new_output[1],
        new_output[2],
        new_output[3],
        new_inner[0],
        new_inner[1],
        new_inner[2],
        new_inner[3],
        new_outer[0],
        new_outer[1],
        new_outer[2],
        new_outer[3],
        new_gains[0],
        new_gains[1],
        new_gains[2],
        new_gains[3],
    )


def solution(mesh):
    in_specs = (
        P("wide", "narrow", None),
        P("wide", "narrow", None),
        P("wide", None),
        P("wide", None),
        P("wide", "narrow", None),
        P(None, ("wide", "narrow"), None),
        P(None, ("wide", "narrow"), None),
        P(None, ("wide", "narrow"), None),
        P(None, ("wide", "narrow"), None),
        P(None, ("wide", "narrow"), None),
        P(None, ("wide", "narrow"), None),
        P(None, None, ("wide", "narrow")),
        P(None, None, ("wide", "narrow")),
        P(None, None, ("wide", "narrow")),
        P(("wide", "narrow"), None),
        P(("wide", "narrow"), None),
        P(("wide", "narrow"), None),
        P(None, ("wide", "narrow")),
        P(None, ("wide", "narrow")),
        P(None, ("wide", "narrow")),
        P(None, ("wide", "narrow")),
        P(None, ("wide", "narrow")),
        P(None, ("wide", "narrow")),
    )
    out_specs = (
        P("wide", "narrow", None),
        P("wide", "narrow", None),
        P("wide", "narrow", None),
        P(None, ("wide", "narrow"), None),
        P(None, ("wide", "narrow"), None),
        P(None, ("wide", "narrow"), None),
        P(None, ("wide", "narrow"), None),
        P(None, ("wide", "narrow"), None),
        P(None, ("wide", "narrow"), None),
        P(None, ("wide", "narrow"), None),
        P(None, ("wide", "narrow"), None),
        P(None, None, ("wide", "narrow")),
        P(None, None, ("wide", "narrow")),
        P(None, None, ("wide", "narrow")),
        P(None, None, ("wide", "narrow")),
        P(("wide", "narrow"), None),
        P(("wide", "narrow"), None),
        P(("wide", "narrow"), None),
        P(("wide", "narrow"), None),
        P(None, ("wide", "narrow")),
        P(None, ("wide", "narrow")),
        P(None, ("wide", "narrow")),
        P(None, ("wide", "narrow")),
        P(None, ("wide", "narrow")),
        P(None, ("wide", "narrow")),
        P(None, ("wide", "narrow")),
        P(None, ("wide", "narrow")),
    )
    return jax.shard_map(
        on_device, mesh=mesh, in_specs=in_specs, out_specs=out_specs, check_vma=False
    )
```

```python
import math

import jax
import jax.numpy as jnp
from jax import lax
from jax.experimental import pallas as pl
from jax.experimental.pallas import tpu as pltpu
from jax.sharding import PartitionSpec as P

HDIM = 64
PAIR = 2 * HDIM
EPS = 1e-06
NEG = -1e30
RATE = 0.02
OUTPUT_RATE = 0.15
LIMIT = 16 * 2**20
BF16 = jnp.bfloat16
F32 = jnp.float32


def dot(left, right, sides):
    return lax.dot_general(
        left, right, (((sides[0],), (sides[1],)), ((), ())), preferred_element_type=F32
    )


def matmul(left, right):
    return dot(left, right, (1, 0))


def matmul_right(left, right):
    return dot(left, right, (1, 1))


def matmul_left(left, right):
    return dot(left, right, (0, 0))


def in_group(block, group):
    low = lax.broadcasted_iota(jnp.int32, block.shape, 1) < HDIM
    turned = jnp.concatenate([block[:, HDIM:], block[:, :HDIM]], axis=1)
    zero = jnp.zeros_like(block)
    if group == 0:
        return jnp.where(low, block, zero), jnp.where(low, turned, zero)
    return jnp.where(low, zero, turned), jnp.where(low, zero, block)


def allowed(kid_ref, qid_ref, bias_ref, span, order):
    keep = kid_ref[:span] == qid_ref[...]
    if order:
        count = qid_ref.shape[1]
        keys = lax.broadcasted_iota(jnp.int32, keep.shape, 0)
        queries = lax.broadcasted_iota(jnp.int32, keep.shape, 1) + pl.program_id(0) * count
        keep &= keys <= queries
    bias_ref[:span] = jnp.where(keep, 0.0, NEG).astype(F32)


def by_span(order, count, full, body):
    if not order:
        body(full)
        return
    for number in range(full // count):
        pl.when(pl.program_id(0) == number)(lambda number=number: body((number + 1) * count))


def forward_kernel(order, query_ref, key_ref, value_ref, kid_ref, qid_ref, *rest):
    out_ref, stat_ref, bias_ref = rest
    count, width = query_ref.shape

    def body(span):
        allowed(kid_ref, qid_ref, bias_ref, span, order)
        keys = key_ref[:span]
        values = value_ref[:span].T
        for group in range(width // PAIR):
            columns = slice(group * PAIR, (group + 1) * PAIR)
            rows = slice(group * HDIM, (group + 1) * HDIM)
            block = query_ref[:, columns] * jnp.asarray(HDIM**-0.5, BF16)
            parts = []
            for side, query in enumerate(in_group(block, group)):
                logits = dot(keys, query, (1, 1)) + bias_ref[:span]
                peak = jnp.max(logits, axis=0, keepdims=True)
                weights = jnp.exp(logits - peak)
                total = jnp.sum(weights, axis=0, keepdims=True)
                probs = (weights * (1.0 / total)).astype(BF16)
                parts.append(dot(values, probs, (1, 0))[rows])
                stat_ref[0, pl.ds(2 * group + side, 1), :] = peak + jnp.log(total)
            out_ref[:, columns] = jnp.concatenate(parts, axis=0).T.astype(BF16)

    by_span(order, count, key_ref.shape[0], body)


def backward_kernel(
    order, query_ref, key_ref, value_ref, kid_ref, qid_ref, grad_ref, stat_ref, *rest
):
    dquery_ref, dkeyval_ref, bias_ref, key_sum, value_sum = rest
    count, width = query_ref.shape

    @pl.when(pl.program_id(0) == 0)
    def _():
        key_sum[...] = jnp.zeros_like(key_sum)
        value_sum[...] = jnp.zeros_like(value_sum)

    def body(span):
        allowed(kid_ref, qid_ref, bias_ref, span, order)
        keys = key_ref[:span]
        values = value_ref[:span]
        keys_turned = keys.T
        dkey, dvalue = None, None
        for group in range(width // PAIR):
            columns = slice(group * PAIR, (group + 1) * PAIR)
            rows = slice(group * HDIM, (group + 1) * HDIM)
            queries = in_group(query_ref[:, columns] * jnp.asarray(HDIM**-0.5, BF16), group)
            grads = in_group(grad_ref[:, columns], group)
            parts = []
            for side in range(2):
                logits = dot(keys, queries[side], (1, 1)) + bias_ref[:span]
                probs = jnp.exp(logits - stat_ref[0, pl.ds(2 * group + side, 1), :])
                dprobs = dot(values, grads[side], (1, 1))
                dots = jnp.sum(probs * dprobs, axis=0, keepdims=True)
                dlogits = (probs * (dprobs - dots)).astype(BF16)
                parts.append(dot(keys_turned, dlogits, (1, 0))[rows])
                more_key = dot(dlogits, queries[side], (1, 0))
                more_value = dot(probs.astype(BF16), grads[side], (1, 0))
                dkey = more_key if dkey is None else dkey + more_key
                dvalue = more_value if dvalue is None else dvalue + more_value
            dquery_ref[:, columns] = (jnp.concatenate(parts, axis=0).T * HDIM**-0.5).astype(BF16)
        key_sum[:span] += dkey
        value_sum[:span] += dvalue

    by_span(order, count, key_ref.shape[0], body)

    @pl.when(pl.program_id(0) == pl.num_programs(0) - 1)
    def _():
        dkeyval_ref[:, :PAIR] = key_sum[...].astype(BF16)
        dkeyval_ref[:, PAIR:] = value_sum[...].astype(BF16)


def attention_specs(joint, count):
    span, width = joint.shape
    q_width = width - 2 * PAIR
    query = pl.BlockSpec((count, q_width), lambda i: (i, 0))
    keys = pl.BlockSpec((span, PAIR), lambda i: (0, q_width // PAIR))
    values = pl.BlockSpec((span, PAIR), lambda i: (0, q_width // PAIR + 1))
    key_ids = pl.BlockSpec((span, 1), lambda i: (0, 0))
    query_ids = pl.BlockSpec((1, count), lambda i: (0, i))
    stat = pl.BlockSpec((1, 8, count), lambda i: (i, 0, 0))
    return q_width, [query, keys, values, key_ids, query_ids], stat


def attention(joint, key_ids, query_ids, count, order):
    span = joint.shape[0]
    q_width, specs, s_spec = attention_specs(joint, count)
    return pl.pallas_call(
        lambda *refs: forward_kernel(order, *refs),
        grid=(span // count,),
        in_specs=specs,
        out_specs=[specs[0], s_spec],
        out_shape=[
            jax.ShapeDtypeStruct((span, q_width), BF16),
            jax.ShapeDtypeStruct((span // count, 8, count), F32),
        ],
        scratch_shapes=[pltpu.VMEM((span, count), F32)],
        compiler_params=pltpu.CompilerParams(vmem_limit_bytes=2 * LIMIT),
        cost_estimate=pl.CostEstimate(
            flops=4 * span * span * q_width, bytes_accessed=8 * span * q_width, transcendentals=0
        ),
    )(joint, joint, joint, key_ids, query_ids)


def attention_back(joint, grad, stat, key_ids, query_ids, count, order):
    span = joint.shape[0]
    q_width, specs, s_spec = attention_specs(joint, count)
    whole = pl.BlockSpec((span, 2 * PAIR), lambda i: (0, 0))
    return pl.pallas_call(
        lambda *refs: backward_kernel(order, *refs),
        grid=(span // count,),
        in_specs=specs + [specs[0], s_spec],
        out_specs=[specs[0], whole],
        out_shape=[
            jax.ShapeDtypeStruct((span, q_width), BF16),
            jax.ShapeDtypeStruct((span, 2 * PAIR), BF16),
        ],
        scratch_shapes=[
            pltpu.VMEM((span, count), F32),
            pltpu.VMEM((span, PAIR), F32),
            pltpu.VMEM((span, PAIR), F32),
        ],
        compiler_params=pltpu.CompilerParams(vmem_limit_bytes=2 * LIMIT),
        cost_estimate=pl.CostEstimate(
            flops=10 * span * span * q_width, bytes_accessed=16 * span * q_width, transcendentals=0
        ),
    )(joint, joint, joint, key_ids, query_ids, grad, stat)


def flip(value, bit):
    count = lax.axis_size("wide")
    return lax.ppermute(value, "wide", [(i, i ^ (1 << bit)) for i in range(count)])


def shift(value, step):
    count = lax.axis_size("narrow")
    return lax.ppermute(value, "narrow", [(i, (i + step) % count) for i in range(count)])


def sync(*values):
    return lax.optimization_barrier(values)


def place(pieces, widths):
    rows = pieces[0][0].shape[0]
    count = 1 + max(number for _, number, _ in pieces)

    def kernel(*refs):
        first = 0
        for target, cut in zip(refs[len(pieces) :], widths):
            for source, (piece, number, begin) in zip(refs, pieces):
                low, high = max(begin, first), min(begin + piece.shape[1], first + cut)
                if low < high:
                    target[number * rows : (number + 1) * rows, low - first : high - first] = source[
                        :, low - begin : high - begin
                    ]
            first += cut

    shapes = [jax.ShapeDtypeStruct((count * rows, cut), BF16) for cut in widths]
    return small_call(kernel, shapes, [piece for piece, _, _ in pieces])


def far(value):
    return pltpu.with_memory_space_constraint(value, pltpu.HBM)


def trade(value):
    return lax.all_to_all(value, "narrow", 0, 0, tiled=True)


def spread(value):
    count = lax.axis_size("narrow")
    return trade(jnp.concatenate([value] * count, axis=0))


def near_steps():
    return sorted({1, lax.axis_size("narrow") - 1})


def far_steps():
    return [s for s in range(1, lax.axis_size("narrow")) if s not in near_steps()]


def spread_steps(value, steps):
    return {step: shift(value, step) for step in steps}


def spread_join(value, came, *widths):
    count = lax.axis_size("narrow")
    pieces = [value] + [came[step] for step in sorted(came)]
    rows, width = value.shape
    widths = widths or (width,)
    firsts = [sum(widths[:number]) for number in range(len(widths))]
    spots = (lax.axis_index("narrow") - jnp.arange(count, dtype=jnp.int32)) % count
    if rows % 16:
        whole = jnp.zeros((count, rows, width), value.dtype)
        for number, piece in enumerate(pieces):
            whole = lax.dynamic_update_index_in_dim(whole, piece, spots[number], 0)
        whole = whole.reshape(count * rows, width)
        return [whole[:, first : first + wide] for first, wide in zip(firsts, widths)]

    def kernel(spot_ref, *refs):
        for number, source in enumerate(refs[:count]):
            spot = pl.multiple_of(spot_ref[number] * rows, rows)
            for target, first, wide in zip(refs[count:], firsts, widths):
                target[pl.ds(spot, rows), :] = source[:, first : first + wide]

    whole = pl.BlockSpec(memory_space=pltpu.VMEM)
    return pl.pallas_call(
        kernel,
        in_specs=[pl.BlockSpec(memory_space=pltpu.SMEM)] + [whole] * count,
        out_specs=[whole] * len(widths),
        out_shape=[jax.ShapeDtypeStruct((count * rows, wide), value.dtype) for wide in widths],
        compiler_params=pltpu.CompilerParams(vmem_limit_bytes=LIMIT),
        cost_estimate=pl.CostEstimate(flops=0, bytes_accessed=2**22, transcendentals=0),
    )(spots, *pieces)


def tight(width):
    return -(-width // PAIR) * PAIR


def cut_columns(parts):
    count = lax.axis_size("narrow")
    rows = parts[0][0].shape[0]
    shares = [wide // count for _, _, wide in parts]
    width = sum(tight(share) for share in shares)
    arrays = list({id(part): part for part, _, _ in parts}.values())
    index = [[part is array for array in arrays].index(True) for part, _, _ in parts]

    def kernel(*refs):
        target = refs[-1]
        for number in range(count):
            first = 0
            for (_, begin, _), source, share in zip(parts, index, shares):
                low = begin + number * share
                block = refs[source][:, low : low + share]
                if share % PAIR:
                    zeros = jnp.zeros((rows, tight(share) - share), BF16)
                    block = jnp.concatenate([block, zeros], axis=1)
                target[number * rows : (number + 1) * rows, first : first + tight(share)] = block
                first += tight(share)

    return small_call(kernel, [jax.ShapeDtypeStruct((count * rows, width), BF16)], arrays)[0]


def join_columns(value, share, kinds=1):
    count = lax.axis_size("narrow")
    rows = value.shape[0] // count

    def kernel(source, target):
        for kind in range(kinds):
            for number in range(count):
                place = (kind * count + number) * share
                target[:, place : place + share] = source[
                    number * rows : (number + 1) * rows,
                    kind * tight(share) : kind * tight(share) + share,
                ]

    shape = jax.ShapeDtypeStruct((rows, kinds * share * count), BF16)
    return small_call(kernel, [shape], (value,))[0]


def vmem(*arrays):
    size = sum(math.prod(shape) * jnp.dtype(kind).itemsize for shape, kind in arrays)
    return pltpu.CompilerParams(vmem_limit_bytes=min(56 * 2**20, max(LIMIT, size + LIMIT)))


def small_call(kernel, out_shape, args):
    whole = pl.BlockSpec(memory_space=pltpu.VMEM)
    return pl.pallas_call(
        kernel,
        in_specs=[whole] * len(args),
        out_specs=[whole] * len(out_shape),
        out_shape=out_shape,
        compiler_params=vmem(*[(v.shape, v.dtype) for v in (*args, *out_shape)]),
        cost_estimate=pl.CostEstimate(flops=0, bytes_accessed=2**22, transcendentals=0),
    )(*args)


def total(value):
    count = lax.axis_size("narrow")
    return jnp.sum(value.reshape((count, -1) + value.shape[1:]).astype(F32), axis=0)


def high_bits():
    return list(range(1, lax.axis_size("wide").bit_length() - 1))


def mirror_first(value):
    return {0: value} | {1 << bit: flip(value, bit) for bit in high_bits()}


def mirror_rest(known):
    bits = high_bits()
    width = known[0].shape[1]
    middle = width // (2 * PAIR) * PAIR
    came = {}
    for order, low, high in ((bits, 0, middle), (bits[::-1], middle, width)):
        have = {0: known[0][:, low:high]}
        for bit in order:
            have |= {
                mask ^ (1 << bit): known[1 << bit][:, low:high] if mask == 0 else flip(part, bit)
                for mask, part in have.items()
            }
        came |= {(mask, low): part for mask, part in have.items() if mask not in known}
    return came


def half_rest(known, turned):
    order = high_bits()[::-1] if turned else high_bits()
    have = {0: known[0]}
    for bit in order:
        have |= {
            mask ^ (1 << bit): known[1 << bit] if mask == 0 else flip(part, bit)
            for mask, part in have.items()
        }
    return {mask: part for mask, part in have.items() if mask not in known}


def half_join(*halves):
    pieces, first = [], 0
    for known, came in halves:
        pieces += [(value, mask >> 1, first) for mask, value in (known | came).items()]
        first += known[0].shape[1]
    (own,) = place(pieces, (first,))
    return own, flip(own, 0)


def mirror_join(known, came, widths):
    pieces = [(value, mask >> 1, 0) for mask, value in known.items()]
    pieces += [(value, mask >> 1, low) for (mask, low), value in came.items()]
    return place(pieces, widths)


def turned_gains(own, other, first):
    def kernel(own_ref, other_ref, out_ref):
        half = own_ref.shape[0]
        for number, source in enumerate((own_ref, other_ref)):
            out_ref[:, number * half : (number + 1) * half] = source[...].astype(F32).T[:8]

    part = pl.BlockSpec((own.shape[0], PAIR), lambda i: (0, first // PAIR))
    return pl.pallas_call(
        kernel,
        grid=(1,),
        in_specs=[part, part],
        out_specs=pl.BlockSpec((8, 2 * own.shape[0]), lambda i: (0, 0)),
        out_shape=jax.ShapeDtypeStruct((8, 2 * own.shape[0]), F32),
    )(far(own), far(other))


def column_block(width):
    return max(b for b in range(PAIR, 1537, PAIR) if width % b == 0)


class Unit:
    def __init__(self, left, right, plane, first, width):
        self.left, self.right, self.plane, self.first, self.width = left, right, plane, first, width


def by_step(starts, values, step):
    found = values[0]
    for start, value in zip(starts[1:], values[1:]):
        found = jnp.where(step >= start, value, found)
    return found


def grad_product(lanes, rows, away, came, joint, begin=0):
    units = [unit for lane in lanes for unit in lane]
    lane_of = [number for number, lane in enumerate(lanes) for _ in lane]
    tokens, features = units[0].left.shape
    count = lax.axis_size("wide")
    cut, tall = features // count, len(rows[0])
    block = min(column_block(unit.width) for unit in units)
    counts = [unit.width // block for unit in units]
    starts = [sum(counts[:number]) for number in range(len(units))]
    lane_starts = [starts[lane_of.index(number)] for number in range(len(lanes))]
    lane_counts = [sum(unit.width for unit in lane) // block for lane in lanes]
    lefts = list({id(unit.left): unit.left for unit in units}.values())
    left_of = [[left is unit.left for left in lefts].index(True) for unit in units]

    def unit_spec(number, unit):
        return pl.BlockSpec(
            (1, tokens, block),
            lambda i: (
                unit.plane,
                0,
                jnp.clip(i - starts[number], 0, counts[number] - 1) + unit.first // block,
            ),
        )

    def away_spec(place):
        return pl.BlockSpec(
            (cut, block),
            lambda i: (by_step(lane_starts, [row[place] for row in rows], i), i + begin // block),
        )

    def lane_spec(number, height, row):
        return pl.BlockSpec(
            (height, block),
            lambda i: (row, jnp.clip(i - lane_starts[number], 0, lane_counts[number] - 1)),
        )

    side = 0 if rows[0][0] < count // 2 else 1
    in_specs = [pl.BlockSpec((tokens, features // 2), lambda i: (0, side)) for _ in lefts]
    in_specs += [unit_spec(number, unit) for number, unit in enumerate(units)]
    args = lefts + [unit.right for unit in units]
    if away is not None:
        in_specs += [away_spec(place) for place in range(tall)]
        args += [away] * tall
    at = {}
    for number, pairs in enumerate(came):
        for place in range(tall):
            at[number, place] = []
            for array, row_blocks in pairs:
                at[number, place].append(len(args))
                in_specs.append(lane_spec(number, cut, row_blocks[place]))
                args.append(array)
    widths = [sum(unit.width for unit in lane) for lane in lanes]
    if joint:
        out_specs = [pl.BlockSpec((tall * cut, block), lambda i: (0, i))]
        out_shape = [pltpu.HBM((tall * cut, sum(widths)), BF16)]
    else:
        out_specs = [lane_spec(number, tall * cut, 0) for number in range(len(lanes))]
        out_shape = [pltpu.HBM((tall * cut, width), BF16) for width in widths]

    def kernel(*refs):
        outs, turned = refs[len(args) : -1], refs[-1]
        step = pl.program_id(0)
        for number, unit in enumerate(units):
            lane = lane_of[number]

            @pl.when(step == starts[number])
            def _():
                for place, row in enumerate(rows[lane]):
                    first = (row - side * (count // 2)) * cut
                    source = refs[left_of[number]][:, first : first + cut]
                    turned[place * cut : (place + 1) * cut, :] = source.T

            @pl.when((step >= starts[number]) & (step < starts[number] + counts[number]))
            def _():
                product = dot(turned[...], refs[len(lefts) + number][0], (1, 0))
                out = outs[0] if joint else outs[lane]
                for place in range(tall):
                    part = product[place * cut : (place + 1) * cut]
                    if away is not None:
                        part += refs[len(lefts) + len(units) + place][...].astype(F32)
                    for spot in at.get((lane, place), ()):
                        part += refs[spot][...].astype(F32)
                    out[place * cut : (place + 1) * cut, :] = part.astype(BF16)

    return pl.pallas_call(
        kernel,
        grid=(sum(counts),),
        in_specs=in_specs,
        out_specs=out_specs,
        out_shape=out_shape,
        scratch_shapes=[pltpu.VMEM((tall * cut, tokens), BF16)],
        compiler_params=vmem(
            *[((2, tokens, features), BF16)] * len(lefts),
            *[((2, tokens, block), BF16)] * len(units),
            *[((2, tall * cut, block), BF16)] * (2 + len(out_shape)),
            *[((2, cut, block), BF16)] * sum(len(pairs) * tall for pairs in came),
            ((tall * cut, block), F32),
        ),
        cost_estimate=pl.CostEstimate(
            flops=2 * tall * cut * sum(widths) * tokens,
            bytes_accessed=4 * tall * cut * sum(widths),
            transcendentals=0,
        ),
    )(*[far(value) for value in args])


class Sum:
    def __init__(self, *lanes):
        bits = high_bits()
        sides = 1 << len(bits)
        self.lanes = lanes
        self.orders = [bits if number % 2 else bits[::-1] for number in range(len(lanes))]
        self.came = [[] for _ in lanes]
        self.keep = []
        for order in self.orders:
            held, lists = list(range(sides)), []
            for bit in order:
                lists.append([mask for mask in held if mask << 1 >> bit & 1])
                held = [mask for mask in held if not mask << 1 >> bit & 1]
                lists.append(held)
            self.keep.append(lists)
        rows = [[sides + mask for mask in range(sides)]] * len(lanes)
        self.state = grad_product(lanes, rows, None, [[] for _ in lanes], True)

    def over_core(self):
        self.away = flip(self.state[0], 0)
        self.state = [self.away]
        return self

    def parts(self, which, level):
        last = level == len(self.orders[0])
        lanes, rows, came, starts = [], [], [], []
        for number in which:
            lists = self.keep[number]
            row = lists[2 * level - 1] if last else lists[2 * level]
            lanes.append(self.lanes[number])
            rows.append(row)
            came.append(
                [
                    (array, [lists[2 * step + 1].index(mask) for mask in row])
                    for step, array in enumerate(self.came[number])
                ]
            )
        widths = [sum(unit.width for unit in lane) for lane in self.lanes]
        return grad_product(lanes, rows, self.away, came, last, sum(widths[: which[0]]))

    def which(self, which):
        return list(which) or list(range(len(self.lanes)))

    def add_own(self, *which):
        which = self.which(which)
        self.ready = dict(zip(which, self.parts(which, 0)))
        self.state = [self.away, self.ready]
        return self

    def sync_from(self, state):
        self.state = state
        self.away = state[0]
        if len(state) > 1:
            self.ready = state[1]
        if len(state) > 2:
            self.came = state[2]

    def over_first(self, *which):
        for number in self.which(which):
            self.came[number] = [flip(self.ready[number], self.orders[number][0])]
        self.state = [self.away, self.ready, self.came]
        return self

    def over_rest(self, *which):
        which = self.which(which)
        for level in range(1, len(self.orders[0])):
            parts = self.parts(which, level)
            for number, part in zip(which, parts):
                self.came[number] = self.came[number] + [flip(part, self.orders[number][level])]
        self.state = [self.away, self.ready, self.came]
        return self

    def whole(self, *which):
        return self.parts(self.which(which), len(self.orders[0]))[0]


def hold(sums, *values):
    flat, tree = jax.tree.flatten(([one.state for one in sums], values))
    states, values = jax.tree.unflatten(tree, lax.optimization_barrier(flat))
    for one, state in zip(sums, states):
        one.sync_from(state)
    return values


def block_order():
    count = lax.axis_size("wide")
    here = lax.axis_index("wide")
    masks = [mask << 1 for mask in range(count // 2)]
    return [here ^ mask for mask in masks + [mask + 1 for mask in masks]]


def blocks_kernel(count, spot_ref, *refs):
    for source, target in zip(refs[: len(refs) // 2], refs[len(refs) // 2 :]):
        width = source.shape[1] // count
        for number in range(count):
            spot = pl.multiple_of(spot_ref[number] * width, PAIR)
            target[:, number * width : (number + 1) * width] = source[:, pl.ds(spot, width)]


def blocks(values, spots):
    count = len(spots)
    whole = pl.BlockSpec(memory_space=pltpu.VMEM)
    return pl.pallas_call(
        lambda *refs: blocks_kernel(count, *refs),
        in_specs=[pl.BlockSpec(memory_space=pltpu.SMEM)] + [whole] * len(values),
        out_specs=[whole] * len(values),
        out_shape=[jax.ShapeDtypeStruct(value.shape, value.dtype) for value in values],
        compiler_params=pltpu.CompilerParams(vmem_limit_bytes=2 * LIMIT),
        cost_estimate=pl.CostEstimate(flops=0, bytes_accessed=2**22, transcendentals=0),
    )(jnp.stack(spots).astype(jnp.int32), *values)


def to_own(*values):
    return blocks(values, block_order())


def from_own(*values):
    count = lax.axis_size("wide")
    here = lax.axis_index("wide")
    places = [((j ^ here) >> 1) + ((j ^ here) & 1) * (count // 2) for j in range(count)]
    return blocks(values, places)


def all_sum_chain(value):
    return [value] + [shift(value, step) for step in range(1, lax.axis_size("narrow"))]


def all_sum_cube(value):
    count = lax.axis_size("wide")

    def over(mask):
        return lax.ppermute(value, "wide", [(i, i ^ mask) for i in range(count)])

    return [value] + [over(mask << 1) for mask in range(1, count // 2)]


def shard_place():
    return lax.axis_index("wide") * lax.axis_size("narrow") + lax.axis_index("narrow")


def matmul_block(width, first):
    fits = [b for b in range(PAIR, 1537, PAIR) if width % b == 0 and first % b == 0]
    return max(fits)


def into(value, weight, first, width, kind):
    tokens, features = value.shape
    half = features // 2
    block = matmul_block(width, first)
    if block == width:
        block //= 2

    def kernel(value_ref, own_ref, other_ref, out_ref):
        product = dot(value_ref[:, :half], own_ref[...], (1, 0))
        product += dot(value_ref[:, half:], other_ref[...], (1, 0))
        out_ref[...] = product.astype(kind)

    part = pl.BlockSpec((half, block), lambda i: (0, i + first // block))
    return pl.pallas_call(
        kernel,
        grid=(width // block,),
        in_specs=[pl.BlockSpec(value.shape, lambda i: (0, 0)), part, part],
        out_specs=pl.BlockSpec((tokens, block), lambda i: (0, i)),
        out_shape=jax.ShapeDtypeStruct((tokens, width), kind),
        compiler_params=vmem(
            (value.shape, F32), ((4, half, block), BF16), ((4, tokens, block), F32)
        ),
        cost_estimate=pl.CostEstimate(
            flops=2 * tokens * features * width,
            bytes_accessed=2 * features * width,
            transcendentals=0,
        ),
    )(value, *[far(part) for part in weight])


def out_of(value, weight, first):
    planes, tokens, width = value.shape
    half = weight[0].shape[0]
    block = matmul_block(width, first)
    if block == width and planes == 1:
        block //= 2
    steps = width // block

    def kernel(value_ref, own_ref, other_ref, out_ref):
        own = dot(value_ref[0], own_ref[...], (1, 1))
        other = dot(value_ref[0], other_ref[...], (1, 1))

        @pl.when(pl.program_id(0) == 0)
        def _():
            out_ref[:, :half] = own
            out_ref[:, half:] = other

        @pl.when(pl.program_id(0) > 0)
        def _():
            out_ref[:, :half] += own
            out_ref[:, half:] += other

    part = pl.BlockSpec((half, block), lambda i: (0, i + first // block))
    return pl.pallas_call(
        kernel,
        grid=(planes * steps,),
        in_specs=[
            pl.BlockSpec((1, tokens, block), lambda i: (i // steps, 0, i % steps)),
            part,
            part,
        ],
        out_specs=pl.BlockSpec((tokens, 2 * half), lambda i: (0, 0)),
        out_shape=jax.ShapeDtypeStruct((tokens, 2 * half), F32),
        compiler_params=vmem(
            ((2, tokens, block), BF16), ((4, half, block), BF16), ((4, tokens, 2 * half), F32)
        ),
        cost_estimate=pl.CostEstimate(
            flops=4 * tokens * half * width * planes,
            bytes_accessed=4 * half * width * planes,
            transcendentals=0,
        ),
    )(value, *[far(part) for part in weight])


def feed_forward(value, weight, width):
    tokens, features = value.shape
    half = features // 2
    block = matmul_block(width, width)

    def kernel(value_ref, own_gate, other_gate, own_up, other_up, gate_ref, up_ref, act_ref):
        own, other = value_ref[:, :half], value_ref[:, half:]
        gate = dot(own, own_gate[...], (1, 0)) + dot(other, other_gate[...], (1, 0))
        up = dot(own, own_up[...], (1, 0)) + dot(other, other_up[...], (1, 0))
        gate_ref[...] = gate
        up_ref[...] = up
        act_ref[...] = gated(gate, up).astype(BF16)

    gate_part = pl.BlockSpec((half, block), lambda i: (0, i))
    up_part = pl.BlockSpec((half, block), lambda i: (0, i + width // block))
    out = pl.BlockSpec((tokens, block), lambda i: (0, i))
    return pl.pallas_call(
        kernel,
        grid=(width // block,),
        in_specs=[pl.BlockSpec(value.shape, lambda i: (0, 0))]
        + [gate_part, gate_part, up_part, up_part],
        out_specs=[out] * 3,
        out_shape=[jax.ShapeDtypeStruct((tokens, width), kind) for kind in (F32, F32, BF16)],
        compiler_params=vmem(((8, half, block), BF16), ((9, tokens, block), F32)),
        cost_estimate=pl.CostEstimate(
            flops=4 * tokens * features * width,
            bytes_accessed=4 * features * width,
            transcendentals=0,
        ),
    )(value, *[far(part) for part in (*weight, *weight)])


def feed_back(value, weight, gate, up):
    tokens, features = value.shape
    half = features // 2
    width = gate.shape[1]
    block = matmul_block(width, 0)

    def kernel(value_ref, own_ref, other_ref, gate_ref, up_ref, out_ref):
        grad = dot(value_ref[:, :half], own_ref[...], (1, 0))
        grad += dot(value_ref[:, half:], other_ref[...], (1, 0))
        dgate, dup = jax.vjp(gated, gate_ref[...], up_ref[...])[1](grad)
        out_ref[0] = dgate.astype(BF16)
        out_ref[1] = dup.astype(BF16)

    part = pl.BlockSpec((half, block), lambda i: (0, i))
    wide = pl.BlockSpec((tokens, block), lambda i: (0, i))
    return pl.pallas_call(
        kernel,
        grid=(width // block,),
        in_specs=[pl.BlockSpec(value.shape, lambda i: (0, 0)), part, part, wide, wide],
        out_specs=pl.BlockSpec((2, tokens, block), lambda i: (0, 0, i)),
        out_shape=jax.ShapeDtypeStruct((2, tokens, width), BF16),
        compiler_params=vmem(((4, half, block), BF16), ((9, tokens, block), F32)),
        cost_estimate=pl.CostEstimate(
            flops=2 * tokens * features * width,
            bytes_accessed=4 * features * width,
            transcendentals=0,
        ),
    )(value, *[far(part) for part in weight], gate, up)


def rms_norm(hidden, gain):
    return hidden * lax.rsqrt(jnp.mean(hidden * hidden, axis=-1, keepdims=True) + EPS) * gain


def gated(gate, up):
    return jax.nn.gelu(gate) * up


def advance(master, moment, trail, grad, rate):
    new_moment = 0.5 * moment + 0.5 * grad
    new_master = master - rate * (grad + 0.5 * new_moment)
    new_trail = 0.5 * trail + 0.5 * new_master
    return (new_master, new_moment, new_trail, new_master.astype(BF16))


def on_device(
    tokens,
    memory,
    dec_ids,
    enc_ids,
    cotangent,
    query_weight,
    query_moment,
    query_trail,
    keyval_weight,
    keyval_moment,
    keyval_trail,
    output_weight,
    output_moment,
    output_trail,
    inner_weight,
    inner_moment,
    inner_trail,
    outer_weight,
    outer_moment,
    outer_trail,
    norm_gains,
    gains_moment,
    gains_trail,
):
    rows, local_len, width = tokens.shape
    mem_local = memory.shape[1]
    narrow_count = lax.axis_size("narrow")
    seq_len = local_len * narrow_count
    inner_width = outer_weight.shape[0]
    q_width, kv_width = query_weight.shape[2], keyval_weight.shape[2]
    gain_count, gain_width = norm_gains.shape
    q_share, kv_share = q_width // narrow_count, kv_width // (2 * narrow_count)

    gain_cols = jnp.pad(norm_gains.astype(BF16).T, ((0, 0), (0, PAIR - gain_count)))
    shard0 = jnp.concatenate(
        [query_weight[0].astype(BF16), keyval_weight[0].astype(BF16), gain_cols], axis=1
    )
    z0 = spread_steps(shard0, near_steps() + far_steps())
    shard1 = jnp.concatenate(
        [
            output_weight[0].T.astype(BF16),
            query_weight[1].astype(BF16),
            keyval_weight[1].astype(BF16),
            output_weight[1].T.astype(BF16),
        ],
        axis=1,
    )
    tokens_own, memory_own, grad_ffn = to_own(
        tokens.reshape(local_len, width),
        memory.reshape(mem_local, width),
        cotangent.reshape(local_len, width),
    )
    z0, shard1, tokens_own, memory_own, grad_ffn = sync(
        z0, shard1, tokens_own, memory_own, grad_ffn
    )
    dec_col, dec_row = dec_ids.reshape(-1, 1), dec_ids.reshape(1, -1)
    enc_col = enc_ids.reshape(-1, 1)
    g0 = mirror_first(*spread_join(shard0, z0))
    z1 = spread_steps(shard1, near_steps())
    shard2 = inner_weight.astype(BF16)
    shard3 = outer_weight.T.astype(BF16)
    hidden = tokens_own.astype(F32)
    g0, z1, shard1, shard2, shard3 = sync(g0, z1, shard1, shard2, shard3)
    r0 = mirror_rest(g0)
    z1 |= spread_steps(shard1, far_steps())
    r0, z1 = sync(r0, z1)
    (own,) = mirror_join(g0, r0, (q_width + kv_width + PAIR,))
    w_zero = (own, flip(own, 0))
    a1, b1 = spread_join(shard1, z1, width + q_width, kv_width + width)
    a1 = mirror_first(a1)
    z2 = spread_steps(shard2, near_steps())
    w_zero, b1 = sync(w_zero, b1)
    gains = turned_gains(*w_zero, q_width + kv_width)
    normed_one = rms_norm(hidden, gains[0]).astype(BF16)
    half_kv = kv_width // 2
    made = into(normed_one, w_zero, 0, q_width + kv_width, BF16)
    pieces = cut_columns(
        [(made, 0, q_width), (made, q_width, half_kv), (made, q_width + half_kv, half_kv)]
    )
    pieces, a1, b1, shard2, z2 = sync(pieces, a1, b1, shard2, z2)
    joint_one = trade(pieces)
    b1 = mirror_first(b1)
    joint_one, b1, shard2 = sync(joint_one, b1, shard2)
    ra1, rb1 = half_rest(a1, False), half_rest(b1, True)
    z2 |= spread_steps(shard2, far_steps())
    context, stat_one = attention(joint_one, dec_col, dec_row, local_len, True)
    context, ra1, rb1, z2 = sync(context, ra1, rb1, z2)
    came = trade(context)
    w_one = half_join((a1, ra1), (b1, rb1))
    a2, b2 = spread_join(shard2, z2, inner_width, inner_width)
    a2 = mirror_first(a2)
    kv_at, o_two_at = width + q_width, width + q_width + kv_width
    keyval_two = into(memory_own, w_one, kv_at, kv_width, BF16)
    came, w_one, shard3, b2, keyval_two = sync(came, w_one, shard3, b2, keyval_two)
    context_one = join_columns(came, q_share)
    after_one = hidden + out_of(context_one[None], w_one, 0)
    normed_two = rms_norm(after_one, gains[1]).astype(BF16)
    query_two = into(normed_two, w_one, width, q_width, BF16)
    pieces = cut_columns(
        [(query_two, 0, q_width), (keyval_two, 0, half_kv), (keyval_two, half_kv, half_kv)]
    )
    a2, pieces, after_one, b2 = sync(a2, pieces, after_one, b2)
    joint_two = trade(pieces)
    b2 = mirror_first(b2)
    joint_two, b2, shard3 = sync(joint_two, b2, shard3)
    ra2, rb2 = half_rest(a2, False), half_rest(b2, True)
    z3 = spread_steps(shard3, near_steps() + far_steps())
    context, stat_two = attention(joint_two, enc_col, dec_row, local_len, False)
    context, ra2, rb2, z3, shard3 = sync(context, ra2, rb2, z3, shard3)
    came = trade(context)
    half_inner = inner_width // 2
    a3, b3 = spread_join(shard3, z3, half_inner, half_inner)
    a3 = mirror_first(a3)
    w_in = half_join((a2, ra2), (b2, rb2))
    came, w_in, a3, b3 = sync(came, w_in, a3, b3)
    b3 = mirror_first(b3)
    context_two = join_columns(came, q_share)
    after_two = after_one + out_of(context_two[None], w_one, o_two_at)
    normed_three = rms_norm(after_two, gains[2]).astype(BF16)
    b3, normed_three, after_two = sync(b3, normed_three, after_two)
    ra3, rb3 = half_rest(a3, False), half_rest(b3, True)
    gate, up, activated = feed_forward(normed_three, w_in, inner_width)
    ra3, rb3, gate, up, activated = sync(ra3, rb3, gate, up, activated)
    w_out = half_join((a3, ra3), (b3, rb3))
    sum_outs = Sum(
        [Unit(grad_ffn, activated[None], 0, 0, half_inner)],
        [Unit(grad_ffn, activated[None], 0, half_inner, half_inner)],
    )
    w_out, activated = hold([sum_outs], w_out, activated)
    sum_outs.over_core()
    grad_inner = feed_back(grad_ffn, w_out, gate, up)
    (grad_inner,) = hold([sum_outs], grad_inner)
    sum_outs.add_own()
    sum_ins = Sum(
        [Unit(normed_three, grad_inner, 0, 0, half_inner)],
        [Unit(normed_three, grad_inner, 0, half_inner, half_inner)],
        [Unit(normed_three, grad_inner, 1, 0, half_inner)],
        [Unit(normed_three, grad_inner, 1, half_inner, half_inner)],
    )
    (grad_inner,) = hold([sum_outs, sum_ins], grad_inner)
    sum_outs.over_first()
    sum_ins.over_core()
    grad_normed = out_of(grad_inner, w_in, 0)
    grad_hidden, grad_gain_three = jax.vjp(rms_norm, after_two, gains[2])[1](grad_normed)
    grad_two = grad_ffn.astype(F32) + grad_hidden
    grad_branch = grad_two.astype(BF16)
    pieces = cut_columns([(into(grad_branch, w_one, o_two_at, width, BF16), 0, width)])
    pieces, grad_branch_two = hold([sum_ins, sum_outs], pieces, grad_branch)
    grad_context = trade(pieces)
    sum_outs.over_rest()
    sum_ins.add_own()
    outer_whole = sum_outs.whole()
    grad_context, outer_whole = hold([sum_ins], grad_context, outer_whole)
    sum_ins.over_first(0, 1)
    outer_parts = trade(outer_whole)
    dquery, dkeyval = attention_back(
        joint_two, grad_context, stat_two, enc_col, dec_row, local_len, False
    )
    dquery, dkeyval, activated, outer_parts = hold(
        [sum_ins], dquery, dkeyval, activated, outer_parts
    )
    came = trade(dquery)
    sum_ins.over_first(2, 3)
    result = after_two + out_of(activated[None], w_out, 0)
    (block_out,) = from_own(result.astype(BF16))
    came, dkeyval, block_out = hold([sum_ins], came, dkeyval, block_out)
    came_too = trade(dkeyval)
    sum_ins.over_rest()
    query_grad_two = join_columns(came, q_share)
    grad_normed_two = out_of(query_grad_two[None], w_one, width)
    grad_hidden, grad_gain_two = jax.vjp(rms_norm, after_one, gains[1])[1](grad_normed_two)
    grad_one = grad_two + grad_hidden
    grad_branch = grad_one.astype(BF16)
    pieces = cut_columns([(into(grad_branch, w_one, 0, width, BF16), 0, width)])
    pieces, grad_branch, came_too = hold([sum_ins], pieces, grad_branch, came_too)
    grad_context = trade(pieces)
    gate_whole = sum_ins.whole(0, 1)
    keyval_grad_two = join_columns(came_too, kv_share, 2)
    sum_mid = Sum(
        [
            Unit(grad_branch_two, context_two[None], 0, 0, width),
            Unit(memory_own, keyval_grad_two[None], 0, 0, kv_width),
        ],
        [
            Unit(normed_two, query_grad_two[None], 0, 0, q_width),
            Unit(grad_branch, context_one[None], 0, 0, width),
        ],
    )
    grad_context, keyval_grad_two, gate_whole = hold(
        [sum_mid, sum_ins], grad_context, keyval_grad_two, gate_whole
    )
    sum_mid.over_core()
    gate_parts = trade(gate_whole)
    dquery, dkeyval = attention_back(
        joint_one, grad_context, stat_one, dec_col, dec_row, local_len, True
    )
    sum_mid.add_own()
    dquery, dkeyval, keyval_grad_two, outer_parts, gate_parts = hold(
        [sum_mid], dquery, dkeyval, keyval_grad_two, outer_parts, gate_parts
    )
    came = trade(dquery)
    sum_mid.over_first()
    (memory_grad,) = from_own(out_of(keyval_grad_two[None], w_one, kv_at))
    sum_outer = total(outer_parts).T
    up_whole = sum_ins.whole(2, 3)
    came, sum_outer, memory_grad, dkeyval, up_whole = hold(
        [sum_mid], came, sum_outer, memory_grad, dkeyval, up_whole
    )
    came_too = trade(dkeyval)
    sum_mid.over_rest()
    query_grad_one = join_columns(came, q_share)
    grad_normed_one = out_of(query_grad_one[None], w_zero, 0)
    came_too, grad_normed_one = hold([sum_mid], came_too, grad_normed_one)
    keyval_grad_one = join_columns(came_too, kv_share, 2)
    sum_last = Sum(
        [Unit(normed_one, query_grad_one[None], 0, 0, q_width)],
        [Unit(normed_one, keyval_grad_one[None], 0, 0, kv_width)],
    )
    up_parts = trade(up_whole)
    mid_whole = sum_mid.whole()
    keyval_grad_one, mid_whole = hold([sum_last], keyval_grad_one, mid_whole)
    sum_last.over_core()
    mid_parts = trade(mid_whole)
    (keyval_grad_one,) = hold([sum_last], keyval_grad_one)
    sum_last.add_own()
    (keyval_grad_one,) = hold([sum_last], keyval_grad_one)
    sum_last.over_first()
    grad_normed_one += out_of(keyval_grad_one[None], w_zero, q_width)
    grad_hidden, grad_gain_one = jax.vjp(rms_norm, hidden, gains[0])[1](grad_normed_one)
    input_grad, full_gains = from_own(
        grad_one + grad_hidden,
    ) + from_own(jnp.stack([grad_gain_one, grad_gain_two, grad_gain_three]))
    input_grad, full_gains = hold([sum_last], input_grad, full_gains)
    sum_last.over_rest()
    gain_parts = all_sum_cube(full_gains)
    sum_inner = jnp.concatenate([total(gate_parts), total(up_parts)], axis=1)
    gain_parts, mid_parts = hold([sum_last], gain_parts, mid_parts)
    sum_two = total(mid_parts)
    last_parts = trade(sum_last.whole())
    part = sum(gain_parts)
    full_gains = sum(all_sum_chain(part + flip(part, 0)))
    sum_gains = lax.dynamic_slice_in_dim(full_gains, shard_place() * gain_width, gain_width, 1)
    sum_one = total(last_parts)
    after_kv, after_q = width + kv_width, width + kv_width + q_width
    sum_query = jnp.stack([sum_one[:, :q_width], sum_two[:, after_kv:after_q]])
    sum_keyval = jnp.stack([sum_one[:, q_width:], sum_two[:, width:after_kv]])
    sum_output = jnp.stack([sum_two[:, after_q:], sum_two[:, :width]]).transpose(0, 2, 1)
    block_out = block_out.reshape(rows, local_len, width)
    input_grad = input_grad.reshape(rows, local_len, width)
    memory_grad = memory_grad.reshape(rows, mem_local, width)
    token_total = rows * lax.axis_size("wide") * seq_len
    rate = RATE / math.sqrt(token_total)
    output_rate = OUTPUT_RATE / math.sqrt(token_total)
    new_query = advance(query_weight, query_moment, query_trail, sum_query, rate)
    new_keyval = advance(keyval_weight, keyval_moment, keyval_trail, sum_keyval, rate)
    new_output = advance(output_weight, output_moment, output_trail, sum_output, output_rate)
    new_inner = advance(inner_weight, inner_moment, inner_trail, sum_inner, rate)
    new_outer = advance(outer_weight, outer_moment, outer_trail, sum_outer, rate)
    new_gains = advance(norm_gains, gains_moment, gains_trail, sum_gains, rate)
    return (
        block_out,
        input_grad,
        memory_grad,
        new_query[0],
        new_query[1],
        new_query[2],
        new_query[3],
        new_keyval[0],
        new_keyval[1],
        new_keyval[2],
        new_keyval[3],
        new_output[0],
        new_output[1],
        new_output[2],
        new_output[3],
        new_inner[0],
        new_inner[1],
        new_inner[2],
        new_inner[3],
        new_outer[0],
        new_outer[1],
        new_outer[2],
        new_outer[3],
        new_gains[0],
        new_gains[1],
        new_gains[2],
        new_gains[3],
    )


def solution(mesh):
    in_specs = (
        P("wide", "narrow", None),
        P("wide", "narrow", None),
        P("wide", None),
        P("wide", None),
        P("wide", "narrow", None),
        P(None, ("wide", "narrow"), None),
        P(None, ("wide", "narrow"), None),
        P(None, ("wide", "narrow"), None),
        P(None, ("wide", "narrow"), None),
        P(None, ("wide", "narrow"), None),
        P(None, ("wide", "narrow"), None),
        P(None, None, ("wide", "narrow")),
        P(None, None, ("wide", "narrow")),
        P(None, None, ("wide", "narrow")),
        P(("wide", "narrow"), None),
        P(("wide", "narrow"), None),
        P(("wide", "narrow"), None),
        P(None, ("wide", "narrow")),
        P(None, ("wide", "narrow")),
        P(None, ("wide", "narrow")),
        P(None, ("wide", "narrow")),
        P(None, ("wide", "narrow")),
        P(None, ("wide", "narrow")),
    )
    out_specs = (
        P("wide", "narrow", None),
        P("wide", "narrow", None),
        P("wide", "narrow", None),
        P(None, ("wide", "narrow"), None),
        P(None, ("wide", "narrow"), None),
        P(None, ("wide", "narrow"), None),
        P(None, ("wide", "narrow"), None),
        P(None, ("wide", "narrow"), None),
        P(None, ("wide", "narrow"), None),
        P(None, ("wide", "narrow"), None),
        P(None, ("wide", "narrow"), None),
        P(None, None, ("wide", "narrow")),
        P(None, None, ("wide", "narrow")),
        P(None, None, ("wide", "narrow")),
        P(None, None, ("wide", "narrow")),
        P(("wide", "narrow"), None),
        P(("wide", "narrow"), None),
        P(("wide", "narrow"), None),
        P(("wide", "narrow"), None),
        P(None, ("wide", "narrow")),
        P(None, ("wide", "narrow")),
        P(None, ("wide", "narrow")),
        P(None, ("wide", "narrow")),
        P(None, ("wide", "narrow")),
        P(None, ("wide", "narrow")),
        P(None, ("wide", "narrow")),
        P(None, ("wide", "narrow")),
    )
    return jax.shard_map(
        on_device, mesh=mesh, in_specs=in_specs, out_specs=out_specs, check_vma=False
    )
```

```python
import math

import jax
import jax.numpy as jnp
from jax import lax
from jax.experimental import pallas as pl
from jax.experimental.pallas import tpu as pltpu
from jax.sharding import PartitionSpec as P

HDIM = 64
PAIR = 2 * HDIM
EPS = 1e-06
NEG = -1e30
RATE = 0.02
OUTPUT_RATE = 0.15
LIMIT = 10 * 2**20
BF16 = jnp.bfloat16
F32 = jnp.float32


def dot(left, right, sides):
    return lax.dot_general(
        left, right, (((sides[0],), (sides[1],)), ((), ())), preferred_element_type=F32
    )


def matmul(left, right):
    return dot(left, right, (1, 0))


def matmul_right(left, right):
    return dot(left, right, (1, 1))


def matmul_left(left, right):
    return dot(left, right, (0, 0))


def in_group(block, group):
    low = lax.broadcasted_iota(jnp.int32, block.shape, 1) < HDIM
    turned = jnp.concatenate([block[:, HDIM:], block[:, :HDIM]], axis=1)
    zero = jnp.zeros_like(block)
    if group == 0:
        return jnp.where(low, block, zero), jnp.where(low, turned, zero)
    return jnp.where(low, zero, turned), jnp.where(low, zero, block)


def allowed(kid_ref, qid_ref, bias_ref, span, order):
    keep = kid_ref[:span] == qid_ref[...]
    if order:
        count = qid_ref.shape[1]
        keys = lax.broadcasted_iota(jnp.int32, keep.shape, 0)
        queries = lax.broadcasted_iota(jnp.int32, keep.shape, 1) + pl.program_id(0) * count
        keep &= keys <= queries
    bias_ref[:span] = jnp.where(keep, 0.0, NEG).astype(F32)


def by_span(order, count, full, body):
    if not order:
        body(full)
        return
    for number in range(full // count):
        pl.when(pl.program_id(0) == number)(lambda number=number: body((number + 1) * count))


def forward_kernel(order, query_ref, key_ref, value_ref, kid_ref, qid_ref, *rest):
    out_ref, stat_ref, bias_ref = rest
    count, width = query_ref.shape

    def body(span):
        allowed(kid_ref, qid_ref, bias_ref, span, order)
        keys = key_ref[:span]
        values = value_ref[:span].T
        for group in range(width // PAIR):
            columns = slice(group * PAIR, (group + 1) * PAIR)
            rows = slice(group * HDIM, (group + 1) * HDIM)
            block = query_ref[:, columns] * jnp.asarray(HDIM**-0.5, BF16)
            parts = []
            for side, query in enumerate(in_group(block, group)):
                logits = dot(keys, query, (1, 1)) + bias_ref[:span]
                peak = jnp.max(logits, axis=0, keepdims=True)
                weights = jnp.exp(logits - peak)
                total = jnp.sum(weights, axis=0, keepdims=True)
                probs = (weights * (1.0 / total)).astype(BF16)
                parts.append(dot(values, probs, (1, 0))[rows])
                stat_ref[0, pl.ds(2 * group + side, 1), :] = peak + jnp.log(total)
            out_ref[:, columns] = jnp.concatenate(parts, axis=0).T.astype(BF16)

    by_span(order, count, key_ref.shape[0], body)


def backward_kernel(
    order, query_ref, key_ref, value_ref, kid_ref, qid_ref, grad_ref, stat_ref, *rest
):
    dquery_ref, dkeyval_ref, bias_ref, key_sum, value_sum = rest
    count, width = query_ref.shape

    @pl.when(pl.program_id(0) == 0)
    def _():
        key_sum[...] = jnp.zeros_like(key_sum)
        value_sum[...] = jnp.zeros_like(value_sum)

    def body(span):
        allowed(kid_ref, qid_ref, bias_ref, span, order)
        keys = key_ref[:span]
        values = value_ref[:span]
        keys_turned = keys.T
        dkey, dvalue = None, None
        for group in range(width // PAIR):
            columns = slice(group * PAIR, (group + 1) * PAIR)
            rows = slice(group * HDIM, (group + 1) * HDIM)
            queries = in_group(query_ref[:, columns] * jnp.asarray(HDIM**-0.5, BF16), group)
            grads = in_group(grad_ref[:, columns], group)
            parts = []
            for side in range(2):
                logits = dot(keys, queries[side], (1, 1)) + bias_ref[:span]
                probs = jnp.exp(logits - stat_ref[0, pl.ds(2 * group + side, 1), :])
                dprobs = dot(values, grads[side], (1, 1))
                dots = jnp.sum(probs * dprobs, axis=0, keepdims=True)
                dlogits = (probs * (dprobs - dots)).astype(BF16)
                parts.append(dot(keys_turned, dlogits, (1, 0))[rows])
                more_key = dot(dlogits, queries[side], (1, 0))
                more_value = dot(probs.astype(BF16), grads[side], (1, 0))
                dkey = more_key if dkey is None else dkey + more_key
                dvalue = more_value if dvalue is None else dvalue + more_value
            dquery_ref[:, columns] = (jnp.concatenate(parts, axis=0).T * HDIM**-0.5).astype(BF16)
        key_sum[:span] += dkey
        value_sum[:span] += dvalue

    by_span(order, count, key_ref.shape[0], body)

    @pl.when(pl.program_id(0) == pl.num_programs(0) - 1)
    def _():
        dkeyval_ref[:, :PAIR] = key_sum[...].astype(BF16)
        dkeyval_ref[:, PAIR:] = value_sum[...].astype(BF16)


def attention_specs(joint, count):
    span, width = joint.shape
    q_width = width - 2 * PAIR
    query = pl.BlockSpec((count, q_width), lambda i: (i, 0))
    keys = pl.BlockSpec((span, PAIR), lambda i: (0, q_width // PAIR))
    values = pl.BlockSpec((span, PAIR), lambda i: (0, q_width // PAIR + 1))
    key_ids = pl.BlockSpec((span, 1), lambda i: (0, 0))
    query_ids = pl.BlockSpec((1, count), lambda i: (0, i))
    stat = pl.BlockSpec((1, 8, count), lambda i: (i, 0, 0))
    return q_width, [query, keys, values, key_ids, query_ids], stat


def attention(joint, key_ids, query_ids, count, order):
    span = joint.shape[0]
    q_width, specs, s_spec = attention_specs(joint, count)
    return pl.pallas_call(
        lambda *refs: forward_kernel(order, *refs),
        grid=(span // count,),
        in_specs=specs,
        out_specs=[specs[0], s_spec],
        out_shape=[
            jax.ShapeDtypeStruct((span, q_width), BF16),
            jax.ShapeDtypeStruct((span // count, 8, count), F32),
        ],
        scratch_shapes=[pltpu.VMEM((span, count), F32)],
        compiler_params=pltpu.CompilerParams(vmem_limit_bytes=24 * 2**20),
        cost_estimate=pl.CostEstimate(
            flops=4 * span * span * q_width, bytes_accessed=8 * span * q_width, transcendentals=0
        ),
    )(joint, joint, joint, key_ids, query_ids)


def attention_back(joint, grad, stat, key_ids, query_ids, count, order):
    span = joint.shape[0]
    q_width, specs, s_spec = attention_specs(joint, count)
    whole = pl.BlockSpec((span, 2 * PAIR), lambda i: (0, 0))
    return pl.pallas_call(
        lambda *refs: backward_kernel(order, *refs),
        grid=(span // count,),
        in_specs=specs + [specs[0], s_spec],
        out_specs=[specs[0], whole],
        out_shape=[
            jax.ShapeDtypeStruct((span, q_width), BF16),
            jax.ShapeDtypeStruct((span, 2 * PAIR), BF16),
        ],
        scratch_shapes=[
            pltpu.VMEM((span, count), F32),
            pltpu.VMEM((span, PAIR), F32),
            pltpu.VMEM((span, PAIR), F32),
        ],
        compiler_params=pltpu.CompilerParams(vmem_limit_bytes=24 * 2**20),
        cost_estimate=pl.CostEstimate(
            flops=10 * span * span * q_width, bytes_accessed=16 * span * q_width, transcendentals=0
        ),
    )(joint, joint, joint, key_ids, query_ids, grad, stat)


def flip(value, bit):
    count = lax.axis_size("wide")
    return lax.ppermute(value, "wide", [(i, i ^ (1 << bit)) for i in range(count)])


def shift(value, step):
    count = lax.axis_size("narrow")
    return lax.ppermute(value, "narrow", [(i, (i + step) % count) for i in range(count)])


def sync(*values):
    return lax.optimization_barrier(values)


def place(pieces, widths):
    rows = pieces[0][0].shape[0]
    count = 1 + max(number for _, number, _ in pieces)

    def kernel(*refs):
        first = 0
        for target, cut in zip(refs[len(pieces) :], widths):
            for source, (piece, number, begin) in zip(refs, pieces):
                low, high = max(begin, first), min(begin + piece.shape[1], first + cut)
                if low < high:
                    target[number * rows : (number + 1) * rows, low - first : high - first] = source[
                        :, low - begin : high - begin
                    ]
            first += cut

    shapes = [jax.ShapeDtypeStruct((count * rows, cut), BF16) for cut in widths]
    return small_call(kernel, shapes, [piece for piece, _, _ in pieces])


def far(value):
    return pltpu.with_memory_space_constraint(value, pltpu.HBM)


def trade(value):
    return lax.all_to_all(value, "narrow", 0, 0, tiled=True)


def spread(value):
    count = lax.axis_size("narrow")
    return trade(jnp.concatenate([value] * count, axis=0))


def near_steps():
    return sorted({1, lax.axis_size("narrow") - 1})


def far_steps():
    return [s for s in range(1, lax.axis_size("narrow")) if s not in near_steps()]


def spread_steps(value, steps):
    return {step: shift(value, step) for step in steps}


def spread_join(value, came, *widths):
    count = lax.axis_size("narrow")
    pieces = [value] + [came[step] for step in sorted(came)]
    rows, width = value.shape
    widths = widths or (width,)
    firsts = [sum(widths[:number]) for number in range(len(widths))]
    spots = (lax.axis_index("narrow") - jnp.arange(count, dtype=jnp.int32)) % count
    if rows % 16:
        whole = jnp.zeros((count, rows, width), value.dtype)
        for number, piece in enumerate(pieces):
            whole = lax.dynamic_update_index_in_dim(whole, piece, spots[number], 0)
        whole = whole.reshape(count * rows, width)
        return [whole[:, first : first + wide] for first, wide in zip(firsts, widths)]

    def kernel(spot_ref, *refs):
        for number, source in enumerate(refs[:count]):
            spot = pl.multiple_of(spot_ref[number] * rows, rows)
            for target, first, wide in zip(refs[count:], firsts, widths):
                target[pl.ds(spot, rows), :] = source[:, first : first + wide]

    whole = pl.BlockSpec(memory_space=pltpu.VMEM)
    return pl.pallas_call(
        kernel,
        in_specs=[pl.BlockSpec(memory_space=pltpu.SMEM)] + [whole] * count,
        out_specs=[whole] * len(widths),
        out_shape=[jax.ShapeDtypeStruct((count * rows, wide), value.dtype) for wide in widths],
        compiler_params=pltpu.CompilerParams(vmem_limit_bytes=16 * 2**20),
        cost_estimate=pl.CostEstimate(flops=0, bytes_accessed=2**22, transcendentals=0),
    )(spots, *pieces)


def tight(width):
    return -(-width // PAIR) * PAIR


def cut_columns(parts):
    count = lax.axis_size("narrow")
    rows = parts[0][0].shape[0]
    shares = [wide // count for _, _, wide in parts]
    width = sum(tight(share) for share in shares)
    arrays = list({id(part): part for part, _, _ in parts}.values())
    index = [[part is array for array in arrays].index(True) for part, _, _ in parts]

    def kernel(*refs):
        target = refs[-1]
        for number in range(count):
            first = 0
            for (_, begin, _), source, share in zip(parts, index, shares):
                low = begin + number * share
                block = refs[source][:, low : low + share]
                if share % PAIR:
                    zeros = jnp.zeros((rows, tight(share) - share), BF16)
                    block = jnp.concatenate([block, zeros], axis=1)
                target[number * rows : (number + 1) * rows, first : first + tight(share)] = block
                first += tight(share)

    return small_call(kernel, [jax.ShapeDtypeStruct((count * rows, width), BF16)], arrays)[0]


def join_columns(value, share, kinds=1):
    count = lax.axis_size("narrow")
    rows = value.shape[0] // count

    def kernel(source, target):
        for kind in range(kinds):
            for number in range(count):
                place = (kind * count + number) * share
                target[:, place : place + share] = source[
                    number * rows : (number + 1) * rows,
                    kind * tight(share) : kind * tight(share) + share,
                ]

    shape = jax.ShapeDtypeStruct((rows, kinds * share * count), BF16)
    return small_call(kernel, [shape], (value,))[0]


def vmem(*arrays):
    size = sum(math.prod(shape) * jnp.dtype(kind).itemsize for shape, kind in arrays)
    return pltpu.CompilerParams(vmem_limit_bytes=min(56 * 2**20, max(LIMIT, size + LIMIT)))


def small_call(kernel, out_shape, args):
    whole = pl.BlockSpec(memory_space=pltpu.VMEM)
    return pl.pallas_call(
        kernel,
        in_specs=[whole] * len(args),
        out_specs=[whole] * len(out_shape),
        out_shape=out_shape,
        compiler_params=vmem(*[(v.shape, v.dtype) for v in (*args, *out_shape)]),
        cost_estimate=pl.CostEstimate(flops=0, bytes_accessed=2**22, transcendentals=0),
    )(*args)


def total(value):
    count = lax.axis_size("narrow")
    return jnp.sum(value.reshape((count, -1) + value.shape[1:]).astype(F32), axis=0)


def high_bits():
    return list(range(1, lax.axis_size("wide").bit_length() - 1))


def mirror_first(value):
    return {0: value} | {1 << bit: flip(value, bit) for bit in high_bits()}


def mirror_rest(known):
    bits = high_bits()
    width = known[0].shape[1]
    middle = width // (2 * PAIR) * PAIR
    came = {}
    for order, low, high in ((bits, 0, middle), (bits[::-1], middle, width)):
        have = {0: known[0][:, low:high]}
        for bit in order:
            have |= {
                mask ^ (1 << bit): known[1 << bit][:, low:high] if mask == 0 else flip(part, bit)
                for mask, part in have.items()
            }
        came |= {(mask, low): part for mask, part in have.items() if mask not in known}
    return came


def half_rest(known, turned):
    order = high_bits()[::-1] if turned else high_bits()
    have = {0: known[0]}
    for bit in order:
        have |= {
            mask ^ (1 << bit): known[1 << bit] if mask == 0 else flip(part, bit)
            for mask, part in have.items()
        }
    return {mask: part for mask, part in have.items() if mask not in known}


def half_join(*halves):
    pieces, first = [], 0
    for known, came in halves:
        pieces += [(value, mask >> 1, first) for mask, value in (known | came).items()]
        first += known[0].shape[1]
    (own,) = place(pieces, (first,))
    return own, flip(own, 0)


def mirror_join(known, came, widths):
    pieces = [(value, mask >> 1, 0) for mask, value in known.items()]
    pieces += [(value, mask >> 1, low) for (mask, low), value in came.items()]
    return place(pieces, widths)


def turned_gains(own, other, first):
    def kernel(own_ref, other_ref, out_ref):
        half = own_ref.shape[0]
        for number, source in enumerate((own_ref, other_ref)):
            out_ref[:, number * half : (number + 1) * half] = source[...].astype(F32).T[:8]

    part = pl.BlockSpec((own.shape[0], PAIR), lambda i: (0, first // PAIR))
    return pl.pallas_call(
        kernel,
        grid=(1,),
        in_specs=[part, part],
        out_specs=pl.BlockSpec((8, 2 * own.shape[0]), lambda i: (0, 0)),
        out_shape=jax.ShapeDtypeStruct((8, 2 * own.shape[0]), F32),
    )(far(own), far(other))


def column_block(width):
    return max(b for b in range(PAIR, 1537, PAIR) if width % b == 0)


class Unit:
    def __init__(self, left, right, plane, first, width):
        self.left, self.right, self.plane, self.first, self.width = left, right, plane, first, width


def by_step(starts, values, step):
    found = values[0]
    for start, value in zip(starts[1:], values[1:]):
        found = jnp.where(step >= start, value, found)
    return found


def grad_product(lanes, rows, away, came, joint, begin=0):
    units = [unit for lane in lanes for unit in lane]
    lane_of = [number for number, lane in enumerate(lanes) for _ in lane]
    tokens, features = units[0].left.shape
    count = lax.axis_size("wide")
    cut, tall = features // count, len(rows[0])
    block = min(column_block(unit.width) for unit in units)
    counts = [unit.width // block for unit in units]
    starts = [sum(counts[:number]) for number in range(len(units))]
    lane_starts = [starts[lane_of.index(number)] for number in range(len(lanes))]
    lane_counts = [sum(unit.width for unit in lane) // block for lane in lanes]
    lefts = list({id(unit.left): unit.left for unit in units}.values())
    left_of = [[left is unit.left for left in lefts].index(True) for unit in units]

    def unit_spec(number, unit):
        return pl.BlockSpec(
            (1, tokens, block),
            lambda i: (
                unit.plane,
                0,
                jnp.clip(i - starts[number], 0, counts[number] - 1) + unit.first // block,
            ),
        )

    def away_spec(place):
        return pl.BlockSpec(
            (cut, block),
            lambda i: (by_step(lane_starts, [row[place] for row in rows], i), i + begin // block),
        )

    def lane_spec(number, height, row):
        return pl.BlockSpec(
            (height, block),
            lambda i: (row, jnp.clip(i - lane_starts[number], 0, lane_counts[number] - 1)),
        )

    side = 0 if rows[0][0] < count // 2 else 1
    in_specs = [pl.BlockSpec((tokens, features // 2), lambda i: (0, side)) for _ in lefts]
    in_specs += [unit_spec(number, unit) for number, unit in enumerate(units)]
    args = lefts + [unit.right for unit in units]
    if away is not None:
        in_specs += [away_spec(place) for place in range(tall)]
        args += [away] * tall
    at = {}
    for number, pairs in enumerate(came):
        for place in range(tall):
            at[number, place] = []
            for array, row_blocks in pairs:
                at[number, place].append(len(args))
                in_specs.append(lane_spec(number, cut, row_blocks[place]))
                args.append(array)
    widths = [sum(unit.width for unit in lane) for lane in lanes]
    if joint:
        out_specs = [pl.BlockSpec((tall * cut, block), lambda i: (0, i))]
        out_shape = [pltpu.HBM((tall * cut, sum(widths)), BF16)]
    else:
        out_specs = [lane_spec(number, tall * cut, 0) for number in range(len(lanes))]
        out_shape = [pltpu.HBM((tall * cut, width), BF16) for width in widths]

    def kernel(*refs):
        outs, turned = refs[len(args) : -1], refs[-1]
        step = pl.program_id(0)
        for number, unit in enumerate(units):
            lane = lane_of[number]

            @pl.when(step == starts[number])
            def _():
                for place, row in enumerate(rows[lane]):
                    first = (row - side * (count // 2)) * cut
                    source = refs[left_of[number]][:, first : first + cut]
                    turned[place * cut : (place + 1) * cut, :] = source.T

            @pl.when((step >= starts[number]) & (step < starts[number] + counts[number]))
            def _():
                product = dot(turned[...], refs[len(lefts) + number][0], (1, 0))
                out = outs[0] if joint else outs[lane]
                for place in range(tall):
                    part = product[place * cut : (place + 1) * cut]
                    if away is not None:
                        part += refs[len(lefts) + len(units) + place][...].astype(F32)
                    for spot in at.get((lane, place), ()):
                        part += refs[spot][...].astype(F32)
                    out[place * cut : (place + 1) * cut, :] = part.astype(BF16)

    return pl.pallas_call(
        kernel,
        grid=(sum(counts),),
        in_specs=in_specs,
        out_specs=out_specs,
        out_shape=out_shape,
        scratch_shapes=[pltpu.VMEM((tall * cut, tokens), BF16)],
        compiler_params=vmem(
            *[((2, tokens, features), BF16)] * len(lefts),
            *[((2, tokens, block), BF16)] * len(units),
            *[((2, tall * cut, block), BF16)] * (2 + len(out_shape)),
            *[((2, cut, block), BF16)] * sum(len(pairs) * tall for pairs in came),
            ((tall * cut, block), F32),
        ),
        cost_estimate=pl.CostEstimate(
            flops=2 * tall * cut * sum(widths) * tokens,
            bytes_accessed=4 * tall * cut * sum(widths),
            transcendentals=0,
        ),
    )(*[far(value) for value in args])


class Sum:
    def __init__(self, *lanes):
        bits = high_bits()
        sides = 1 << len(bits)
        self.lanes = lanes
        self.orders = [bits if number % 2 else bits[::-1] for number in range(len(lanes))]
        self.came = [[] for _ in lanes]
        self.keep = []
        for order in self.orders:
            held, lists = list(range(sides)), []
            for bit in order:
                lists.append([mask for mask in held if mask << 1 >> bit & 1])
                held = [mask for mask in held if not mask << 1 >> bit & 1]
                lists.append(held)
            self.keep.append(lists)
        rows = [[sides + mask for mask in range(sides)]] * len(lanes)
        self.state = grad_product(lanes, rows, None, [[] for _ in lanes], True)

    def over_core(self):
        self.away = flip(self.state[0], 0)
        self.state = [self.away]
        return self

    def parts(self, which, level):
        last = level == len(self.orders[0])
        lanes, rows, came, starts = [], [], [], []
        for number in which:
            lists = self.keep[number]
            row = lists[2 * level - 1] if last else lists[2 * level]
            lanes.append(self.lanes[number])
            rows.append(row)
            came.append(
                [
                    (array, [lists[2 * step + 1].index(mask) for mask in row])
                    for step, array in enumerate(self.came[number])
                ]
            )
        widths = [sum(unit.width for unit in lane) for lane in self.lanes]
        return grad_product(lanes, rows, self.away, came, last, sum(widths[: which[0]]))

    def which(self, which):
        return list(which) or list(range(len(self.lanes)))

    def add_own(self, *which):
        which = self.which(which)
        self.ready = dict(zip(which, self.parts(which, 0)))
        self.state = [self.away, self.ready]
        return self

    def sync_from(self, state):
        self.state = state
        self.away = state[0]
        if len(state) > 1:
            self.ready = state[1]
        if len(state) > 2:
            self.came = state[2]

    def over_first(self, *which):
        for number in self.which(which):
            self.came[number] = [flip(self.ready[number], self.orders[number][0])]
        self.state = [self.away, self.ready, self.came]
        return self

    def over_rest(self, *which):
        which = self.which(which)
        for level in range(1, len(self.orders[0])):
            parts = self.parts(which, level)
            for number, part in zip(which, parts):
                self.came[number] = self.came[number] + [flip(part, self.orders[number][level])]
        self.state = [self.away, self.ready, self.came]
        return self

    def whole(self, *which):
        return self.parts(self.which(which), len(self.orders[0]))[0]


def hold(sums, *values):
    flat, tree = jax.tree.flatten(([one.state for one in sums], values))
    states, values = jax.tree.unflatten(tree, lax.optimization_barrier(flat))
    for one, state in zip(sums, states):
        one.sync_from(state)
    return values


def block_order():
    count = lax.axis_size("wide")
    here = lax.axis_index("wide")
    masks = [mask << 1 for mask in range(count // 2)]
    return [here ^ mask for mask in masks + [mask + 1 for mask in masks]]


def blocks_kernel(count, spot_ref, *refs):
    for source, target in zip(refs[: len(refs) // 2], refs[len(refs) // 2 :]):
        width = source.shape[1] // count
        for number in range(count):
            spot = pl.multiple_of(spot_ref[number] * width, PAIR)
            target[:, number * width : (number + 1) * width] = source[:, pl.ds(spot, width)]


def blocks(values, spots):
    count = len(spots)
    whole = pl.BlockSpec(memory_space=pltpu.VMEM)
    return pl.pallas_call(
        lambda *refs: blocks_kernel(count, *refs),
        in_specs=[pl.BlockSpec(memory_space=pltpu.SMEM)] + [whole] * len(values),
        out_specs=[whole] * len(values),
        out_shape=[jax.ShapeDtypeStruct(value.shape, value.dtype) for value in values],
        compiler_params=pltpu.CompilerParams(vmem_limit_bytes=24 * 2**20),
        cost_estimate=pl.CostEstimate(flops=0, bytes_accessed=2**22, transcendentals=0),
    )(jnp.stack(spots).astype(jnp.int32), *values)


def to_own(*values):
    return blocks(values, block_order())


def from_own(*values):
    count = lax.axis_size("wide")
    here = lax.axis_index("wide")
    places = [((j ^ here) >> 1) + ((j ^ here) & 1) * (count // 2) for j in range(count)]
    return blocks(values, places)


def all_sum_chain(value):
    return [value] + [shift(value, step) for step in range(1, lax.axis_size("narrow"))]


def all_sum_cube(value):
    count = lax.axis_size("wide")

    def over(mask):
        return lax.ppermute(value, "wide", [(i, i ^ mask) for i in range(count)])

    return [value] + [over(mask << 1) for mask in range(1, count // 2)]


def shard_place():
    return lax.axis_index("wide") * lax.axis_size("narrow") + lax.axis_index("narrow")


def matmul_block(width, first):
    fits = [b for b in range(PAIR, 1537, PAIR) if width % b == 0 and first % b == 0]
    return max(fits)


def into(value, weight, first, width, kind):
    tokens, features = value.shape
    half = features // 2
    block = matmul_block(width, first)
    if block == width:
        block //= 2

    def kernel(value_ref, own_ref, other_ref, out_ref):
        product = dot(value_ref[:, :half], own_ref[...], (1, 0))
        product += dot(value_ref[:, half:], other_ref[...], (1, 0))
        out_ref[...] = product.astype(kind)

    part = pl.BlockSpec((half, block), lambda i: (0, i + first // block))
    return pl.pallas_call(
        kernel,
        grid=(width // block,),
        in_specs=[pl.BlockSpec(value.shape, lambda i: (0, 0)), part, part],
        out_specs=pl.BlockSpec((tokens, block), lambda i: (0, i)),
        out_shape=jax.ShapeDtypeStruct((tokens, width), kind),
        compiler_params=vmem(
            (value.shape, F32), ((4, half, block), BF16), ((4, tokens, block), F32)
        ),
        cost_estimate=pl.CostEstimate(
            flops=2 * tokens * features * width,
            bytes_accessed=2 * features * width,
            transcendentals=0,
        ),
    )(value, *[far(part) for part in weight])


def out_of(value, weight, first):
    planes, tokens, width = value.shape
    half = weight[0].shape[0]
    block = matmul_block(width, first)
    if block == width and planes == 1:
        block //= 2
    steps = width // block

    def kernel(value_ref, own_ref, other_ref, out_ref):
        own = dot(value_ref[0], own_ref[...], (1, 1))
        other = dot(value_ref[0], other_ref[...], (1, 1))

        @pl.when(pl.program_id(0) == 0)
        def _():
            out_ref[:, :half] = own
            out_ref[:, half:] = other

        @pl.when(pl.program_id(0) > 0)
        def _():
            out_ref[:, :half] += own
            out_ref[:, half:] += other

    part = pl.BlockSpec((half, block), lambda i: (0, i + first // block))
    return pl.pallas_call(
        kernel,
        grid=(planes * steps,),
        in_specs=[
            pl.BlockSpec((1, tokens, block), lambda i: (i // steps, 0, i % steps)),
            part,
            part,
        ],
        out_specs=pl.BlockSpec((tokens, 2 * half), lambda i: (0, 0)),
        out_shape=jax.ShapeDtypeStruct((tokens, 2 * half), F32),
        compiler_params=vmem(
            ((2, tokens, block), BF16), ((4, half, block), BF16), ((4, tokens, 2 * half), F32)
        ),
        cost_estimate=pl.CostEstimate(
            flops=4 * tokens * half * width * planes,
            bytes_accessed=4 * half * width * planes,
            transcendentals=0,
        ),
    )(value, *[far(part) for part in weight])


def feed_forward(value, weight, width):
    tokens, features = value.shape
    half = features // 2
    block = matmul_block(width, width)

    def kernel(value_ref, own_gate, other_gate, own_up, other_up, gate_ref, up_ref, act_ref):
        own, other = value_ref[:, :half], value_ref[:, half:]
        gate = dot(own, own_gate[...], (1, 0)) + dot(other, other_gate[...], (1, 0))
        up = dot(own, own_up[...], (1, 0)) + dot(other, other_up[...], (1, 0))
        gate_ref[...] = gate
        up_ref[...] = up
        act_ref[...] = gated(gate, up).astype(BF16)

    gate_part = pl.BlockSpec((half, block), lambda i: (0, i))
    up_part = pl.BlockSpec((half, block), lambda i: (0, i + width // block))
    out = pl.BlockSpec((tokens, block), lambda i: (0, i))
    return pl.pallas_call(
        kernel,
        grid=(width // block,),
        in_specs=[pl.BlockSpec(value.shape, lambda i: (0, 0))]
        + [gate_part, gate_part, up_part, up_part],
        out_specs=[out] * 3,
        out_shape=[jax.ShapeDtypeStruct((tokens, width), kind) for kind in (F32, F32, BF16)],
        compiler_params=vmem(((8, half, block), BF16), ((9, tokens, block), F32)),
        cost_estimate=pl.CostEstimate(
            flops=4 * tokens * features * width,
            bytes_accessed=4 * features * width,
            transcendentals=0,
        ),
    )(value, *[far(part) for part in (*weight, *weight)])


def feed_back(value, weight, gate, up):
    tokens, features = value.shape
    half = features // 2
    width = gate.shape[1]
    block = matmul_block(width, 0)

    def kernel(value_ref, own_ref, other_ref, gate_ref, up_ref, out_ref):
        grad = dot(value_ref[:, :half], own_ref[...], (1, 0))
        grad += dot(value_ref[:, half:], other_ref[...], (1, 0))
        dgate, dup = jax.vjp(gated, gate_ref[...], up_ref[...])[1](grad)
        out_ref[0] = dgate.astype(BF16)
        out_ref[1] = dup.astype(BF16)

    part = pl.BlockSpec((half, block), lambda i: (0, i))
    wide = pl.BlockSpec((tokens, block), lambda i: (0, i))
    return pl.pallas_call(
        kernel,
        grid=(width // block,),
        in_specs=[pl.BlockSpec(value.shape, lambda i: (0, 0)), part, part, wide, wide],
        out_specs=pl.BlockSpec((2, tokens, block), lambda i: (0, 0, i)),
        out_shape=jax.ShapeDtypeStruct((2, tokens, width), BF16),
        compiler_params=vmem(((4, half, block), BF16), ((9, tokens, block), F32)),
        cost_estimate=pl.CostEstimate(
            flops=2 * tokens * features * width,
            bytes_accessed=4 * features * width,
            transcendentals=0,
        ),
    )(value, *[far(part) for part in weight], gate, up)


def rms_norm(hidden, gain):
    return hidden * lax.rsqrt(jnp.mean(hidden * hidden, axis=-1, keepdims=True) + EPS) * gain


def gated(gate, up):
    return jax.nn.gelu(gate) * up


def advance(master, moment, trail, grad, rate):
    new_moment = 0.5 * moment + 0.5 * grad
    new_master = master - rate * (grad + 0.5 * new_moment)
    new_trail = 0.5 * trail + 0.5 * new_master
    return (new_master, new_moment, new_trail, new_master.astype(BF16))


def on_device(
    tokens,
    memory,
    dec_ids,
    enc_ids,
    cotangent,
    query_weight,
    query_moment,
    query_trail,
    keyval_weight,
    keyval_moment,
    keyval_trail,
    output_weight,
    output_moment,
    output_trail,
    inner_weight,
    inner_moment,
    inner_trail,
    outer_weight,
    outer_moment,
    outer_trail,
    norm_gains,
    gains_moment,
    gains_trail,
):
    rows, local_len, width = tokens.shape
    mem_local = memory.shape[1]
    narrow_count = lax.axis_size("narrow")
    seq_len = local_len * narrow_count
    inner_width = outer_weight.shape[0]
    q_width, kv_width = query_weight.shape[2], keyval_weight.shape[2]
    gain_count, gain_width = norm_gains.shape
    q_share, kv_share = q_width // narrow_count, kv_width // (2 * narrow_count)

    gain_cols = jnp.pad(norm_gains.astype(BF16).T, ((0, 0), (0, PAIR - gain_count)))
    shard0 = jnp.concatenate(
        [query_weight[0], keyval_weight[0], gain_cols.astype(F32)], axis=1
    ).astype(BF16)
    z0 = spread_steps(shard0, near_steps() + far_steps())
    shard1 = jnp.concatenate(
        [
            output_weight[0].T.astype(BF16),
            query_weight[1].astype(BF16),
            keyval_weight[1].astype(BF16),
            output_weight[1].T.astype(BF16),
        ],
        axis=1,
    )
    tokens_own, memory_own, grad_ffn = to_own(
        tokens.reshape(local_len, width),
        memory.reshape(mem_local, width),
        cotangent.reshape(local_len, width),
    )
    z0, shard1, tokens_own, memory_own, grad_ffn = sync(
        z0, shard1, tokens_own, memory_own, grad_ffn
    )
    dec_col, dec_row = dec_ids.reshape(-1, 1), dec_ids.reshape(1, -1)
    enc_col = enc_ids.reshape(-1, 1)
    g0 = mirror_first(*spread_join(shard0, z0))
    z1 = spread_steps(shard1, near_steps())
    shard2 = inner_weight.astype(BF16)
    shard3 = outer_weight.T.astype(BF16)
    hidden = tokens_own.astype(F32)
    g0, z1, shard1, shard2, shard3 = sync(g0, z1, shard1, shard2, shard3)
    r0 = mirror_rest(g0)
    z1 |= spread_steps(shard1, far_steps())
    r0, z1 = sync(r0, z1)
    (own,) = mirror_join(g0, r0, (q_width + kv_width + PAIR,))
    w_zero = (own, flip(own, 0))
    a1, b1 = spread_join(shard1, z1, width + q_width, kv_width + width)
    a1 = mirror_first(a1)
    z2 = spread_steps(shard2, near_steps())
    w_zero, b1 = sync(w_zero, b1)
    gains = turned_gains(*w_zero, q_width + kv_width)
    normed_one = rms_norm(hidden, gains[0]).astype(BF16)
    half_kv = kv_width // 2
    made = into(normed_one, w_zero, 0, q_width + kv_width, BF16)
    pieces = cut_columns(
        [(made, 0, q_width), (made, q_width, half_kv), (made, q_width + half_kv, half_kv)]
    )
    pieces, a1, b1, shard2, z2 = sync(pieces, a1, b1, shard2, z2)
    joint_one = trade(pieces)
    b1 = mirror_first(b1)
    joint_one, b1, shard2 = sync(joint_one, b1, shard2)
    ra1, rb1 = half_rest(a1, False), half_rest(b1, True)
    z2 |= spread_steps(shard2, far_steps())
    context, stat_one = attention(joint_one, dec_col, dec_row, local_len, True)
    context, ra1, rb1, z2 = sync(context, ra1, rb1, z2)
    came = trade(context)
    w_one = half_join((a1, ra1), (b1, rb1))
    a2, b2 = spread_join(shard2, z2, inner_width, inner_width)
    a2 = mirror_first(a2)
    kv_at, o_two_at = width + q_width, width + q_width + kv_width
    keyval_two = into(memory_own, w_one, kv_at, kv_width, BF16)
    came, w_one, shard3, b2, keyval_two = sync(came, w_one, shard3, b2, keyval_two)
    context_one = join_columns(came, q_share)
    after_one = hidden + out_of(context_one[None], w_one, 0)
    normed_two = rms_norm(after_one, gains[1]).astype(BF16)
    query_two = into(normed_two, w_one, width, q_width, BF16)
    pieces = cut_columns(
        [(query_two, 0, q_width), (keyval_two, 0, half_kv), (keyval_two, half_kv, half_kv)]
    )
    a2, pieces, after_one, b2 = sync(a2, pieces, after_one, b2)
    joint_two = trade(pieces)
    b2 = mirror_first(b2)
    joint_two, b2, shard3 = sync(joint_two, b2, shard3)
    ra2, rb2 = half_rest(a2, False), half_rest(b2, True)
    z3 = spread_steps(shard3, near_steps() + far_steps())
    context, stat_two = attention(joint_two, enc_col, dec_row, local_len, False)
    context, ra2, rb2, z3, shard3 = sync(context, ra2, rb2, z3, shard3)
    came = trade(context)
    half_inner = inner_width // 2
    a3, b3 = spread_join(shard3, z3, half_inner, half_inner)
    a3 = mirror_first(a3)
    w_in = half_join((a2, ra2), (b2, rb2))
    came, w_in, a3, b3 = sync(came, w_in, a3, b3)
    b3 = mirror_first(b3)
    context_two = join_columns(came, q_share)
    after_two = after_one + out_of(context_two[None], w_one, o_two_at)
    normed_three = rms_norm(after_two, gains[2]).astype(BF16)
    b3, normed_three, after_two = sync(b3, normed_three, after_two)
    ra3, rb3 = half_rest(a3, False), half_rest(b3, True)
    gate, up, activated = feed_forward(normed_three, w_in, inner_width)
    ra3, rb3, gate, up, activated = sync(ra3, rb3, gate, up, activated)
    w_out = half_join((a3, ra3), (b3, rb3))
    sum_outs = Sum(
        [Unit(grad_ffn, activated[None], 0, 0, half_inner)],
        [Unit(grad_ffn, activated[None], 0, half_inner, half_inner)],
    )
    w_out, activated = hold([sum_outs], w_out, activated)
    sum_outs.over_core()
    grad_inner = feed_back(grad_ffn, w_out, gate, up)
    (grad_inner,) = hold([sum_outs], grad_inner)
    sum_outs.add_own()
    sum_ins = Sum(
        [Unit(normed_three, grad_inner, 0, 0, half_inner)],
        [Unit(normed_three, grad_inner, 0, half_inner, half_inner)],
        [Unit(normed_three, grad_inner, 1, 0, half_inner)],
        [Unit(normed_three, grad_inner, 1, half_inner, half_inner)],
    )
    (grad_inner,) = hold([sum_outs, sum_ins], grad_inner)
    sum_outs.over_first()
    sum_ins.over_core()
    grad_normed = out_of(grad_inner, w_in, 0)
    grad_hidden, grad_gain_three = jax.vjp(rms_norm, after_two, gains[2])[1](grad_normed)
    grad_two = grad_ffn.astype(F32) + grad_hidden
    grad_branch = grad_two.astype(BF16)
    pieces = cut_columns([(into(grad_branch, w_one, o_two_at, width, BF16), 0, width)])
    pieces, grad_branch_two = hold([sum_ins, sum_outs], pieces, grad_branch)
    grad_context = trade(pieces)
    sum_outs.over_rest()
    sum_ins.add_own()
    outer_whole = sum_outs.whole()
    grad_context, outer_whole = hold([sum_ins], grad_context, outer_whole)
    sum_ins.over_first(0, 1)
    outer_parts = trade(outer_whole)
    dquery, dkeyval = attention_back(
        joint_two, grad_context, stat_two, enc_col, dec_row, local_len, False
    )
    dquery, dkeyval, activated, outer_parts = hold(
        [sum_ins], dquery, dkeyval, activated, outer_parts
    )
    came = trade(dquery)
    sum_ins.over_first(2, 3)
    result = after_two + out_of(activated[None], w_out, 0)
    (block_out,) = from_own(result.astype(BF16))
    came, dkeyval, block_out = hold([sum_ins], came, dkeyval, block_out)
    came_too = trade(dkeyval)
    sum_ins.over_rest()
    query_grad_two = join_columns(came, q_share)
    grad_normed_two = out_of(query_grad_two[None], w_one, width)
    grad_hidden, grad_gain_two = jax.vjp(rms_norm, after_one, gains[1])[1](grad_normed_two)
    grad_one = grad_two + grad_hidden
    grad_branch = grad_one.astype(BF16)
    pieces = cut_columns([(into(grad_branch, w_one, 0, width, BF16), 0, width)])
    pieces, grad_branch, came_too = hold([sum_ins], pieces, grad_branch, came_too)
    grad_context = trade(pieces)
    gate_whole = sum_ins.whole(0, 1)
    keyval_grad_two = join_columns(came_too, kv_share, 2)
    sum_mid = Sum(
        [
            Unit(grad_branch_two, context_two[None], 0, 0, width),
            Unit(memory_own, keyval_grad_two[None], 0, 0, kv_width),
        ],
        [
            Unit(normed_two, query_grad_two[None], 0, 0, q_width),
            Unit(grad_branch, context_one[None], 0, 0, width),
        ],
    )
    grad_context, keyval_grad_two, gate_whole = hold(
        [sum_mid, sum_ins], grad_context, keyval_grad_two, gate_whole
    )
    sum_mid.over_core()
    gate_parts = trade(gate_whole)
    dquery, dkeyval = attention_back(
        joint_one, grad_context, stat_one, dec_col, dec_row, local_len, True
    )
    sum_mid.add_own()
    dquery, dkeyval, keyval_grad_two, outer_parts, gate_parts = hold(
        [sum_mid], dquery, dkeyval, keyval_grad_two, outer_parts, gate_parts
    )
    came = trade(dquery)
    sum_mid.over_first()
    (memory_grad,) = from_own(out_of(keyval_grad_two[None], w_one, kv_at))
    sum_outer = total(outer_parts).T
    up_whole = sum_ins.whole(2, 3)
    came, sum_outer, memory_grad, dkeyval, up_whole = hold(
        [sum_mid], came, sum_outer, memory_grad, dkeyval, up_whole
    )
    came_too = trade(dkeyval)
    sum_mid.over_rest()
    query_grad_one = join_columns(came, q_share)
    grad_normed_one = out_of(query_grad_one[None], w_zero, 0)
    came_too, grad_normed_one = hold([sum_mid], came_too, grad_normed_one)
    keyval_grad_one = join_columns(came_too, kv_share, 2)
    sum_last = Sum(
        [Unit(normed_one, query_grad_one[None], 0, 0, q_width)],
        [Unit(normed_one, keyval_grad_one[None], 0, 0, kv_width)],
    )
    up_parts = trade(up_whole)
    mid_whole = sum_mid.whole()
    keyval_grad_one, mid_whole = hold([sum_last], keyval_grad_one, mid_whole)
    sum_last.over_core()
    mid_parts = trade(mid_whole)
    (keyval_grad_one,) = hold([sum_last], keyval_grad_one)
    sum_last.add_own()
    (keyval_grad_one,) = hold([sum_last], keyval_grad_one)
    sum_last.over_first()
    grad_normed_one += out_of(keyval_grad_one[None], w_zero, q_width)
    grad_hidden, grad_gain_one = jax.vjp(rms_norm, hidden, gains[0])[1](grad_normed_one)
    input_grad, full_gains = from_own(
        grad_one + grad_hidden,
    ) + from_own(jnp.stack([grad_gain_one, grad_gain_two, grad_gain_three]))
    input_grad, full_gains = hold([sum_last], input_grad, full_gains)
    sum_last.over_rest()
    gain_parts = all_sum_cube(full_gains)
    sum_inner = jnp.concatenate([total(gate_parts), total(up_parts)], axis=1)
    gain_parts, mid_parts = hold([sum_last], gain_parts, mid_parts)
    sum_two = total(mid_parts)
    last_parts = trade(sum_last.whole())
    part = sum(gain_parts)
    full_gains = sum(all_sum_chain(part + flip(part, 0)))
    sum_gains = lax.dynamic_slice_in_dim(full_gains, shard_place() * gain_width, gain_width, 1)
    sum_one = total(last_parts)
    after_kv, after_q = width + kv_width, width + kv_width + q_width
    sum_query = jnp.stack([sum_one[:, :q_width], sum_two[:, after_kv:after_q]])
    sum_keyval = jnp.stack([sum_one[:, q_width:], sum_two[:, width:after_kv]])
    sum_output = jnp.stack([sum_two[:, after_q:], sum_two[:, :width]]).transpose(0, 2, 1)
    block_out = block_out.reshape(rows, local_len, width)
    input_grad = input_grad.reshape(rows, local_len, width)
    memory_grad = memory_grad.reshape(rows, mem_local, width)
    token_total = rows * lax.axis_size("wide") * seq_len
    rate = RATE / math.sqrt(token_total)
    output_rate = OUTPUT_RATE / math.sqrt(token_total)
    new_query = advance(query_weight, query_moment, query_trail, sum_query, rate)
    new_keyval = advance(keyval_weight, keyval_moment, keyval_trail, sum_keyval, rate)
    new_output = advance(output_weight, output_moment, output_trail, sum_output, output_rate)
    new_inner = advance(inner_weight, inner_moment, inner_trail, sum_inner, rate)
    new_outer = advance(outer_weight, outer_moment, outer_trail, sum_outer, rate)
    new_gains = advance(norm_gains, gains_moment, gains_trail, sum_gains, rate)
    return (
        block_out,
        input_grad,
        memory_grad,
        new_query[0],
        new_query[1],
        new_query[2],
        new_query[3],
        new_keyval[0],
        new_keyval[1],
        new_keyval[2],
        new_keyval[3],
        new_output[0],
        new_output[1],
        new_output[2],
        new_output[3],
        new_inner[0],
        new_inner[1],
        new_inner[2],
        new_inner[3],
        new_outer[0],
        new_outer[1],
        new_outer[2],
        new_outer[3],
        new_gains[0],
        new_gains[1],
        new_gains[2],
        new_gains[3],
    )


def solution(mesh):
    in_specs = (
        P("wide", "narrow", None),
        P("wide", "narrow", None),
        P("wide", None),
        P("wide", None),
        P("wide", "narrow", None),
        P(None, ("wide", "narrow"), None),
        P(None, ("wide", "narrow"), None),
        P(None, ("wide", "narrow"), None),
        P(None, ("wide", "narrow"), None),
        P(None, ("wide", "narrow"), None),
        P(None, ("wide", "narrow"), None),
        P(None, None, ("wide", "narrow")),
        P(None, None, ("wide", "narrow")),
        P(None, None, ("wide", "narrow")),
        P(("wide", "narrow"), None),
        P(("wide", "narrow"), None),
        P(("wide", "narrow"), None),
        P(None, ("wide", "narrow")),
        P(None, ("wide", "narrow")),
        P(None, ("wide", "narrow")),
        P(None, ("wide", "narrow")),
        P(None, ("wide", "narrow")),
        P(None, ("wide", "narrow")),
    )
    out_specs = (
        P("wide", "narrow", None),
        P("wide", "narrow", None),
        P("wide", "narrow", None),
        P(None, ("wide", "narrow"), None),
        P(None, ("wide", "narrow"), None),
        P(None, ("wide", "narrow"), None),
        P(None, ("wide", "narrow"), None),
        P(None, ("wide", "narrow"), None),
        P(None, ("wide", "narrow"), None),
        P(None, ("wide", "narrow"), None),
        P(None, ("wide", "narrow"), None),
        P(None, None, ("wide", "narrow")),
        P(None, None, ("wide", "narrow")),
        P(None, None, ("wide", "narrow")),
        P(None, None, ("wide", "narrow")),
        P(("wide", "narrow"), None),
        P(("wide", "narrow"), None),
        P(("wide", "narrow"), None),
        P(("wide", "narrow"), None),
        P(None, ("wide", "narrow")),
        P(None, ("wide", "narrow")),
        P(None, ("wide", "narrow")),
        P(None, ("wide", "narrow")),
        P(None, ("wide", "narrow")),
        P(None, ("wide", "narrow")),
        P(None, ("wide", "narrow")),
        P(None, ("wide", "narrow")),
    )
    return jax.shard_map(
        on_device, mesh=mesh, in_specs=in_specs, out_specs=out_specs, check_vma=False
    )
```
